32 devices in a mesh: blk: 4 (over y, core), dp: 8 (over z, x).
Axes of the slice: x: 2, y: 2, z: 4, core: 2. Of those that a mesh axis runs over, the one named last changes fastest.
Arguments:
- inputs: bfloat16 [8, 1024, 512], P('dp', 'blk'), may hold values from -6 to 6
- segments: int32 [8, 1024], P('dp'), may hold values from 0 to 32, as said below
- attention_routes: int32 [2, 8, 1024, 4], P(None, 'dp', 'blk'), may hold values from 0 to 7, all different within a row
- expert_routes: int32 [2, 8, 1024, 2], P(None, 'dp', 'blk'), may hold values from 0 to 15, all different within a row; in each aligned block of 256 rows (0 to 255, 256 to 511, ..., all dimensions but the last counted through in order) at most 48 rows name the same one
- gain_mixer: bfloat16 [512], replicated, may hold values from 0.5 to 1.5
- gain_expert: bfloat16 [512], replicated, may hold values from 0.5 to 1.5
- weight_query: bfloat16 [8, 512, 512], P(None, 'dp', 'blk'), may hold values from -0.25 to 0.25
- weight_key: bfloat16 [512, 512], P('dp', 'blk'), may hold values from -0.25 to 0.25
- weight_value: bfloat16 [512, 512], P('dp', 'blk'), may hold values from -0.25 to 0.25
- weight_out: bfloat16 [8, 512, 512], P(None, 'blk', 'dp'), may hold values from -2 to 2
- router_mixer: bfloat16 [512, 8], replicated, may hold values from -0.125 to 0.125
- router_expert: bfloat16 [512, 16], replicated, may hold values from -0.1875 to 0.1875
- weight_in: bfloat16 [16, 512, 2048], P('dp', 'blk'), may hold values from -0.25 to 0.25
- weight_back: bfloat16 [16, 2048, 512], P('dp', 'blk'), may hold values from -0.125 to 0.125
- halt_weight: bfloat16 [512], replicated, may hold values from -0.25 to 0.25
- cotangent: bfloat16 [8, 1024, 512], P('dp', 'blk'), may hold values from -6 to 6
Outputs:
- result: bfloat16 [8, 1024, 512], P('dp', 'blk')
- input_grad: bfloat16 [8, 1024, 512], P('dp', 'blk')
- gain_mixer_grad: float32 [512], replicated
- gain_expert_grad: float32 [512], replicated
- query_grad: float32 [8, 512, 512], P(None, 'dp', 'blk')
- key_grad: float32 [512, 512], P('dp', 'blk')
- value_grad: float32 [512, 512], P('dp', 'blk')
- out_grad: float32 [8, 512, 512], P(None, 'blk', 'dp')
- router_mixer_grad: float32 [512, 8], replicated
- router_expert_grad: float32 [512, 16], replicated
- in_grad: float32 [16, 512, 2048], P('dp', 'blk')
- back_grad: float32 [16, 2048, 512], P('dp', 'blk')
- halt_grad: float32 [512], replicated
The draws below stay inside these ranges and needn't reach their ends.
Inputs may be any that keep to these rules, and one draw needn't show every extreme that they name: `segments`: each pack is cut into sentences along its positions: a first one of 1 to b - 1 positions, then sentences of exactly b positions, the last one possibly shorter, where the pack's bucket length b is 256, 128, 64 or 32; pack 0 has b = 256 and the last pack b = 32. No sentence begins at a multiple of 256. Ids number the sentences of a pack from 0 in order. `attention_routes`: each position names 4 different attention experts. `expert_routes`: each position names 2 different experts. In each aligned block of 256 positions of one step and pack, no expert is named by more than 48 positions; some expert is named by exactly 48 in some blocks.
All inputs are finite; a program needn't handle non-finite values.
Results may differ from the reference program's by a relative error of at most 0.024.
Values may be sent and summed in bfloat16 or wider, within the bound.
A program may use at most 256 MiB of HBM per device.

```python
import math
import jax
import jax.numpy as jnp
import numpy as np
from jax import lax

D = 512
HEADS = 8
HD = 64
DA = 512
FF = 2048
EA = 8
TOPA = 4
EXPERTS = 16
TOPF = 2
STEPS = 2
MAXLEN = 256
SEQ_DEV = 256
ROWS = 8
LENGTH = 1024
CAP = 48
CAPR = 192
QB = 512
KW = 768


def draw_segments(key, part):
    key = jax.random.fold_in(key, 7)
    shift_key, offset_key = jax.random.split(key)
    halvings = jax.random.randint(shift_key, (ROWS,), 0, 4).astype(jnp.int32)
    halvings = halvings.at[0].set(0)
    halvings = halvings.at[ROWS - 1].set(3)
    bucket = jnp.right_shift(jnp.full((ROWS,), MAXLEN, jnp.int32), halvings)
    offset = jax.random.randint(offset_key, (ROWS,), 0, 1 << 20).astype(jnp.int32) % (bucket - 1) + 1
    positions = jnp.arange(LENGTH, dtype=jnp.int32)
    return ((positions[None, :] + offset[:, None]) // bucket[:, None]).astype(jnp.int32)


def levels(own_key, extent, cuts, least, high):
    level, own = 1.0, jax.random.fold_in(own_key, 6)
    for position, blocks in cuts:
        steps = jnp.exp(jax.random.uniform(jax.random.fold_in(own, position), (blocks,), jnp.float32, least / len(cuts), high / len(cuts)))
        level = level * jnp.repeat(steps, extent[position] // blocks).reshape([-1 if axis == position else 1 for axis in range(len(extent))])
    return level


def choose_distinct(stream_key, rows, amount, top, lift):
    sequence = jax.random.permutation(jax.random.fold_in(stream_key, 1), amount)
    boost = sequence
    for power in range(3):
        boost = boost * boost // amount
    boost = boost * lift // amount
    lots = jax.random.randint(jax.random.fold_in(stream_key, 2), (rows, amount), 0, 4096) + boost
    sure = jax.random.permutation(jax.random.fold_in(stream_key, 3), rows)[jnp.arange(amount) % rows]
    lots = jnp.where(jnp.arange(rows)[:, None] == sure[None, :], 1 << 14, lots)
    score = lots * amount + jnp.arange(amount)
    return lax.top_k(score.astype(jnp.int32), top)[1].astype(jnp.int32)


def deal_out(key, own, number, rows, number_of, top, most, slope):
    ranking = jax.random.permutation(key, number_of)
    heavy_load, ordinary = load_shares(number_of, rows * top, most, slope, True), load_shares(number_of, rows * top, most, slope, False)
    places = jnp.arange(number_of)

    def named(lengths, offset_by):
        used = int((lengths > 0).sum())
        fixed = max(1, used // 4)
        shifted = fixed + (places - fixed + offset_by * (used - fixed)) % max(1, number_of - fixed)
        return jnp.zeros((number_of,), jnp.int32).at[ranking[jnp.where(places < fixed, places, shifted)]].set(jnp.asarray(lengths, jnp.int32))

    lengths = jnp.where(number % 4 == 0, named(heavy_load, number // 4), named(ordinary, number - number // 4 - 1))
    mixed = jax.random.permutation(jax.random.fold_in(own, 3), number_of)
    source_of, sink = mixed[0:number_of // 2 * 2:2], mixed[1:number_of // 2 * 2:2]
    slack = jnp.minimum(lengths[source_of] - 1, most - lengths[sink]) // 2
    slack = jnp.where((source_of == ranking[0]) | (sink == ranking[0]) | (lengths[sink] == 0), 0, jnp.maximum(slack, 0))
    shifted = jax.random.randint(jax.random.fold_in(own, 4), (number_of // 2,), 0, 1 << 20) % (slack + 1)
    lengths = lengths.at[source_of].add(-shifted).at[sink].add(shifted)
    labels = jnp.searchsorted(jnp.cumsum(lengths), jnp.arange(rows * top), side="right").astype(jnp.int32)
    table = labels.reshape(top, rows).T
    table = table[jax.random.permutation(jax.random.fold_in(own, 1), rows)]
    offset_by = jax.random.randint(jax.random.fold_in(own, 2), (rows, 1), 0, top)
    return jnp.take_along_axis(table, (jnp.arange(top)[None, :] + offset_by) % top, axis=1)


def load_shares(amount, total, reach, skew, full):
    portions = [(1 << 20) // math.isqrt(grade ** skew) + 1 for grade in range(1, amount + 1)]
    largest = reach if full else min(reach, max(-(-total // amount), total * portions[0] // sum(portions)))
    least = 1 if total - largest >= amount - 1 else 0
    given, surplus = [largest] + [least] * (amount - 1), total - largest - least * (amount - 1)
    while surplus > 0:
        movable = [i for i in range(1, amount) if given[i] < largest] or [i for i in range(1, amount) if given[i] < reach]
        mass, left = sum([portions[i] for i in movable]), surplus
        for i in movable:
            addition = min(reach - given[i], max(1, left * portions[i] // mass), surplus)
            given[i] = given[i] + addition
            surplus = surplus - addition
    return np.array(given)


def gaussian(rng, extent, spread, reach, pieces=(), kind=jnp.bfloat16):
    level = levels(rng, extent, pieces, -0.22, 0.18) if pieces else 1.0
    values = jax.random.normal(rng, extent, jnp.float32) * spread * level
    return jnp.minimum(jnp.maximum(values, -reach), reach).astype(kind)


def setup_inputs(seed: int = 0) -> dict:
    key_of = jax.random.split(jax.random.key(seed), 17)
    inputs = gaussian(key_of[0], (ROWS, LENGTH, D), 1.0, 6.0, ((0, 8), (1, 4)))
    segments = draw_segments(jax.random.fold_in(key_of[16], 71), 0)
    attention_routes = choose_distinct(key_of[2], STEPS * ROWS * LENGTH, EA, TOPA, 0).reshape((STEPS, ROWS, LENGTH, TOPA))
    expert_routes_keys = jax.random.split(jax.random.fold_in(key_of[3], 1), STEPS * ROWS * LENGTH // SEQ_DEV)
    expert_routes_turns = jax.random.permutation(jax.random.fold_in(key_of[3], 3), STEPS * ROWS * LENGTH // SEQ_DEV)
    expert_routes = jax.vmap(lambda own, number: deal_out(jax.random.fold_in(key_of[3], 2), own, number, SEQ_DEV, EXPERTS, TOPF, CAP, 1))(expert_routes_keys, expert_routes_turns).reshape((STEPS, ROWS, LENGTH, TOPF))
    gain_mixer = jnp.clip(1.0 + 0.1 * jax.random.normal(key_of[4], (D,), jnp.float32), 0.5, 1.5).astype(jnp.bfloat16)
    gain_expert = jnp.clip(1.0 + 0.1 * jax.random.normal(key_of[5], (D,), jnp.float32), 0.5, 1.5).astype(jnp.bfloat16)
    weight_query = gaussian(key_of[6], (EA, D, DA), D ** -0.5, 0.25, ((1, 8), (2, 4)))
    weight_key = gaussian(key_of[7], (D, DA), D ** -0.5, 0.25, ((0, 8), (1, 4)))
    weight_value = gaussian(key_of[8], (D, DA), D ** -0.5, 0.25, ((0, 8), (1, 4)))
    weight_out = gaussian(key_of[9], (EA, DA, D), (DA // 64) ** -0.5, 2.0, ((1, 4), (2, 8)))
    router_mixer = gaussian(key_of[10], (D, EA), (4 * D) ** -0.5, 0.125)
    router_expert = gaussian(key_of[11], (D, EXPERTS), (2 * D) ** -0.5, 0.1875)
    weight_in = gaussian(key_of[12], (EXPERTS, D, FF), D ** -0.5, 0.25, ((0, 8), (1, 4)))
    weight_back = gaussian(key_of[13], (EXPERTS, FF, D), FF ** -0.5, 0.125, ((0, 8), (1, 4)))
    halt_weight = gaussian(key_of[14], (D,), D ** -0.5, 0.25)
    cotangent = gaussian(key_of[15], (ROWS, LENGTH, D), 1.0, 6.0, ((0, 8), (1, 4)))
    return {"inputs": inputs, "segments": segments, "attention_routes": attention_routes, "expert_routes": expert_routes, "gain_mixer": gain_mixer, "gain_expert": gain_expert, "weight_query": weight_query, "weight_key": weight_key, "weight_value": weight_value, "weight_out": weight_out, "router_mixer": router_mixer, "router_expert": router_expert, "weight_in": weight_in, "weight_back": weight_back, "halt_weight": halt_weight, "cotangent": cotangent}


EPSILON = 1e-06
PRECISE = lax.Precision.HIGHEST
MASKED_SCORE = -1e+30

@jax.custom_vjp
def low(v):
    return lax.optimization_barrier(v.astype(jnp.bfloat16)).astype(jnp.float32)

@jax.custom_vjp
def low_back(v):
    return v

def low_keep(v):
    return (low(v), None)

def low_pass(kept, grad):
    return (grad,)

def back_keep(v):
    return (v, None)

def back_low(kept, grad):
    return (low(grad),)
low.defvjp(low_keep, low_pass)
low_back.defvjp(back_keep, back_low)

def norm_scale(values_in, gain_vec):
    return values_in * lax.rsqrt(lax.optimization_barrier(jnp.mean(values_in * values_in, axis=-1, keepdims=True)) + EPSILON) * gain_vec

def attention(queries, keys, values, seg_row):
    score_scale = HD ** (-0.5)

    def block(start):
        key_start = jnp.minimum(jnp.maximum(start - MAXLEN, 0), LENGTH - KW).astype(jnp.int32)
        query_part = lax.dynamic_slice_in_dim(queries, start, QB, 1)
        key_part = lax.dynamic_slice_in_dim(keys, key_start, KW, 0)
        value_part = lax.dynamic_slice_in_dim(values, key_start, KW, 0)
        query_pos = start + jnp.arange(QB, dtype=jnp.int32)
        key_pos = key_start + jnp.arange(KW, dtype=jnp.int32)
        query_seg = lax.dynamic_slice_in_dim(seg_row, start, QB, 0)
        key_seg = lax.dynamic_slice_in_dim(seg_row, key_start, KW, 0)
        allowed = (key_pos[None, :] <= query_pos[:, None]) & (key_seg[None, :] == query_seg[:, None])
        scores = low_back(jnp.einsum('jqhc,khc->jhqk', query_part, key_part, precision=PRECISE) * score_scale)
        scores = jnp.where(allowed[None, None], scores, MASKED_SCORE)
        top_score = lax.optimization_barrier(jnp.max(scores, axis=-1, keepdims=True))
        exp_scores = jnp.exp(scores - top_score)
        probs = low(exp_scores / lax.optimization_barrier(jnp.sum(exp_scores, axis=-1, keepdims=True)))
        return jnp.einsum('jhqk,khc->jqhc', probs, value_part, precision=PRECISE)
    starts = jnp.arange(LENGTH // QB, dtype=jnp.int32) * QB
    blocks = lax.map(jax.checkpoint(block), starts)
    return jnp.transpose(blocks, (1, 0, 2, 3, 4)).reshape(TOPA, LENGTH, HEADS * HD)

def expert_layer(normed_two, expert_pick, router_expert, weight_in, weight_back):
    logits = jnp.dot(normed_two, router_expert, precision=PRECISE)
    gates = jax.nn.softmax(jnp.take_along_axis(logits, expert_pick, axis=-1), axis=-1)
    flat_pick = expert_pick.reshape(-1)
    member = (flat_pick[:, None] == jnp.arange(EXPERTS, dtype=jnp.int32)[None, :]).astype(jnp.int32)
    within = lax.optimization_barrier(jnp.sum(jnp.cumsum(member, axis=0) * member, axis=1)) - 1
    slot_index = flat_pick * CAPR + within
    copies = jnp.repeat(normed_two, TOPF, axis=0)
    buffer = jnp.zeros((EXPERTS * CAPR, D), jnp.float32).at[slot_index].set(copies)
    buffer = low_back(buffer).reshape(EXPERTS, CAPR, D)
    inner = low_back(jnp.einsum('ecd,edf->ecf', buffer, weight_in, precision=PRECISE))
    hidden_act = low(jax.nn.gelu(inner, approximate=False))
    outputs = low_back(low(jnp.einsum('ecf,efd->ecd', hidden_act, weight_back, precision=PRECISE)))
    returned = outputs.reshape(EXPERTS * CAPR, D)[slot_index].reshape(LENGTH, TOPF, D)
    return lax.optimization_barrier(jnp.sum(gates[:, :, None] * returned, axis=1))

def layer_step(layer_in, seg_row, mixer_pick, expert_pick, params):
    gain_mixer, gain_expert, weight_query, weight_key, weight_value, weight_out, router_mixer, router_expert, weight_in, weight_back, halt_weight = params
    normed = low(norm_scale(layer_in, gain_mixer))
    keys = low_back(low(jnp.dot(normed, weight_key, precision=PRECISE)))
    values = low_back(low(jnp.dot(normed, weight_value, precision=PRECISE)))
    mixer_logits = jnp.dot(normed, router_mixer, precision=PRECISE)
    mixer_gates = jax.nn.softmax(jnp.take_along_axis(mixer_logits, mixer_pick, axis=-1), axis=-1)
    mixer_hot = (mixer_pick[:, :, None] == jnp.arange(EA, dtype=jnp.int32)[None, None, :]).astype(jnp.float32)
    every_query = low_back(low(jnp.einsum('ld,edc->elc', normed, weight_query, precision=PRECISE)))
    picked = jnp.einsum('lje,elc->jlc', mixer_hot, every_query, precision=PRECISE)
    attended = low_back(attention(picked.reshape(TOPA, LENGTH, HEADS, HD), keys.reshape(LENGTH, HEADS, HD), values.reshape(LENGTH, HEADS, HD), seg_row))
    mixed = low(jnp.einsum('lje,lj,jlc->elc', mixer_hot, mixer_gates, attended, precision=PRECISE))
    middle = layer_in + low_back(jnp.einsum('elc,ecd->ld', mixed, weight_out, precision=PRECISE))
    normed_two = low(norm_scale(middle, gain_expert))
    return middle + expert_layer(normed_two, expert_pick, router_expert, weight_in, weight_back)

def forward_row(row_in, seg_row, mixer_picks, expert_picks, params):
    first_out = layer_step(row_in, seg_row, mixer_picks[0], expert_picks[0], params)
    second_out = layer_step(first_out, seg_row, mixer_picks[1], expert_picks[1], params)
    stop_prob = jax.nn.sigmoid(jnp.dot(first_out, params[10], precision=PRECISE))[:, None]
    return stop_prob * first_out + (1.0 - stop_prob) * second_out

def reference(inputs, segments, attention_routes, expert_routes, gain_mixer, gain_expert, weight_query, weight_key, weight_value, weight_out, router_mixer, router_expert, weight_in, weight_back, halt_weight, cotangent):
    params = tuple((one_param.astype(jnp.float32) for one_param in (gain_mixer, gain_expert, weight_query, weight_key, weight_value, weight_out, router_mixer, router_expert, weight_in, weight_back, halt_weight)))

    def one_row(totals, row_data):
        row_in, seg_row, mixer_picks, expert_picks, row_cot = row_data

        def run_forward(start_state, all_params):
            return forward_row(start_state, seg_row, mixer_picks, expert_picks, all_params)
        row_out, pull_back = jax.vjp(run_forward, row_in.astype(jnp.float32), params)
        grad_state, grad_params = pull_back(row_cot.astype(jnp.float32))
        totals = jax.tree.map(jnp.add, totals, grad_params)
        return (totals, (row_out.astype(jnp.bfloat16), grad_state.astype(jnp.bfloat16)))
    zeros_init = tuple((jnp.zeros(one_param.shape, jnp.float32) for one_param in params))
    totals, (result, input_grad) = lax.scan(one_row, zeros_init, (inputs, segments, jnp.transpose(attention_routes, (1, 0, 2, 3)), jnp.transpose(expert_routes, (1, 0, 2, 3)), cotangent))
    return (result, input_grad, totals[0], totals[1], totals[2], totals[3], totals[4], totals[5], totals[6], totals[7], totals[8], totals[9], totals[10])
```

```python
import functools
from typing import NamedTuple

import jax
import jax.numpy as jnp
from jax import lax
from jax.experimental import pallas as pl
from jax.experimental.pallas import tpu as pltpu
from jax.sharding import PartitionSpec as P

HEADS = 8
HD = 64
MAXLEN = 256
QROWS = 128
WINDOW = MAXLEN + QROWS
LANES = 128
EPSILON = 1e-06
MASKED_SCORE = -1e30
MESH = pl.DeviceIdType.MESH
BF = jnp.bfloat16
F32 = jnp.float32
VMEM_BYTES = 58 * 2**20


class Plan(NamedTuple):
    blk: int
    dp: int
    lo: int
    hi: int
    seq: int
    width: int
    heads: int
    mixers: int
    top: int
    experts: int
    local: int
    group: int
    cap: int
    ff: int

    @property
    def length(self):
        return self.blk * self.seq

    @property
    def cols(self):
        return self.heads * HD

    @property
    def qkv(self):
        return (self.mixers + 2) * self.cols

    @property
    def all_cols(self):
        return (2 * self.mixers + 2) * self.cols

    @property
    def blocks(self):
        return self.length // QROWS

    @property
    def slots(self):
        return self.experts * self.cap

    @property
    def chips(self):
        return self.blk // 2


def mm(a, b):
    return lax.dot_general(a, b, (((1,), (0,)), ((), ())), preferred_element_type=F32)


def mm_nt(a, b):
    return lax.dot_general(a, b, (((1,), (1,)), ((), ())), preferred_element_type=F32)


def place():
    return lax.axis_index("blk"), lax.axis_index("dp")


def turn(index, by, size):
    return lax.rem(index + (by % size), size)


def greet(peers):
    barrier = pltpu.get_barrier_semaphore()
    for peer in peers:
        pl.semaphore_signal(barrier, inc=1, device_id=peer, device_id_type=MESH)
    pl.semaphore_wait(barrier, len(peers))


def send(src, dst, sems, slot, peer):
    copy = pltpu.make_async_remote_copy(
        src_ref=src,
        dst_ref=dst,
        send_sem=sems[0].at[slot],
        recv_sem=sems[1].at[slot],
        device_id=peer,
        device_id_type=MESH,
    )
    copy.start()
    return copy


def aligned(value, by):
    return pl.multiple_of(value, by)


def pack_peers(p):
    b, d = place()
    y, c = b // 2, lax.rem(b, 2)
    peers = [(2 * y + 1 - c, d)]
    return peers + [(2 * turn(y, s, p.chips) + c, d) for s in range(1, p.chips)]


def slot_peer(p, s):
    b, d = place()
    e, g = b // p.group, lax.rem(b, p.group)
    return (turn(e, s // p.dp, p.local) * p.group + g, turn(d, s % p.dp, p.dp))


def slot_peers(p):
    return [slot_peer(p, s) for s in range(1, p.experts)]


def slot_source(p, s):
    b, d = place()
    e, g = b // p.group, lax.rem(b, p.group)
    return (turn(e, -(s // p.dp), p.local) * p.group + g, turn(d, -(s % p.dp), p.dp))


def dp_peers(p):
    b, d = place()
    z, x = d // p.lo, lax.rem(d, p.lo)
    peers = [(b, turn(z, s, p.hi) * p.lo + x) for s in range(1, p.hi)]
    return peers + [(b, z * p.lo + turn(x, t, p.lo)) for t in range(1, p.lo)]


def expert_peers(p):
    b, d = place()
    e, g = b // p.group, lax.rem(b, p.group)
    peers = [(turn(e, s, p.local) * p.group + g, d) for s in range(1, p.local)]
    return peers + [(e * p.group + turn(g, t, p.group), d) for t in range(1, p.group)]


class PackGather:
    def __init__(self, p, buf, far, near):
        self.p, self.buf, self.far, self.near = p, buf, far, near

    def begin(self):
        p = self.p
        b, d = place()
        y, c = b // 2, lax.rem(b, 2)
        own = self.buf.at[b]
        self.first = [
            send(own, own, self.far, s - 1, (2 * turn(y, s, p.chips) + c, d))
            for s in range(1, p.chips)
        ]
        self.second = [send(own, own, self.near, 0, (2 * y + 1 - c, d))]

    def finish(self):
        p = self.p
        b, d = place()
        y, c = b // 2, lax.rem(b, 2)
        for s in range(1, p.chips):
            self.first[s - 1].wait_recv()
            block = self.buf.at[2 * turn(y, -s, p.chips) + c]
            self.second.append(send(block, block, self.near, s, (2 * y + 1 - c, d)))
        for copy in self.second:
            copy.wait()
        for copy in self.first:
            copy.wait_send()


def pack_sems(p):
    return [
        pltpu.SemaphoreType.DMA((max(1, p.chips - 1),)),
        pltpu.SemaphoreType.DMA((max(1, p.chips - 1),)),
        pltpu.SemaphoreType.DMA((p.chips,)),
        pltpu.SemaphoreType.DMA((p.chips,)),
    ]


def pack_sum(p, make, part, own, near_in, far_out, far_in, sems):
    near, far = (sems[2], sems[3]), (sems[0], sems[1])
    b, d = place()
    y, c = b // 2, lax.rem(b, 2)
    order = [turn(y, s, p.chips) for s in list(range(1, p.chips)) + [0]]
    first = []
    for k, yy in enumerate(order):
        other = 2 * yy + 1 - c
        part[other] = make(other).astype(BF)
        first.append(send(part.at[other], near_in.at[k], near, k, (2 * y + 1 - c, d)))
    second = []
    for k, yy in enumerate(order):
        term = make(2 * yy + c)
        first[k].wait_recv()
        term = term + near_in[k].astype(F32)
        if k < p.chips - 1:
            far_out[k] = term.astype(BF)
            second.append(send(far_out.at[k], far_in.at[k], far, k, (2 * yy + c, d)))
        else:
            own[...] = term
    total = own[...]
    for k, copy in enumerate(second):
        copy.wait_recv()
        total = total + far_in[k].astype(F32)
    for copy in first + second:
        copy.wait_send()
    return total


def slot_send(p, src, dst, sems, s, peer):
    rows = pl.ds(s * p.cap, p.cap)
    return send(src.at[rows], dst.at[rows], sems, s, peer)


def setup_kernel(p, wall, win, wback, picks, routes, all_w, all_in, all_back, all_picks, disp, comb, both, mine, *sems):
    b, d = place()
    z, x = d // p.lo, lax.rem(d, p.lo)
    e, g = b // p.group, lax.rem(b, p.group)
    hi, lo, wide, near, pack, slot = (sems[2 * k : 2 * k + 2] for k in range(6))
    pack = sems[8:12]
    slot = sems[12:14]
    local = sems[14]
    greet(pack_peers(p) + slot_peers(p) + dp_peers(p) + expert_peers(p))
    own_rows = wall.shape[0]
    in_rows, back_rows = win.shape[1], wback.shape[1]

    def dp_rows(index):
        return all_w.at[pl.ds(aligned(index * own_rows, own_rows), own_rows)]

    def in_at(index):
        return all_in.at[pl.ds(aligned(index * in_rows, in_rows), in_rows)]

    def back_at(index):
        return all_back.at[pl.ds(aligned(index * back_rows, back_rows), back_rows)]

    waits = []
    here = [
        pltpu.make_async_copy(wall, dp_rows(d), local.at[0]),
        pltpu.make_async_copy(win.at[e], in_at(b), local.at[1]),
        pltpu.make_async_copy(wback.at[e], back_at(b), local.at[2]),
    ]
    for copy in here:
        copy.start()
    along = [send(wall, dp_rows(d), hi, s - 1, (b, turn(z, s, p.hi) * p.lo + x)) for s in range(1, p.hi)]
    for t in range(1, p.lo):
        waits.append(send(wall, dp_rows(d), lo, t - 1, (b, z * p.lo + turn(x, t, p.lo))))
    over = []
    for s in range(1, p.local):
        to = turn(e, s, p.local)
        over.append(send(win.at[to], in_at(b), wide, 2 * s - 2, (to * p.group + g, d)))
        over.append(send(wback.at[to], back_at(b), wide, 2 * s - 1, (to * p.group + g, d)))
    for t in range(1, p.group):
        to = e * p.group + turn(g, t, p.group)
        waits.append(send(win.at[e], in_at(b), near, 2 * t - 2, (to, d)))
        waits.append(send(wback.at[e], back_at(b), near, 2 * t - 1, (to, d)))

    all_picks[b] = picks[...]
    spread = PackGather(p, all_picks, pack[0:2], pack[2:4])
    spread.begin()

    place_in = lax.broadcasted_iota(jnp.int32, (p.experts, 1), 0)
    ids = lax.rem(d + lax.rem(place_in, p.dp), p.dp) * p.local + lax.rem(e + place_in // p.dp, p.local)
    earlier = (
        lax.broadcasted_iota(jnp.int32, (p.seq, p.seq), 0) < lax.broadcasted_iota(jnp.int32, (p.seq, p.seq), 1)
    ).astype(BF)
    slot_ids = lax.broadcasted_iota(jnp.int32, (p.cap, p.seq), 0).astype(F32)
    lane_ids = lax.broadcasted_iota(jnp.int32, (LANES, 1), 0)
    sent = []
    for step in range(2):
        one, two = routes[2 * step : 2 * step + 1, :], routes[2 * step + 1 : 2 * step + 2, :]
        member = jnp.where((one == ids) | (two == ids), 1.0, 0.0)
        rank = mm(member.astype(BF), earlier)
        rank = jnp.where(member > 0.5, rank, -1.0)
        for s in range(p.experts):
            disp[step, pl.ds(s * p.cap, p.cap), :] = jnp.where(rank[s : s + 1, :] == slot_ids, 1.0, 0.0).astype(BF)
        table = disp[step]
        comb[step] = table.astype(F32).T.astype(BF)
        pair = jnp.where((one == lane_ids) | (two == lane_ids), 1.0, 0.0).astype(BF)
        both[step] = mm_nt(table, pair).astype(BF)
        mine[step, 0 : p.cap, :] = both[step, 0 : p.cap, :]
        for s in range(1, p.experts):
            rows = pl.ds(s * p.cap, p.cap)
            sent.append(
                send(both.at[step, rows], mine.at[step, rows], slot, step * p.experts + s, slot_peer(p, s))
            )

    for s in range(1, p.hi):
        along[s - 1].wait_recv()
        rows = dp_rows(turn(z, -s, p.hi) * p.lo + x)
        for t in range(1, p.lo):
            k = s * (p.lo - 1) + t - 1
            waits.append(send(rows, rows, lo, k, (b, z * p.lo + turn(x, t, p.lo))))
    spread.finish()
    for s in range(1, p.local):
        source = turn(e, -s, p.local) * p.group + g
        for which, rows in ((0, in_at(source)), (1, back_at(source))):
            over[2 * s - 2 + which].wait_recv()
            for t in range(1, p.group):
                k = (s * (p.group - 1) + t - 1) * 2 + which
                waits.append(send(rows, rows, near, k, (e * p.group + turn(g, t, p.group), d)))
    for copy in waits + sent:
        copy.wait()
    for copy in along + over:
        copy.wait_send()
    for copy in here:
        copy.wait()


def attention_mask(seg_cols, seg_rows, start):
    keys = seg_cols[pl.ds(start, WINDOW), :]
    queries = seg_rows[:, pl.ds(start, QROWS)]
    key_at = lax.broadcasted_iota(jnp.int32, (WINDOW, QROWS), 0) - MAXLEN
    query_at = lax.broadcasted_iota(jnp.int32, (WINDOW, QROWS), 1)
    return jnp.where((key_at <= query_at) & (keys == queries), 0.0, MASKED_SCORE)


def head_rows(p, dst, values):
    flat = values.T
    lane = lax.broadcasted_iota(jnp.int32, flat.shape, 1) // HD
    for h in range(p.heads):
        dst(h, jnp.where(lane == h, flat, 0.0).astype(BF))


def pick_rows(p, routes, terms):
    picked = []
    for j in range(p.top):
        row = routes[j : j + 1, :]
        total = None
        for e in range(p.mixers):
            term = jnp.where(row == e, terms(e), 0.0)
            total = term if total is None else total + term
        picked.append(total)
    return picked


def spread_rows(p, routes, values, e):
    total = None
    for j in range(p.top):
        term = jnp.where(routes[j : j + 1, :] == e, values[j], 0.0)
        total = term if total is None else total + term
    return total


def attention_forward_kernel(
    p, step, h_ref, gain_one, gain_two, w_ref, router, picks, seg_rows, seg_cols,
    middle, m_ref, nt, qs, kt, vt, lse, att, mix, gates,
    w_t, k_heads, part, own, near_in, far_out, far_in, *sems,
):
    b, _ = place()
    cols, top = p.cols, p.top
    greet(pack_peers(p))
    h = h_ref[...]
    inverse = lax.rsqrt(jnp.mean(h * h, axis=-1, keepdims=True) + EPSILON)
    nt[b] = (h * inverse * gain_one[...]).T.astype(BF)
    spread = PackGather(p, nt, sems[0:2], sems[2:4])
    spread.begin()
    for start in range(0, p.qkv, 2 * cols):
        w_t[start : start + 2 * cols, :] = w_ref[:, start : start + 2 * cols].astype(F32).T.astype(BF)
    k_heads[:, 0:MAXLEN, :] = jnp.zeros((p.heads, MAXLEN, cols), BF)
    kt[:, 0:MAXLEN] = jnp.zeros((cols, MAXLEN), BF)
    vt[:, 0:MAXLEN] = jnp.zeros((cols, MAXLEN), BF)
    spread.finish()

    @pl.loop(0, p.blk)
    def _(bb):
        states = nt[bb]
        table = picks[bb, step * top : (step + 1) * top, :]
        logits = mm(router[...], states)
        chosen = pick_rows(p, table, lambda e: logits[e : e + 1, :])
        peak = functools.reduce(jnp.maximum, chosen)
        chosen = [jnp.exp(row - peak) for row in chosen]
        scale = 1.0 / sum(chosen)
        for j in range(top):
            gates[bb, j : j + 1, :] = chosen[j] * scale
        values = mm(w_t[...], states)
        for k in range(p.seq // QROWS):
            lanes = slice(k * QROWS, (k + 1) * QROWS)
            queries = pick_rows(
                p, table[:, lanes], lambda e: values[e * cols : (e + 1) * cols, lanes]
            )
            for j in range(top):
                qs[bb * (p.seq // QROWS) + k, :, j * QROWS : (j + 1) * QROWS] = (
                    queries[j] * (HD**-0.5)
                ).astype(BF)
        at = aligned(MAXLEN + bb * p.seq, QROWS)
        keys = values[p.mixers * cols : (p.mixers + 1) * cols, :]
        kt[:, pl.ds(at, p.seq)] = keys.astype(BF)
        vt[:, pl.ds(at, p.seq)] = values[(p.mixers + 1) * cols :, :].astype(BF)

        def put(head, rows):
            k_heads[head, pl.ds(at, p.seq), :] = rows

        head_rows(p, put, keys)

    @pl.loop(0, p.blocks)
    def _(i):
        start = aligned(i * QROWS, QROWS)
        bias = attention_mask(seg_cols, seg_rows, start)
        bias = jnp.concatenate([bias] * top, axis=1)
        queries = qs[i]
        for head in range(p.heads):
            scores = mm(k_heads[head, pl.ds(start, WINDOW), :], queries) + bias
            peak = jnp.max(scores, axis=0, keepdims=True)
            scores = jnp.exp(scores - peak)
            total = jnp.sum(scores, axis=0, keepdims=True)
            lse[i, head : head + 1, :] = peak + jnp.log(total)
            probs = (scores * (1.0 / total)).astype(BF)
            rows = slice(head * HD, (head + 1) * HD)
            att[i, rows, :] = mm(vt[rows, pl.ds(start, WINDOW)], probs).astype(BF)
        bb = i // (p.seq // QROWS)
        at = pl.ds(aligned(lax.rem(i, p.seq // QROWS) * QROWS, QROWS), QROWS)
        table = picks[bb, step * top : (step + 1) * top, at]
        weights = gates[bb, 0:top, at]
        values = [
            att[i, :, j * QROWS : (j + 1) * QROWS].astype(F32) * weights[j : j + 1, :] for j in range(top)
        ]
        for e in range(p.mixers):
            mix[e * cols : (e + 1) * cols, pl.ds(start, QROWS)] = spread_rows(p, table, values, e).astype(BF)

    def branch(index):
        lanes = pl.ds(aligned(index * p.seq, p.seq), p.seq)
        return mm(w_ref[:, p.qkv :], mix[:, lanes])

    total = pack_sum(p, branch, part, own, near_in, far_out, far_in, sems[4:8])
    state = h_ref[...] + total.T
    middle[...] = state
    inverse = lax.rsqrt(jnp.mean(state * state, axis=-1, keepdims=True) + EPSILON)
    m_ref[...] = (state * inverse * gain_two[...]).astype(BF)


def attention_backward_kernel(
    p, step, first, grad_ref, base_ref, h_ref, gain_one, w_ref, router_col, picks, seg_rows, seg_cols,
    nt, qs, kt, vt, lse, att, mix, gates, *rest,
):
    if first:
        before, router_before, gain_before = None, None, None
    else:
        before, router_before, gain_before = rest[0:3]
        rest = rest[3:]
    grad_in, grad_w, grad_router, grad_gain = rest[0:4]
    gt, wo, k_heads, v_heads, da, dlog, dkt, dvt, dall, part, own, near_in, far_out, far_in = rest[4:18]
    sems = rest[18:]
    b, _ = place()
    cols, top = p.cols, p.top
    sub = p.seq // QROWS
    greet(pack_peers(p))
    gt[b] = grad_ref[...].T.astype(BF)
    spread = PackGather(p, gt, sems[0:2], sems[2:4])
    spread.begin()
    for start in range(0, p.mixers * cols, 2 * cols):
        piece = w_ref[:, p.qkv + start : p.qkv + start + 2 * cols]
        wo[start : start + 2 * cols, :] = piece.astype(F32).T.astype(BF)
    dkt[...] = jnp.zeros_like(dkt)
    dvt[...] = jnp.zeros_like(dvt)

    @pl.loop(0, (p.length + MAXLEN) // QROWS)
    def _(k):
        at = aligned(k * QROWS, QROWS)

        def put_key(head, rows):
            k_heads[head, pl.ds(at, QROWS), :] = rows

        def put_value(head, rows):
            v_heads[head, pl.ds(at, QROWS), :] = rows

        head_rows(p, put_key, kt[:, pl.ds(at, QROWS)].astype(F32))
        head_rows(p, put_value, vt[:, pl.ds(at, QROWS)].astype(F32))

    spread.finish()

    @pl.loop(0, p.blk)
    def _(bb):
        table = picks[bb, step * top : (step + 1) * top, :]
        weights = gates[bb, 0:top, :]
        values = mm(wo[...], gt[bb])
        for k in range(sub):
            lanes = slice(k * QROWS, (k + 1) * QROWS)
            here = table[:, lanes]
            picked = pick_rows(p, here, lambda e: values[e * cols : (e + 1) * cols, lanes])
            grads = []
            for j in range(top):
                slot = slice(j * QROWS, (j + 1) * QROWS)
                past = att[bb * sub + k, :, slot].astype(F32)
                grads.append(jnp.sum(picked[j] * past, axis=0, keepdims=True))
                da[bb * sub + k, :, slot] = (picked[j] * weights[j : j + 1, lanes]).astype(BF)
            mean = sum(weights[j : j + 1, lanes] * grads[j] for j in range(top))
            back = [weights[j : j + 1, lanes] * (grads[j] - mean) for j in range(top)]
            for e in range(p.mixers):
                dlog[bb, e : e + 1, lanes] = spread_rows(p, here, back, e)

    @pl.loop(0, p.blocks)
    def _(i):
        start = aligned(i * QROWS, QROWS)
        keys = pl.ds(start, WINDOW)
        bias = attention_mask(seg_cols, seg_rows, start)
        bias = jnp.concatenate([bias] * top, axis=1)
        queries = qs[i]
        grads = da[i]
        past = att[i]
        query_grads = []
        for head in range(p.heads):
            rows = slice(head * HD, (head + 1) * HD)
            scores = mm(k_heads[head, keys, :], queries) + bias
            probs = jnp.exp(scores - lse[i, head : head + 1, :])
            mean = jnp.sum(grads[rows].astype(F32) * past[rows].astype(F32), axis=0, keepdims=True)
            dscores = (probs * (mm(v_heads[head, keys, :], grads) - mean)).astype(BF)
            dvt[rows, keys] += mm_nt(grads[rows], probs.astype(BF))
            dkt[rows, keys] += mm_nt(queries[rows], dscores)
            query_grads.append(mm(kt[rows, keys], dscores) * (HD**-0.5))
        bb = i // sub
        at = pl.ds(aligned(lax.rem(i, sub) * QROWS, QROWS), QROWS)
        table = picks[bb, step * top : (step + 1) * top, at]
        merged = jnp.concatenate(query_grads, axis=0)
        values = [merged[:, j * QROWS : (j + 1) * QROWS] for j in range(top)]
        for e in range(p.mixers):
            dall[e * cols : (e + 1) * cols, pl.ds(start, QROWS)] = spread_rows(p, table, values, e).astype(BF)

    dall[p.mixers * cols : (p.mixers + 1) * cols, :] = dkt[:, MAXLEN:].astype(BF)
    dall[(p.mixers + 1) * cols :, :] = dvt[:, MAXLEN:].astype(BF)

    def branch(index):
        lanes = pl.ds(aligned(index * p.seq, p.seq), p.seq)
        return mm(w_ref[:, : p.qkv], dall[:, lanes]) + mm(router_col[...], dlog[index].astype(BF))

    total = pack_sum(p, branch, part, own, near_in, far_out, far_in, sems[4:8])
    grad_n = total.T
    h = h_ref[...]
    inverse = lax.rsqrt(jnp.mean(h * h, axis=-1, keepdims=True) + EPSILON)
    scaled = grad_n * gain_one[...]
    back = inverse * scaled - h * (inverse * inverse * inverse) * jnp.mean(scaled * h, axis=-1, keepdims=True)
    grad_in[...] = (base_ref[...] + grad_ref[...] + back if first else grad_ref[...] + back).astype(grad_in.dtype)
    gain = jnp.sum(grad_n * h * inverse, axis=0, keepdims=True)
    grad_gain[...] = gain if first else gain_before[...] + gain
    router = sum(mm_nt(dlog[bb].astype(BF), nt[bb]) for bb in range(p.blk))
    grad_router[...] = router if first else router_before[...] + router
    tile = 2 * cols
    for start in range(0, p.all_cols, tile):
        total = None
        for bb in range(p.blk):
            lanes = slice(bb * p.seq, (bb + 1) * p.seq)
            if start < p.qkv:
                term = mm_nt(nt[bb], dall[start : start + tile, lanes])
            else:
                term = mm_nt(gt[bb], mix[start - p.qkv : start - p.qkv + tile, lanes])
            total = term if total is None else total + term
        at = slice(start, start + tile)
        grad_w[:, at] = total if first else before[:, at] + total


def own_lane(p):
    b, d = place()
    mine = d * p.local + b // p.group
    return jnp.where(lax.broadcasted_iota(jnp.int32, (1, LANES), 1) == mine, 1.0, 0.0)


def slot_gates(p, rows, pair, router):
    own = own_lane(p)
    logits = mm(rows, router)
    return 1.0 / (1.0 + jnp.exp(jnp.sum(logits * (pair - 2.0 * own), axis=-1, keepdims=True)))


def gelu_of(inner):
    return inner * (0.5 * (1.0 + lax.erf(inner * 0.7071067811865476)))


def gelu_both(inner):
    half = 0.5 * (1.0 + lax.erf(inner * 0.7071067811865476))
    slope = half + inner * jnp.exp(-0.5 * inner * inner) * 0.3989422804014327
    return inner * half, slope


FTILE = 512


def expert_forward(p, rows, w_in, w_back):
    total = None
    for start in range(0, p.ff, FTILE):
        at = slice(start, start + FTILE)
        act = gelu_of(mm(rows, w_in[:, at])).astype(BF)
        term = mm(act, w_back[at, :])
        total = term if total is None else total + term
    return total


def expert_backward(p, arrived, grads, w_in, w_back, grad_w_in, grad_w_back, before_in, before_back, arrived_t, grad_rows):
    arrived_t[...] = arrived[...].astype(F32).T.astype(BF)
    for k, start in enumerate(range(0, p.ff, FTILE)):
        at = slice(start, start + FTILE)
        act, slope = gelu_both(mm(arrived[...], w_in[:, at]))
        act_t = act.T.astype(BF)
        rows = grads[...]
        term = mm(act_t, rows)
        grad_w_back[at, :] = term if before_back is None else before_back[at, :] + term
        inner = (mm_nt(rows, w_back[at, :]) * slope).astype(BF)
        term = mm(arrived_t[...], inner)
        grad_w_in[:, at] = term if before_in is None else before_in[:, at] + term
        term = mm_nt(inner, w_in[:, at])
        if k == 0:
            grad_rows[...] = term
        else:
            grad_rows[...] += term


def router_back(p, gate, dots, pair, arrived, router, grad_rows):
    coeff = gate * (1.0 - gate) * dots * (2.0 * own_lane(p) - pair)
    grad_rows[...] += mm_nt(coeff.astype(BF), router)
    return mm(coeff.T.astype(BF), arrived)


def expert_forward_kernel(
    p, m_ref, middle, disp, comb, pair, w_in, w_back, router,
    out_ref, arrived, produced, outgoing, ret_out, ret_in, *sems,
):
    greet(slot_peers(p))
    outgoing[...] = mm(disp[...], m_ref[...]).astype(BF)
    arrived[0 : p.cap, :] = outgoing[0 : p.cap, :]
    there = {s: slot_send(p, outgoing, arrived, sems[0:2], s, slot_peer(p, s)) for s in range(1, p.experts)}
    back = []
    per = max(1, p.experts // 4)
    for first in range(0, p.experts, per):
        for s in range(max(first, 1), first + per):
            there[s].wait_recv()
        at = pl.ds(first * p.cap, per * p.cap)
        rows = arrived[at, :]
        out = expert_forward(p, rows, w_in, w_back)
        produced[at, :] = out.astype(BF)
        ret_out[at, :] = (out * slot_gates(p, rows, pair[at, :].astype(F32), router[...])).astype(BF)
        for s in range(max(first, 1), first + per):
            back.append(slot_send(p, ret_out, ret_in, sems[2:4], s, slot_source(p, s)))
    ret_in[0 : p.cap, :] = ret_out[0 : p.cap, :]
    for copy in back:
        copy.wait()
    for copy in there.values():
        copy.wait_send()
    out_ref[...] = middle[...] + mm(comb[...], ret_in[...])


def norm_two_back(middle, gain, grad_m, grad_out):
    state = middle[...]
    inverse = lax.rsqrt(jnp.mean(state * state, axis=-1, keepdims=True) + EPSILON)
    scaled = grad_m * gain[...]
    back = inverse * scaled - state * (inverse * inverse * inverse) * jnp.mean(
        scaled * state, axis=-1, keepdims=True
    )
    return grad_out + back, jnp.sum(grad_m * state * inverse, axis=0, keepdims=True)


def expert_both_kernel(
    p, m_ref, middle, first_ref, cot_ref, halt, gain_two, disp, comb, pair, w_in, w_back, router,
    result, grad_first, grad_middle, grad_gain, grad_halt, grad_w_in, grad_w_back, grad_router,
    outgoing, arrived, u_out, u_in, ret_out, ret_in, gret_out, gret_in, arrived_t, grads, grad_rows, produced, *sems,
):
    greet(slot_peers(p))
    outgoing[...] = mm(disp[...], m_ref[...]).astype(BF)
    arrived[0 : p.cap, :] = outgoing[0 : p.cap, :]
    there = {s: slot_send(p, outgoing, arrived, sems[0:2], s, slot_peer(p, s)) for s in range(1, p.experts)}
    first = first_ref[...]
    cot = cot_ref[...].astype(F32)
    stop = 1.0 / (1.0 + jnp.exp(-jnp.sum(first * halt[...], axis=-1, keepdims=True)))
    u_out[...] = mm(disp[...], ((1.0 - stop) * cot).astype(BF)).astype(BF)
    u_in[0 : p.cap, :] = u_out[0 : p.cap, :]
    there_u = [slot_send(p, u_out, u_in, sems[4:6], s, slot_peer(p, s)) for s in range(1, p.experts)]
    back = []
    per = max(1, p.experts // 4)
    for begin in range(0, p.experts, per):
        for s in range(max(begin, 1), begin + per):
            there[s].wait_recv()
        at = pl.ds(begin * p.cap, per * p.cap)
        rows = arrived[at, :]
        out = expert_forward(p, rows, w_in, w_back)
        produced[at, :] = out
        ret_out[at, :] = (out * slot_gates(p, rows, pair[at, :].astype(F32), router[...])).astype(BF)
        for s in range(max(begin, 1), begin + per):
            back.append(slot_send(p, ret_out, ret_in, sems[2:4], s, slot_source(p, s)))
    ret_in[0 : p.cap, :] = ret_out[0 : p.cap, :]
    for copy in there_u:
        copy.wait_recv()
    pairs = pair[...].astype(F32)
    gate = slot_gates(p, arrived[...], pairs, router[...])
    u = u_in[...].astype(F32)
    grads[...] = (u * gate).astype(BF)
    dots = jnp.sum(u * produced[...], axis=-1, keepdims=True)
    expert_backward(
        p, arrived, grads, w_in, w_back, grad_w_in, grad_w_back, None, None, arrived_t, grad_rows
    )
    grad_router[...] = router_back(p, gate, dots, pairs, arrived[...], router[...], grad_rows)
    gret_out[...] = grad_rows[...].astype(BF)
    gret_in[0 : p.cap, :] = gret_out[0 : p.cap, :]
    back_g = [slot_send(p, gret_out, gret_in, sems[6:8], s, slot_source(p, s)) for s in range(1, p.experts)]
    for copy in back:
        copy.wait()
    second = middle[...] + mm(comb[...], ret_in[...])
    result[...] = (stop * first + (1.0 - stop) * second).astype(BF)
    grad_stop = jnp.sum(cot * (first - second), axis=-1, keepdims=True)
    coeff = grad_stop * stop * (1.0 - stop)
    grad_halt[...] = jnp.sum(coeff * first, axis=0, keepdims=True)
    grad_first[...] = stop * cot + coeff * halt[...]
    for copy in back_g:
        copy.wait()
    for copy in list(there.values()) + there_u:
        copy.wait_send()
    grad_middle[...], grad_gain[...] = norm_two_back(
        middle, gain_two, mm(comb[...], gret_in[...]), (1.0 - stop) * cot
    )


def expert_backward_kernel(
    p, g_ref, middle, gain_two, gain_before, disp, comb, pair, w_in, w_back, router, arrived, produced,
    before_in, before_back, before_router,
    grad_middle, grad_gain, grad_w_in, grad_w_back, grad_router,
    u_out, u_in, gret_out, gret_in, arrived_t, grads, grad_rows, *sems,
):
    greet(slot_peers(p))
    u_out[...] = mm(disp[...], g_ref[...].astype(BF)).astype(BF)
    u_in[0 : p.cap, :] = u_out[0 : p.cap, :]
    there = [slot_send(p, u_out, u_in, sems[0:2], s, slot_peer(p, s)) for s in range(1, p.experts)]
    pairs = pair[...].astype(F32)
    gate = slot_gates(p, arrived[...], pairs, router[...])
    for copy in there:
        copy.wait_recv()
    u = u_in[...].astype(F32)
    grads[...] = (u * gate).astype(BF)
    dots = jnp.sum(u * produced[...].astype(F32), axis=-1, keepdims=True)
    expert_backward(
        p, arrived, grads, w_in, w_back, grad_w_in, grad_w_back, before_in, before_back, arrived_t, grad_rows
    )
    grad_router[...] = before_router[...] + router_back(p, gate, dots, pairs, arrived[...], router[...], grad_rows)
    gret_out[...] = grad_rows[...].astype(BF)
    gret_in[0 : p.cap, :] = gret_out[0 : p.cap, :]
    back = [slot_send(p, gret_out, gret_in, sems[2:4], s, slot_source(p, s)) for s in range(1, p.experts)]
    for copy in back:
        copy.wait()
    for copy in there:
        copy.wait_send()
    grad_middle[...], gain = norm_two_back(middle, gain_two, mm(comb[...], gret_in[...]), g_ref[...])
    grad_gain[...] = gain_before[...] + gain


def sums_kernel(
    p, grad_w, grad_in, grad_back, small, out_w, out_in, out_back, out_small,
    w_out1, w_in1, w_out2, w_in2, in_out1, in_in1, in_out2, in_in2, bk_out1, bk_in1, bk_out2, bk_in2, all_small, *sems,
):
    b, d = place()
    z, x = d // p.lo, lax.rem(d, p.lo)
    y, c = b // 2, lax.rem(b, 2)
    e, g = b // p.group, lax.rem(b, p.group)
    greet(pack_peers(p) + dp_peers(p) + expert_peers(p))
    rows = out_w.shape[0]
    in_rows, back_rows = out_in.shape[1], out_back.shape[1]
    lo, hi, near, wide, tiny = (sems[2 * k : 2 * k + 2] for k in range(5))

    def rows_of(ref, index, size):
        return ref[pl.ds(aligned(index * size, size), size), :]

    near_copies = {}
    for k in range(p.local):
        to = turn(e, k + 1, p.local)
        for t in range(1, p.group):
            member = turn(g, t, p.group)
            slot = k * (p.group - 1) + t - 1
            in_out1[slot] = rows_of(grad_in, to * p.group + member, in_rows).astype(BF)
            bk_out1[slot] = rows_of(grad_back, to * p.group + member, back_rows).astype(BF)
            peer = (e * p.group + member, d)
            near_copies[k, t] = [
                send(in_out1.at[slot], in_in1.at[slot], near, 2 * slot, peer),
                send(bk_out1.at[slot], bk_in1.at[slot], near, 2 * slot + 1, peer),
            ]
    lo_copies = {}
    for k in range(p.hi):
        to = turn(z, k + 1, p.hi)
        for t in range(1, p.lo):
            slot = k * (p.lo - 1) + t - 1
            xx = turn(x, t, p.lo)
            w_out1[slot] = rows_of(grad_w, to * p.lo + xx, rows).astype(BF)
            lo_copies[k, t] = send(w_out1.at[slot], w_in1.at[slot], lo, slot, (b, z * p.lo + xx))
    wide_copies = []
    for k in range(p.local):
        to = turn(e, k + 1, p.local)
        for copies in [near_copies[k, t] for t in range(1, p.group)]:
            for copy in copies:
                copy.wait_recv()
        slots = [k * (p.group - 1) + t - 1 for t in range(1, p.group)]
        total_in = rows_of(grad_in, to * p.group + g, in_rows)
        total_back = rows_of(grad_back, to * p.group + g, back_rows)
        for slot in slots:
            total_in = total_in + in_in1[slot].astype(F32)
            total_back = total_back + bk_in1[slot].astype(F32)
        if k < p.local - 1:
            in_out2[k] = total_in.astype(BF)
            bk_out2[k] = total_back.astype(BF)
            peer = (to * p.group + g, d)
            wide_copies.append(send(in_out2.at[k], in_in2.at[k], wide, 2 * k, peer))
            wide_copies.append(send(bk_out2.at[k], bk_in2.at[k], wide, 2 * k + 1, peer))
        else:
            out_in[e] = total_in
            out_back[e] = total_back
    hi_copies = []
    total_w = None
    for k in range(p.hi):
        to = turn(z, k + 1, p.hi)
        for t in range(1, p.lo):
            lo_copies[k, t].wait_recv()
        total = rows_of(grad_w, to * p.lo + x, rows)
        for t in range(1, p.lo):
            total = total + w_in1[k * (p.lo - 1) + t - 1].astype(F32)
        if k < p.hi - 1:
            w_out2[k] = total.astype(BF)
            hi_copies.append(send(w_out2.at[k], w_in2.at[k], hi, k, (b, to * p.lo + x)))
        else:
            total_w = total
    current = small[...]
    tiny_copies = []
    sem = 0
    axes = (
        (2, c, lambda t: (2 * y + turn(c, t, 2), d)),
        (p.chips, y, lambda t: (2 * turn(y, t, p.chips) + c, d)),
        (p.lo, x, lambda t: (b, z * p.lo + turn(x, t, p.lo))),
        (p.hi, z, lambda t: (b, turn(z, t, p.hi) * p.lo + x)),
    )
    base = 0
    for size, index, peer in axes:
        all_small[base + index] = current
        copies = []
        for t in range(1, size):
            at = all_small.at[base + index]
            copies.append(send(at, at, tiny, sem, peer(t)))
            sem += 1
        for copy in copies:
            copy.wait_recv()
        current = all_small[base]
        for k in range(1, size):
            current = current + all_small[base + k]
        base += size
        tiny_copies += copies
    out_small[...] = current
    for k, copy in enumerate(hi_copies):
        copy.wait_recv()
        total_w = total_w + w_in2[k].astype(F32)
    out_w[...] = total_w
    for copy in wide_copies:
        copy.wait_recv()
    for k in range(p.local - 1):
        source = turn(e, -(k + 1), p.local)
        out_in[source] = in_in2[k].astype(F32)
        out_back[source] = bk_in2[k].astype(F32)
    for copies in near_copies.values():
        for copy in copies:
            copy.wait_send()
    for copy in list(lo_copies.values()) + wide_copies + hi_copies + tiny_copies:
        copy.wait_send()


def dma_pairs(*sizes):
    return [pltpu.SemaphoreType.DMA((max(1, size),)) for size in sizes for _ in range(2)]


def call(kernel, name, number, outs, ins, scratch, any_in=(), any_out=()):
    vmem = pl.BlockSpec(memory_space=pltpu.VMEM)
    anywhere = pl.BlockSpec(memory_space=pl.ANY)
    return pl.pallas_call(
        kernel,
        out_shape=tuple(jax.ShapeDtypeStruct(shape, dtype) for shape, dtype in outs),
        in_specs=[anywhere if k in any_in else vmem for k in range(len(ins))],
        out_specs=tuple(anywhere if k in any_out else vmem for k in range(len(outs))),
        scratch_shapes=scratch,
        compiler_params=pltpu.CompilerParams(
            collective_id=number, has_side_effects=True, vmem_limit_bytes=VMEM_BYTES
        ),
        name=name,
    )(*ins)


def on_device(
    inputs,
    segments,
    attention_routes,
    expert_routes,
    gain_mixer,
    gain_expert,
    weight_query,
    weight_key,
    weight_value,
    weight_out,
    router_mixer,
    router_expert,
    weight_in,
    weight_back,
    halt_weight,
    cotangent,
):
    blk, dp = lax.axis_size("blk"), lax.axis_size("dp")
    seq, width = inputs.shape[1:]
    experts, local = router_expert.shape[1], weight_in.shape[0]
    slots_of = max(2, 3 * seq // experts)
    hi = 4
    p = Plan(
        blk=blk,
        dp=dp,
        lo=dp // hi,
        hi=hi,
        seq=seq,
        width=width,
        heads=HEADS // blk,
        mixers=weight_query.shape[0],
        top=attention_routes.shape[-1],
        experts=experts,
        local=local,
        group=blk // local,
        cap=-(-slots_of // 16) * 16,
        ff=weight_in.shape[2],
    )
    cols, length, blocks, top = p.cols, p.length, p.blocks, p.top
    share = weight_key.shape[0]

    wall = jnp.concatenate(
        [
            jnp.transpose(weight_query, (1, 0, 2)).reshape(share, p.mixers * cols),
            weight_key,
            weight_value,
            jnp.transpose(weight_out, (2, 0, 1)).reshape(share, p.mixers * cols),
        ],
        axis=1,
    )
    picks = jnp.transpose(attention_routes[:, 0], (0, 2, 1)).reshape(2 * top, seq)
    routes = jnp.transpose(expert_routes[:, 0], (0, 2, 1)).reshape(-1, seq)
    seg_rows = segments.reshape(1, length)
    seg_cols = jnp.pad(segments[0], (MAXLEN, 0), constant_values=-1).reshape(length + MAXLEN, 1)
    gain_one = gain_mixer.astype(F32).reshape(1, width)
    gain_two = gain_expert.astype(F32).reshape(1, width)
    halt = halt_weight.astype(F32).reshape(1, width)
    router_row = router_mixer.T
    router = jnp.pad(router_expert, ((0, 0), (0, LANES - experts)))
    start = inputs[0].astype(F32)

    all_w, all_in, all_back, all_picks, disp, comb, _, pair = call(
        functools.partial(setup_kernel, p),
        "setup",
        0,
        [
            ((width, p.all_cols), BF),
            ((width, p.ff), BF),
            ((p.ff, width), BF),
            ((blk, 2 * top, seq), jnp.int32),
            ((2, p.slots, seq), BF),
            ((2, seq, p.slots), BF),
            ((2, p.slots, LANES), BF),
            ((2, p.slots, LANES), BF),
        ],
        [wall, weight_in, weight_back, picks, routes],
        dma_pairs(
            p.hi - 1,
            p.hi * (p.lo - 1),
            2 * (p.local - 1),
            2 * p.local * (p.group - 1),
        )
        + pack_sems(p)
        + dma_pairs(2 * p.experts)
        + [pltpu.SemaphoreType.DMA((3,))],
        any_in=(0, 1, 2),
        any_out=(0, 1, 2),
    )

    def pack_scratch():
        return [
            pltpu.VMEM((blk, width, seq), BF),
            pltpu.VMEM((width, seq), F32),
            pltpu.VMEM((p.chips, width, seq), BF),
            pltpu.VMEM((max(1, p.chips - 1), width, seq), BF),
            pltpu.VMEM((max(1, p.chips - 1), width, seq), BF),
        ] + pack_sems(p) * 2

    def attention_forward(state, step):
        return call(
            functools.partial(attention_forward_kernel, p, step),
            f"attention_forward_{step}",
            1 + step,
            [
                ((seq, width), F32),
                ((seq, width), BF),
                ((blk, width, seq), BF),
                ((blocks, cols, top * QROWS), BF),
                ((cols, length + MAXLEN), BF),
                ((cols, length + MAXLEN), BF),
                ((blocks, 8, top * QROWS), F32),
                ((blocks, cols, top * QROWS), BF),
                ((p.mixers * cols, length), BF),
                ((blk, 8, seq), F32),
            ],
            [state, gain_one, gain_two, all_w, router_row, all_picks, seg_rows, seg_cols],
            [
                pltpu.VMEM((p.qkv, width), BF),
                pltpu.VMEM((p.heads, length + MAXLEN, cols), BF),
            ]
            + pack_scratch(),
        )

    def attention_backward(grad, base, state, saved, step, before):
        ins = [grad, base, state, gain_one, all_w, router_mixer, all_picks, seg_rows, seg_cols, *saved]
        return call(
            functools.partial(attention_backward_kernel, p, step, before is None),
            f"attention_backward_{step}",
            3 + step,
            [
                ((seq, width), F32 if before is None else BF),
                ((width, p.all_cols), F32),
                ((p.mixers, width), F32),
                ((1, width), F32),
            ],
            ins + ([] if before is None else list(before)),
            [
                pltpu.VMEM((blk, width, seq), BF),
                pltpu.VMEM((p.mixers * cols, width), BF),
                pltpu.VMEM((p.heads, length + MAXLEN, cols), BF),
                pltpu.VMEM((p.heads, length + MAXLEN, cols), BF),
                pltpu.VMEM((blocks, cols, top * QROWS), BF),
                pltpu.VMEM((blk, p.mixers, seq), F32),
                pltpu.VMEM((cols, length + MAXLEN), F32),
                pltpu.VMEM((cols, length + MAXLEN), F32),
                pltpu.VMEM((p.qkv, length), BF),
            ]
            + pack_scratch(),
        )

    rows_bf = pltpu.VMEM((p.slots, width), BF)
    rows_f = pltpu.VMEM((p.slots, width), F32)
    cols_bf = pltpu.VMEM((width, p.slots), BF)

    middle0, m0, *saved0 = attention_forward(start, 0)
    first, arrived0, produced0 = call(
        functools.partial(expert_forward_kernel, p),
        "expert_forward",
        5,
        [((seq, width), F32), ((p.slots, width), BF), ((p.slots, width), BF)],
        [m0, middle0, disp[0], comb[0], pair[0], all_in, all_back, router],
        [rows_bf] * 3 + dma_pairs(p.experts, p.experts),
    )
    middle1, m1, *saved1 = attention_forward(first, 1)
    result, grad_first, grad_middle1, gain_two1, grad_halt, in1, back1, router1 = call(
        functools.partial(expert_both_kernel, p),
        "expert_both",
        6,
        [
            ((seq, width), BF),
            ((seq, width), F32),
            ((seq, width), F32),
            ((1, width), F32),
            ((1, width), F32),
            ((width, p.ff), F32),
            ((p.ff, width), F32),
            ((LANES, width), F32),
        ],
        [m1, middle1, first, cotangent[0], halt, gain_two, disp[1], comb[1], pair[1], all_in, all_back, router],
        [rows_bf] * 8
        + [cols_bf, rows_bf, rows_f, rows_f]
        + dma_pairs(p.experts, p.experts, p.experts, p.experts),
    )
    grad_first, w1, mixer1, gain_one1 = attention_backward(grad_middle1, grad_first, first, saved1, 1, None)
    grad_middle0, grad_gain_two, grad_in, grad_back, grad_router = call(
        functools.partial(expert_backward_kernel, p),
        "expert_backward",
        7,
        [
            ((seq, width), F32),
            ((1, width), F32),
            ((width, p.ff), F32),
            ((p.ff, width), F32),
            ((LANES, width), F32),
        ],
        [
            grad_first, middle0, gain_two, gain_two1, disp[0], comb[0], pair[0], all_in, all_back, router,
            arrived0, produced0, in1, back1, router1,
        ],
        [rows_bf] * 4 + [cols_bf, rows_bf, rows_f] + dma_pairs(p.experts, p.experts),
    )
    input_grad, grad_w, grad_mixer, grad_gain_one = attention_backward(
        grad_middle0, grad_middle0, start, saved0, 0, (w1, mixer1, gain_one1)
    )
    small = jnp.concatenate(
        [
            grad_gain_one,
            grad_gain_two,
            grad_halt,
            jnp.zeros((5, width), F32),
            grad_mixer,
            grad_router[:experts],
        ]
    )
    in_rows, back_rows = weight_in.shape[1], weight_back.shape[1]
    near = p.local * (p.group - 1)
    far = max(1, p.local - 1)
    out_w, out_in, out_back, small = call(
        functools.partial(sums_kernel, p),
        "sums",
        8,
        [
            ((share, p.all_cols), F32),
            ((local, in_rows, p.ff), F32),
            ((local, back_rows, width), F32),
            (small.shape, F32),
        ],
        [grad_w, grad_in, grad_back, small],
        [pltpu.VMEM((p.hi * (p.lo - 1), share, p.all_cols), BF)] * 2
        + [pltpu.VMEM((p.hi - 1, share, p.all_cols), BF)] * 2
        + [pltpu.VMEM((near, in_rows, p.ff), BF)] * 2
        + [pltpu.VMEM((far, in_rows, p.ff), BF)] * 2
        + [pltpu.VMEM((near, back_rows, width), BF)] * 2
        + [pltpu.VMEM((far, back_rows, width), BF)] * 2
        + [pltpu.VMEM((2 + p.chips + p.lo + p.hi, *small.shape), F32)]
        + dma_pairs(
            p.hi * (p.lo - 1),
            p.hi - 1,
            2 * near,
            2 * (p.local - 1),
            2 + p.chips + p.lo + p.hi,
        ),
    )
    q_cols = p.mixers * cols
    query = jnp.transpose(out_w[:, :q_cols].reshape(share, p.mixers, cols), (1, 0, 2))
    out = jnp.transpose(out_w[:, p.qkv :].reshape(share, p.mixers, cols), (1, 2, 0))
    return (
        result[None],
        input_grad[None],
        small[0],
        small[1],
        query,
        out_w[:, q_cols : q_cols + cols],
        out_w[:, q_cols + cols : p.qkv],
        out,
        small[8 : 8 + p.mixers].T,
        small[8 + p.mixers :].T,
        out_in,
        out_back,
        small[2],
    )


def solution(mesh):
    return jax.shard_map(
        on_device,
        mesh=mesh,
        in_specs=(
            P("dp", "blk", None),
            P("dp", None),
            P(None, "dp", "blk", None),
            P(None, "dp", "blk", None),
            P(),
            P(),
            P(None, "dp", "blk"),
            P("dp", "blk"),
            P("dp", "blk"),
            P(None, "blk", "dp"),
            P(),
            P(),
            P("dp", "blk", None),
            P("dp", "blk", None),
            P(),
            P("dp", "blk", None),
        ),
        out_specs=(
            P("dp", "blk", None),
            P("dp", "blk", None),
            P(),
            P(),
            P(None, "dp", "blk"),
            P("dp", "blk"),
            P("dp", "blk"),
            P(None, "blk", "dp"),
            P(),
            P(),
            P("dp", "blk", None),
            P("dp", "blk", None),
            P(),
        ),
        check_vma=False,
    )
```

```python
import functools
from types import SimpleNamespace
from typing import NamedTuple

import jax
import jax.numpy as jnp
from jax import lax
from jax.experimental import pallas as pl
from jax.experimental.pallas import tpu as pltpu
from jax.sharding import PartitionSpec as P

HEADS = 8
HD = 64
MAXLEN = 256
QROWS = 128
WINDOW = MAXLEN + QROWS
LANES = 128
EPSILON = 1e-06
MASKED_SCORE = -1e30
MESH = pl.DeviceIdType.MESH
BF = jnp.bfloat16
F32 = jnp.float32
VMEM_BYTES = 61 * 2**20


class Plan(NamedTuple):
    blk: int
    dp: int
    lo: int
    hi: int
    seq: int
    width: int
    heads: int
    mixers: int
    top: int
    experts: int
    local: int
    group: int
    cap: int
    ff: int

    @property
    def length(self):
        return self.blk * self.seq

    @property
    def cols(self):
        return self.heads * HD

    @property
    def qkv(self):
        return (self.mixers + 2) * self.cols

    @property
    def all_cols(self):
        return (2 * self.mixers + 2) * self.cols

    @property
    def blocks(self):
        return self.length // QROWS

    @property
    def slots(self):
        return self.experts * self.cap

    @property
    def tile(self):
        return 512 if self.slots <= 768 else 256

    @property
    def chips(self):
        return self.blk // 2


def mm(a, b):
    return lax.dot_general(a, b, (((1,), (0,)), ((), ())), preferred_element_type=F32)


def mm_nt(a, b):
    return lax.dot_general(a, b, (((1,), (1,)), ((), ())), preferred_element_type=F32)


def place():
    return lax.axis_index("blk"), lax.axis_index("dp")


def turn(index, by, size):
    return lax.rem(index + (by % size), size)


def greet(peers):
    barrier = pltpu.get_barrier_semaphore()
    for peer in peers:
        pl.semaphore_signal(barrier, inc=1, device_id=peer, device_id_type=MESH)
    pl.semaphore_wait(barrier, len(peers))


def send(src, dst, sems, slot, peer):
    copy = pltpu.make_async_remote_copy(
        src_ref=src,
        dst_ref=dst,
        send_sem=sems[0].at[slot],
        recv_sem=sems[1].at[slot],
        device_id=peer,
        device_id_type=MESH,
    )
    copy.start()
    return copy


def aligned(value, by):
    return pl.multiple_of(value, by)


def pack_peers(p):
    b, d = place()
    y, c = b // 2, lax.rem(b, 2)
    peers = [(2 * y + 1 - c, d)]
    return peers + [(2 * turn(y, s, p.chips) + c, d) for s in range(1, p.chips)]


def slot_peer(p, s):
    b, d = place()
    e, g = b // p.group, lax.rem(b, p.group)
    return (turn(e, s // p.dp, p.local) * p.group + g, turn(d, s % p.dp, p.dp))


def slot_peers(p):
    return [slot_peer(p, s) for s in range(1, p.experts)]


def slot_source(p, s):
    b, d = place()
    e, g = b // p.group, lax.rem(b, p.group)
    return (turn(e, -(s // p.dp), p.local) * p.group + g, turn(d, -(s % p.dp), p.dp))


def dp_peers(p):
    b, d = place()
    z, x = d // p.lo, lax.rem(d, p.lo)
    peers = [(b, turn(z, s, p.hi) * p.lo + x) for s in range(1, p.hi)]
    return peers + [(b, z * p.lo + turn(x, t, p.lo)) for t in range(1, p.lo)]


def expert_peers(p):
    b, d = place()
    e, g = b // p.group, lax.rem(b, p.group)
    peers = [(turn(e, s, p.local) * p.group + g, d) for s in range(1, p.local)]
    return peers + [(e * p.group + turn(g, t, p.group), d) for t in range(1, p.group)]


class PackGather:
    def __init__(self, p, buf, sems):
        self.p, self.buf, self.far, self.near = p, buf, sems[0:2], sems[2:4]
        self.done_near = self.done_far = False

    def begin(self):
        p = self.p
        b, d = place()
        y, c = b // 2, lax.rem(b, 2)
        own = self.buf.at[b]
        self.first = [
            send(own, own, self.far, s - 1, (2 * turn(y, s, p.chips) + c, d))
            for s in range(1, p.chips)
        ]
        self.second = [send(own, own, self.near, 0, (2 * y + 1 - c, d))]

    def finish_near(self):
        if not self.done_near:
            self.second[0].wait_recv()
        self.done_near = True

    def finish_far(self):
        if self.done_far:
            return
        self.done_far = True
        p = self.p
        b, d = place()
        y, c = b // 2, lax.rem(b, 2)
        for s in range(1, p.chips):
            self.first[s - 1].wait_recv()
            block = self.buf.at[2 * turn(y, -s, p.chips) + c]
            self.second.append(send(block, block, self.near, s, (2 * y + 1 - c, d)))
        self.finish_near()
        for copy in self.second[1:]:
            copy.wait_recv()

    def end(self):
        for copy in self.first + self.second:
            copy.wait_send()


class PackSum:
    def __init__(self, p, bufs, sems):
        self.p, self.bufs = p, bufs
        self.far, self.near = sems[0:2], sems[2:4]
        self.first, self.second = {}, []

    def give(self, s, term):
        p, r = self.p, self.bufs
        b, d = place()
        y, c = b // 2, lax.rem(b, 2)
        r.part[s] = term.astype(BF)
        self.first[s] = send(r.part.at[s], r.near_in.at[s], self.near, s, (2 * y + 1 - c, d))

    def pass_on(self, s, term):
        p, r = self.p, self.bufs
        b, d = place()
        y, c = b // 2, lax.rem(b, 2)
        self.first[s].wait_recv()
        r.far_out[s - 1] = (term + r.near_in[s].astype(F32)).astype(BF)
        self.second.append(
            send(r.far_out.at[s - 1], r.far_in.at[s - 1], self.far, s - 1, (2 * turn(y, s, p.chips) + c, d))
        )

    def total(self, term):
        r = self.bufs
        self.first[0].wait_recv()
        term = term + r.near_in[0].astype(F32)
        for k, copy in enumerate(self.second):
            copy.wait_recv()
            term = term + r.far_in[k].astype(F32)
        for copy in list(self.first.values()) + self.second:
            copy.wait_send()
        return term


def slot_send(p, src, dst, sems, s, peer):
    rows = pl.ds(s * p.cap, p.cap)
    return send(src.at[rows], dst.at[rows], sems, s, peer)


def slot_sends(p, src, dst, sems, peer):
    dst[0 : p.cap, :] = src[0 : p.cap, :]
    return {s: slot_send(p, src, dst, sems, s, peer(p, s)) for s in range(1, p.experts)}


def receive(copies, sources):
    for s in sources:
        if s in copies:
            copies[s].wait_recv()


def sent(copies):
    for copy in copies.values() if isinstance(copies, dict) else copies:
        copy.wait_send()


def move(r, src, dst):
    copy = pltpu.make_async_copy(src, dst, r.moves.at[r.moved])
    r.moved += 1
    copy.start()
    return copy


def moves(r, pairs):
    return [move(r, src, dst) for src, dst in pairs]


def arrive(copies):
    for copy in copies:
        copy.wait()
    copies.clear()


def norm_parts(state):
    inverse = lax.rsqrt(jnp.mean(state * state, axis=-1, keepdims=True) + EPSILON)
    return inverse, state * inverse


def norm_back(state, gain, grad):
    inverse, unit = norm_parts(state)
    scaled = grad * gain
    back = inverse * scaled - state * (inverse * inverse * inverse) * jnp.mean(
        scaled * state, axis=-1, keepdims=True
    )
    return back, jnp.sum(grad * unit, axis=0, keepdims=True)


def segment_columns(p, segments, seg_cols):
    seg_cols[0:MAXLEN, :] = jnp.full((MAXLEN, 8), -1.0, F32)
    for start in range(0, p.length, QROWS):
        row = segments[:, start : start + QROWS].astype(F32)
        seg_cols[MAXLEN + start : MAXLEN + start + QROWS, :] = jnp.broadcast_to(row, (8, QROWS)).T


def attention_mask(r, start):
    keys = r.seg_cols[pl.ds(start, WINDOW), 0:1]
    queries = r.segments[:, pl.ds(start, QROWS)].astype(F32)
    key_at = lax.broadcasted_iota(jnp.int32, (WINDOW, QROWS), 0) - MAXLEN
    query_at = lax.broadcasted_iota(jnp.int32, (WINDOW, QROWS), 1)
    return jnp.where((key_at <= query_at) & (keys == queries), 0.0, MASKED_SCORE)


def head_rows(p, dst, at, values):
    flat = values.T
    lane = lax.broadcasted_iota(jnp.int32, flat.shape, 1) // HD
    for h in range(p.heads):
        dst[h, at, :] = jnp.where(lane == h, flat, 0.0).astype(BF)


def pick_rows(p, routes, terms):
    picked = []
    for j in range(p.top):
        row = routes[j : j + 1, :]
        total = None
        for e in range(p.mixers):
            term = jnp.where(row == e, terms(e), 0.0)
            total = term if total is None else total + term
        picked.append(total)
    return picked


def spread_rows(p, routes, values, e):
    total = None
    for j in range(p.top):
        term = jnp.where(routes[j : j + 1, :] == e, values[j], 0.0)
        total = term if total is None else total + term
    return total


def pick_table(p, r, step, bb):
    return r.all_picks[bb, 8 * step : 8 * step + p.top, :]


def transposed(dst, src, rows, first, tile):
    for start in range(0, rows, tile):
        dst[start : start + tile, :] = src[:, first + start : first + start + tile].astype(F32).T.astype(BF)


def project(p, r, a, step, bb):
    cols, sub = p.cols, p.seq // QROWS
    states = a.nt[bb]
    table = pick_table(p, r, step, bb)
    logits = mm(r.router_row[...], states)
    chosen = pick_rows(p, table, lambda e: logits[e : e + 1, :])
    peak = functools.reduce(jnp.maximum, chosen)
    chosen = [jnp.exp(row - peak) for row in chosen]
    scale = 1.0 / sum(chosen)
    for j in range(p.top):
        a.gates[bb, j : j + 1, :] = chosen[j] * scale
    values = mm(r.w_t[...], states)
    for k in range(sub):
        lanes = slice(k * QROWS, (k + 1) * QROWS)
        queries = pick_rows(p, table[:, lanes], lambda e: values[e * cols : (e + 1) * cols, lanes])
        for j in range(p.top):
            a.qs[bb * sub + k, :, j * QROWS : (j + 1) * QROWS] = (queries[j] * (HD**-0.5)).astype(BF)
    at = pl.ds(aligned(MAXLEN + bb * p.seq, QROWS), p.seq)
    keys = values[p.mixers * cols : (p.mixers + 1) * cols, :]
    a.kt[:, at] = keys.astype(BF)
    a.vt[:, at] = values[(p.mixers + 1) * cols :, :].astype(BF)
    head_rows(p, r.k_heads, at, keys)


def attend(p, r, a, step, bb):
    cols, sub = p.cols, p.seq // QROWS

    @pl.loop(0, sub)
    def _(k):
        i = bb * sub + k
        start = aligned(i * QROWS, QROWS)
        keys = pl.ds(start, WINDOW)
        bias = attention_mask(r, start)
        bias = jnp.concatenate([bias] * p.top, axis=1)
        queries = a.qs[i]
        for head in range(p.heads):
            scores = mm(r.k_heads[head, keys, :], queries) + bias
            peak = jnp.max(scores, axis=0, keepdims=True)
            scores = jnp.exp(scores - peak)
            total = jnp.sum(scores, axis=0, keepdims=True)
            a.lse[i, head : head + 1, :] = peak + jnp.log(total)
            probs = (scores * (1.0 / total)).astype(BF)
            rows = slice(head * HD, (head + 1) * HD)
            a.att[i, rows, :] = mm(a.vt[rows, keys], probs).astype(BF)
        at = pl.ds(aligned(k * QROWS, QROWS), QROWS)
        table = r.all_picks[bb, 8 * step : 8 * step + p.top, at]
        weights = a.gates[bb, 0 : p.top, at]
        values = [
            a.att[i, :, j * QROWS : (j + 1) * QROWS].astype(F32) * weights[j : j + 1, :] for j in range(p.top)
        ]
        for e in range(p.mixers):
            a.mix[e * cols : (e + 1) * cols, pl.ds(start, QROWS)] = spread_rows(p, table, values, e).astype(BF)


def attention_forward(p, r, a, step, state, before, out_ready, after):
    b, _ = place()
    y, c = b // 2, lax.rem(b, 2)
    a.nt[b] = (norm_parts(state)[1] * r.gain_one[...]).T.astype(BF)
    gather = PackGather(p, a.nt, a.gather_sems)
    gather.begin()
    r.k_heads[:, 0:MAXLEN, :] = jnp.zeros((p.heads, MAXLEN, p.cols), BF)
    a.kt[:, 0:MAXLEN] = jnp.zeros((p.cols, MAXLEN), BF)
    a.vt[:, 0:MAXLEN] = jnp.zeros((p.cols, MAXLEN), BF)
    before(gather)
    project(p, r, a, step, b)
    gather.finish_near()
    project(p, r, a, step, 2 * y + 1 - c)
    attend(p, r, a, step, 2 * y + 1)
    gather.finish_far()
    for s in range(1, p.chips):
        yy = turn(y, s, p.chips)

        @pl.loop(0, 2)
        def _(k):
            project(p, r, a, step, 2 * yy + k)

    def branch(bb):
        return mm(r.all_w[:, p.qkv :], a.mix[:, pl.ds(aligned(bb * p.seq, p.seq), p.seq)])

    shares = PackSum(p, r, a.sum_sems)
    for s in range(1, p.chips):
        yy = turn(y, s, p.chips)
        attend(p, r, a, step, 2 * yy + 1 - c)
        if s == 1:
            out_ready()
        shares.give(s, branch(2 * yy + 1 - c))
        attend(p, r, a, step, 2 * yy + c)
        shares.pass_on(s, branch(2 * yy + c))
    after()
    attend(p, r, a, step, 2 * y)
    shares.give(0, branch(2 * y + 1 - c))
    total = shares.total(branch(b))
    gather.end()
    return total


def attention_grads(p, r, a, step, bb):
    cols, sub = p.cols, p.seq // QROWS
    table = pick_table(p, r, step, bb)
    weights = a.gates[bb, 0 : p.top, :]
    values = mm(r.wo[...], r.gt[bb])
    for k in range(sub):
        lanes = slice(k * QROWS, (k + 1) * QROWS)
        here = table[:, lanes]
        picked = pick_rows(p, here, lambda e: values[e * cols : (e + 1) * cols, lanes])
        grads = []
        for j in range(p.top):
            slot = slice(j * QROWS, (j + 1) * QROWS)
            products = picked[j] * a.att[bb * sub + k, :, slot].astype(F32)
            grads.append(jnp.sum(products, axis=0, keepdims=True))
            for head in range(p.heads):
                mean = jnp.sum(products[head * HD : (head + 1) * HD], axis=0, keepdims=True)
                r.means[bb * sub + k, head : head + 1, slot] = mean * weights[j : j + 1, lanes]
            a.att[bb * sub + k, :, slot] = (picked[j] * weights[j : j + 1, lanes]).astype(BF)
        mean = sum(weights[j : j + 1, lanes] * grads[j] for j in range(p.top))
        back = [weights[j : j + 1, lanes] * (grads[j] - mean) for j in range(p.top)]
        for e in range(p.mixers):
            r.dlog[bb, e : e + 1, lanes] = spread_rows(p, here, back, e)


def attend_back(p, r, a, step, bb):
    cols, sub = p.cols, p.seq // QROWS

    @pl.loop(0, sub)
    def _(k):
        i = bb * sub + k
        start = aligned(i * QROWS, QROWS)
        keys = pl.ds(start, WINDOW)
        bias = attention_mask(r, start)
        bias = jnp.concatenate([bias] * p.top, axis=1)
        queries = a.qs[i]
        grads = a.att[i]
        query_grads = []
        for head in range(p.heads):
            rows = slice(head * HD, (head + 1) * HD)
            scores = mm(r.k_heads[head, keys, :], queries) + bias
            probs = jnp.exp(scores - a.lse[i, head : head + 1, :])
            mean = r.means[i, head : head + 1, :]
            dscores = (probs * (mm(r.v_heads[head, keys, :], grads) - mean)).astype(BF)
            r.dvt[rows, keys] += mm_nt(grads[rows], probs.astype(BF))
            r.dkt[rows, keys] += mm_nt(queries[rows], dscores)
            query_grads.append(mm(a.kt[rows, keys], dscores) * (HD**-0.5))
        at = pl.ds(aligned(k * QROWS, QROWS), QROWS)
        table = r.all_picks[bb, 8 * step : 8 * step + p.top, at]
        merged = jnp.concatenate(query_grads, axis=0)
        values = [merged[:, j * QROWS : (j + 1) * QROWS] for j in range(p.top)]
        for e in range(p.mixers):
            r.dall[e * cols : (e + 1) * cols, pl.ds(start, QROWS)] = spread_rows(p, table, values, e).astype(BF)


def attention_backward(p, r, a, step, state, grad, before, middle, last):
    b, _ = place()
    y, c = b // 2, lax.rem(b, 2)
    r.gt[b] = grad.T.astype(BF)
    gather = PackGather(p, r.gt, a.back_gather_sems)
    gather.begin()
    r.dkt[...] = jnp.zeros_like(r.dkt)
    r.dvt[...] = jnp.zeros_like(r.dvt)
    before()

    @pl.loop(0, (p.length + MAXLEN) // QROWS)
    def _(k):
        at = pl.ds(aligned(k * QROWS, QROWS), QROWS)
        head_rows(p, r.k_heads, at, a.kt[:, at].astype(F32))
        head_rows(p, r.v_heads, at, a.vt[:, at].astype(F32))

    attention_grads(p, r, a, step, b)
    gather.finish_near()
    attention_grads(p, r, a, step, 2 * y + 1 - c)
    attend_back(p, r, a, step, 2 * y)
    gather.finish_far()
    for s in range(1, p.chips):
        yy = turn(y, s, p.chips)

        @pl.loop(0, 2)
        def _(k):
            attention_grads(p, r, a, step, 2 * yy + k)

    middle()
    for s in range(1, p.chips):
        yy = turn(y, s, p.chips)

        @pl.loop(0, 2)
        def _(k):
            attend_back(p, r, a, step, 2 * yy + k)

    cols = p.cols

    def branch(bb):
        lanes = pl.ds(aligned(bb * p.seq, p.seq), p.seq)
        past = pl.ds(aligned(bb * p.seq + MAXLEN, QROWS), p.seq)
        r.dall[p.mixers * cols : (p.mixers + 1) * cols, lanes] = r.dkt[:, past].astype(BF)
        r.dall[(p.mixers + 1) * cols :, lanes] = r.dvt[:, past].astype(BF)
        return mm(r.all_w[:, : p.qkv], r.dall[:, lanes]) + mm(r.router_col[...], r.dlog[bb].astype(BF))

    shares = PackSum(p, r, a.back_sum_sems)
    for s in range(1, p.chips):
        yy = turn(y, s, p.chips)
        shares.give(s, branch(2 * yy + 1 - c))
        shares.pass_on(s, branch(2 * yy + c))
    attend_back(p, r, a, step, 2 * y + 1)
    shares.give(0, branch(2 * y + 1 - c))
    own = branch(b)
    last()
    router = sum(mm_nt(r.dlog[bb].astype(BF), a.nt[bb]) for bb in range(p.blk))
    grad_n = shares.total(own).T
    gather.end()
    back, gain = norm_back(state, r.gain_one[...], grad_n)
    return grad + back, gain, router


def attention_weight_grads(p, r, a, start, stop, add):
    tile = 2 * p.cols
    for first in range(start, stop, tile):
        total = None
        for bb in range(p.blk):
            lanes = slice(bb * p.seq, (bb + 1) * p.seq)
            if first < p.qkv:
                term = mm_nt(a.nt[bb], r.dall[first : first + tile, lanes])
            else:
                term = mm_nt(r.gt[bb], a.mix[first - p.qkv : first - p.qkv + tile, lanes])
            total = term if total is None else total + term
        at = slice(first, first + tile)
        r.grad_w[:, at] = (r.grad_w[:, at].astype(F32) + total if add else total).astype(BF)


def own_lane(p):
    b, d = place()
    mine = d * p.local + b // p.group
    return jnp.where(lax.broadcasted_iota(jnp.int32, (1, LANES), 1) == mine, 1.0, 0.0)


def slot_gates(p, r, rows, pair):
    own = own_lane(p)
    logits = mm(rows, r.router[...])
    return 1.0 / (1.0 + jnp.exp(jnp.sum(logits * (pair - 2.0 * own), axis=-1, keepdims=True)))


def gelu_both(inner):
    half = 0.5 * (1.0 + lax.erf(inner * 0.7071067811865476))
    slope = half + inner * jnp.exp(-0.5 * inner * inner) * 0.3989422804014327
    return inner * half, slope


def slot_groups(p):
    per = max(1, p.experts // 4)
    return [(pl.ds(first * p.cap, per * p.cap), range(first, first + per)) for first in range(0, p.experts, per)]


def expert_output(p, r, rows, at, keep):
    total = None
    for start in range(0, p.ff, p.tile):
        lanes = slice(start, start + p.tile)
        inner = mm(rows, r.all_in[:, lanes])
        if keep:
            act, slope = gelu_both(inner)
            act = act.astype(BF)
            r.act[at, lanes] = act
            r.slope[at, lanes] = slope.astype(BF)
        else:
            act = (inner * (0.5 * (1.0 + lax.erf(inner * 0.7071067811865476)))).astype(BF)
        term = mm(act, r.all_back[lanes, :])
        total = term if total is None else total + term
    return total


def expert_keep(p, r, rows, at):
    for start in range(0, p.ff, p.tile):
        lanes = slice(start, start + p.tile)
        act, slope = gelu_both(mm(rows, r.all_in[:, lanes]))
        r.act[at, lanes] = act.astype(BF)
        r.slope[at, lanes] = slope.astype(BF)


def expert_input_grad(p, r, at, u, rows, out, pair, dst):
    gate = slot_gates(p, r, rows, pair)
    grads = (u * gate).astype(BF)
    r.u_in[at, :] = grads
    coeff = gate * (1.0 - gate) * jnp.sum(u * out, axis=-1, keepdims=True) * (2.0 * own_lane(p) - pair)
    coeff = coeff.astype(BF)
    r.coeff[at, :] = coeff
    dst[at, :] = mm_nt(coeff, r.router[...]).astype(BF)
    total = None
    for start in range(0, p.ff, p.tile):
        lanes = slice(start, start + p.tile)
        inner = (mm_nt(grads, r.all_back[lanes, :]) * r.slope[at, lanes].astype(F32)).astype(BF)
        r.slope[at, lanes] = inner
        term = mm_nt(inner, r.all_in[:, lanes])
        total = term if total is None else total + term
    dst[at, :] = (total + dst[at, :].astype(F32)).astype(BF)


def expert_weight_grads(p, r, arrived, add):
    r.arrived_t[...] = arrived[...].astype(F32).T.astype(BF)
    for start in range(0, p.ff, p.tile // 2):
        lanes = slice(start, start + p.tile // 2)
        term = mm(r.act[:, lanes].astype(F32).T.astype(BF), r.u_in[...])
        r.grad_back[lanes, :] = (r.grad_back[lanes, :].astype(F32) + term if add else term).astype(BF)
        term = mm(r.arrived_t[...], r.slope[:, lanes])
        r.grad_in[:, lanes] = (r.grad_in[:, lanes].astype(F32) + term if add else term).astype(BF)
    return mm(r.coeff[...].astype(F32).T.astype(BF)[0 : p.experts], arrived[...])


def slot_tables(p, r):
    b, d = place()
    e = b // p.group
    place_in = lax.broadcasted_iota(jnp.int32, (p.experts, 1), 0)
    ids = lax.rem(d + lax.rem(place_in, p.dp), p.dp) * p.local + lax.rem(e + place_in // p.dp, p.local)
    earlier = (
        lax.broadcasted_iota(jnp.int32, (p.seq, p.seq), 0) < lax.broadcasted_iota(jnp.int32, (p.seq, p.seq), 1)
    ).astype(BF)
    slot_ids = lax.broadcasted_iota(jnp.int32, (p.cap, p.seq), 0).astype(F32)
    lane_ids = lax.broadcasted_iota(jnp.int32, (LANES, 1), 0)
    copies = []
    for step in range(2):
        one = r.routes[8 * step + p.top : 8 * step + p.top + 1, :]
        two = r.routes[8 * step + p.top + 1 : 8 * step + p.top + 2, :]
        member = jnp.where((one == ids) | (two == ids), 1.0, 0.0)
        rank = jnp.where(member > 0.5, mm(member.astype(BF), earlier), -1.0)
        for s in range(p.experts):
            r.disp[step, pl.ds(s * p.cap, p.cap), :] = jnp.where(rank[s : s + 1, :] == slot_ids, 1.0, 0.0).astype(BF)
        table = r.disp[step]
        r.comb[step] = table.astype(F32).T.astype(BF)
        pair = jnp.where((one == lane_ids) | (two == lane_ids), 1.0, 0.0).astype(BF)
        r.pair_out[step] = mm_nt(table, pair).astype(BF)
        r.pair[step, 0 : p.cap, :] = r.pair_out[step, 0 : p.cap, :]
        for s in range(1, p.experts):
            rows = pl.ds(s * p.cap, p.cap)
            slot = step * p.experts + s
            copies.append(
                send(r.pair_out.at[step, rows], r.pair.at[step, rows], (r.pair_s, r.pair_r), slot, slot_peer(p, s))
            )
    return copies


def forward_kernel(p, r):
    b, d = place()
    z, x = d // p.lo, lax.rem(d, p.lo)
    e, g = b // p.group, lax.rem(b, p.group)
    own_rows = r.wall.shape[0]
    in_rows, back_rows = r.weight_in.shape[1], r.weight_back.shape[1]

    def w_at(index, part):
        lanes = slice(0, p.qkv) if part == 0 else slice(p.qkv, p.all_cols)
        return r.all_w.at[pl.ds(aligned(index * own_rows, own_rows), own_rows), lanes]

    def in_at(index):
        return r.all_in.at[pl.ds(aligned(index * in_rows, in_rows), in_rows)]

    def back_at(index):
        return r.all_back.at[pl.ds(aligned(index * back_rows, back_rows), back_rows)]

    greet(pack_peers(p) + slot_peers(p) + dp_peers(p) + expert_peers(p))
    r.all_w[pl.ds(aligned(d * own_rows, own_rows), own_rows), :] = r.wall[...]
    along, across = {}, {}

    def w_begin(part):
        own = w_at(d, part)
        for s in range(1, p.hi):
            k = part * (p.hi - 1) + s - 1
            along[part, s] = send(own, own, (r.hi_s, r.hi_r), k, (b, turn(z, s, p.hi) * p.lo + x))

    def w_cross(part, s):
        rows = w_at(turn(z, -s, p.hi) * p.lo + x, part)
        for t in range(1, p.lo):
            k = (part * p.hi + s) * (p.lo - 1) + t - 1
            across[part, s, t] = send(rows, rows, (r.lo_s, r.lo_r), k, (b, z * p.lo + turn(x, t, p.lo)))

    def w_finish(part):
        for s in range(p.hi):
            for t in range(1, p.lo):
                across[part, s, t].wait_recv()

    local, over, beside = [], {}, []

    def experts_begin():
        for s in range(1, p.local):
            to = turn(e, s, p.local)
            peer = (to * p.group + g, d)
            over[s, 0] = send(r.weight_in.at[to], in_at(b), (r.wide_s, r.wide_r), 2 * s - 2, peer)
            over[s, 1] = send(r.weight_back.at[to], back_at(b), (r.wide_s, r.wide_r), 2 * s - 1, peer)
        for t in range(1, p.group):
            peer = (e * p.group + turn(g, t, p.group), d)
            beside.append(send(r.weight_in.at[e], in_at(b), (r.near_s, r.near_r), 2 * t - 2, peer))
            beside.append(send(r.weight_back.at[e], back_at(b), (r.near_s, r.near_r), 2 * t - 1, peer))

    def experts_pass():
        for s in range(1, p.local):
            source = turn(e, -s, p.local) * p.group + g
            for which, rows in ((0, in_at(source)), (1, back_at(source))):
                over[s, which].wait_recv()
                for t in range(1, p.group):
                    k = (s * (p.group - 1) + t - 1) * 2 + which
                    peer = (e * p.group + turn(g, t, p.group), d)
                    beside.append(send(rows, rows, (r.near_s, r.near_r), k, peer))

    tables = []
    saves = []

    w_begin(0)
    w_cross(0, 0)
    r.all_picks[b] = r.routes[...]
    picks = PackGather(p, r.all_picks, r.picks_sems)
    picks.begin()
    state = r.x[...].astype(F32)

    def before(gather):
        local.extend(moves(r, [(r.weight_in.at[e], in_at(b)), (r.weight_back.at[e], back_at(b))]))
        segment_columns(p, r.segments, r.seg_cols)
        tables.extend(slot_tables(p, r))
        gather.finish_far()
        picks.finish_far()
        for s in range(1, p.hi):
            along[0, s].wait_recv()
            w_cross(0, s)
        w_begin(1)
        w_cross(1, 0)
        experts_begin()
        w_finish(0)
        transposed(r.w_t, r.all_w, p.qkv, 0, 2 * p.cols)

    def out_ready():
        for s in range(1, p.hi):
            along[1, s].wait_recv()
            w_cross(1, s)
        w_finish(1)

    def after():
        saves.extend(moves(r, [(r.all_w, r.all_w_out), (r.disp, r.disp_out), (r.comb, r.comb_out)]))
        experts_pass()

    total = attention_forward(p, r, r.a, 0, state, before, out_ready, after)
    middle = state + total.T
    r.middle[...] = middle
    m = (norm_parts(middle)[1] * r.gain_two[...]).astype(BF)
    r.outgoing[...] = mm(r.disp[0], m).astype(BF)
    there = slot_sends(p, r.outgoing, r.arrived, (r.go_s, r.go_r), slot_peer)
    saves.extend(moves(r, [(getattr(r.a, k), getattr(r, k + "_out")) for k in SAVED]))
    for copy in tables:
        copy.wait_recv()
    for copy in beside:
        copy.wait_recv()
    arrive(local)
    saves.extend(moves(r, [(r.all_in, r.all_in_out), (r.all_back, r.all_back_out), (r.pair, r.pair_end)]))
    back = {}
    for at, sources in slot_groups(p):
        receive(there, sources)
        rows = r.arrived[at, :]
        out = expert_output(p, r, rows, at, False)
        r.produced[at, :] = out.astype(BF)
        r.ret_out[at, :] = (out * slot_gates(p, r, rows, r.pair[0, at, :].astype(F32))).astype(BF)
        for s in sources:
            if s:
                back[s] = slot_send(p, r.ret_out, r.ret_in, (r.ret_s, r.ret_r), s, slot_source(p, s))
    r.ret_in[0 : p.cap, :] = r.ret_out[0 : p.cap, :]
    receive(back, range(p.experts))
    r.first[...] = r.middle[...] + mm(r.comb[0], r.ret_in[...])
    sent(there)
    sent(back)
    sent(tables)
    sent(beside)
    sent(along)
    sent(across)
    sent(over)
    picks.end()
    arrive(saves)


def turn_kernel(p, r):
    greet(pack_peers(p) + slot_peers(p))
    early = moves(r, [(r.all_w_in, r.all_w), (r.disp_in, r.disp), (r.comb_in, r.comb), (r.pair_in, r.pair)])
    weights = moves(r, [(r.all_in_in, r.all_in), (r.all_back_in, r.all_back)])
    first = r.first[...]
    stop = 1.0 / (1.0 + jnp.exp(-jnp.sum(first * r.halt[...], axis=-1, keepdims=True)))
    cot = r.cot[...].astype(F32)
    there_u, saves = {}, []

    def before(gather):
        arrive(early)
        r.u_out[...] = mm(r.disp[...], ((1.0 - stop) * cot).astype(BF)).astype(BF)
        there_u.update(slot_sends(p, r.u_out, r.u_in, (r.u_s, r.u_r), slot_peer))
        segment_columns(p, r.segments, r.seg_cols)
        transposed(r.w_t, r.all_w, p.qkv, 0, 2 * p.cols)

    total = attention_forward(p, r, r.a, 1, first, before, lambda: None, lambda: None)
    middle = first + total.T
    r.middle[...] = middle
    m = (norm_parts(middle)[1] * r.gain_two[...]).astype(BF)
    r.outgoing[...] = mm(r.disp[...], m).astype(BF)
    there = slot_sends(p, r.outgoing, r.arrived, (r.go_s, r.go_r), slot_peer)
    transposed(r.wo, r.all_w, p.mixers * p.cols, p.qkv, 2 * p.cols)
    arrive(weights)
    sent(there_u)
    ret_out = r.u_out
    back, back_out = {}, {}
    for at, sources in slot_groups(p):
        receive(there_u, sources)
        receive(there, sources)
        rows = r.arrived[at, :]
        pair = r.pair[at, :].astype(F32)
        out = expert_output(p, r, rows, at, True)
        ret_out[at, :] = (out * slot_gates(p, r, rows, pair)).astype(BF)
        expert_input_grad(p, r, at, r.u_in[at, :].astype(F32), rows, out, pair, r.gret_out)
        for s in sources:
            if s:
                back[s] = slot_send(p, r.gret_out, r.gret_in, (r.gret_s, r.gret_r), s, slot_source(p, s))
    r.gret_in[0 : p.cap, :] = r.gret_out[0 : p.cap, :]
    r.ret_in[0 : p.cap, :] = ret_out[0 : p.cap, :]
    r.grad_router[...] = expert_weight_grads(p, r, r.arrived, False)
    saves.extend(moves(r, [(r.grad_in, r.grad_in_out), (r.grad_back, r.grad_back_out)]))
    receive(back, range(p.experts))
    step_back, gain_two = norm_back(r.middle[...], r.gain_two[...], mm(r.comb[...], r.gret_in[...]))
    r.grad_gain_two[...] = gain_two
    grad_middle = (1.0 - stop) * cot + step_back

    def before_back():
        for s in range(1, p.experts):
            back_out[s] = slot_send(p, ret_out, r.ret_in, (r.ret_s, r.ret_r), s, slot_source(p, s))

    def last():
        attention_weight_grads(p, r, r.a, 0, p.all_cols, False)

    grad, gain_one, router = attention_backward(
        p, r, r.a, 1, first, grad_middle, before_back, lambda: None, last
    )
    saves.extend(moves(r, [(r.grad_w, r.grad_w_out)]))
    r.grad_gain_one[...] = gain_one
    r.grad_mixer[...] = router
    receive(back_out, range(p.experts))
    second = r.middle[...] + mm(r.comb[...], r.ret_in[...])
    r.result[...] = (stop * first + (1.0 - stop) * second).astype(BF)
    grad_stop = jnp.sum(cot * (first - second), axis=-1, keepdims=True)
    coeff = grad_stop * stop * (1.0 - stop)
    r.grad_halt[...] = jnp.sum(coeff * first, axis=0, keepdims=True)
    r.grad_first[...] = stop * cot + coeff * r.halt[...] + grad
    for copies in (there, back, back_out):
        sent(copies)
    arrive(saves)


def backward_kernel(p, r):
    b, d = place()
    z, x = d // p.lo, lax.rem(d, p.lo)
    y, c = b // 2, lax.rem(b, 2)
    e, g = b // p.group, lax.rem(b, p.group)
    rows = r.out_w.shape[0]
    in_rows, back_rows = r.out_in.shape[1], r.out_back.shape[1]
    greet(pack_peers(p) + slot_peers(p) + dp_peers(p) + expert_peers(p))
    early = moves(
        r,
        [
            (r.disp_in, r.disp),
            (r.pair_in, r.pair),
            (r.arrived_in, r.arrived),
            (r.all_in_in, r.all_in),
            (r.all_back_in, r.all_back),
            (r.produced_in, r.produced),
        ],
    )
    later = moves(
        r, [(r.grad_in_in, r.grad_in), (r.grad_back_in, r.grad_back), (r.comb_in, r.comb), (r.all_w_in, r.all_w)]
    )
    later += moves(r, [(r.grad_w_in, r.grad_w)])
    later += moves(r, [(getattr(r, k + "_in"), getattr(r.a, k)) for k in SAVED])
    grad_first = r.grad_first[...]
    arrive(early)
    r.u_out[...] = mm(r.disp[...], grad_first.astype(BF)).astype(BF)
    there = slot_sends(p, r.u_out, r.u_in, (r.u_s, r.u_r), slot_peer)
    for at, _ in slot_groups(p):
        expert_keep(p, r, r.arrived[at, :], at)
    segment_columns(p, r.segments, r.seg_cols)
    arrive(later)
    transposed(r.wo, r.all_w, p.mixers * p.cols, p.qkv, 2 * p.cols)
    back = {}
    for at, sources in slot_groups(p):
        receive(there, sources)
        pair = r.pair[at, :].astype(F32)
        out = r.produced[at, :].astype(F32)
        expert_input_grad(p, r, at, r.u_in[at, :].astype(F32), r.arrived[at, :], out, pair, r.produced)
        for s in sources:
            if s:
                back[s] = slot_send(p, r.produced, r.gret_in, (r.gret_s, r.gret_r), s, slot_source(p, s))
    r.gret_in[0 : p.cap, :] = r.produced[0 : p.cap, :]
    r.grad_router[...] = expert_weight_grads(p, r, r.arrived, True)

    def row_block(ref, index, size, lanes=slice(None)):
        return ref.at[pl.ds(aligned(index * size, size), size), lanes]

    near = {}
    for k in range(p.local):
        to = turn(e, k + 1, p.local)
        for t in range(1, p.group):
            member = turn(g, t, p.group)
            slot = k * (p.group - 1) + t - 1
            peer = (e * p.group + member, d)
            owner = to * p.group + member
            near[k, t, 0] = send(
                row_block(r.grad_in, owner, in_rows), r.in_near.at[slot], (r.near_s, r.near_r), 2 * slot, peer
            )
            near[k, t, 1] = send(
                row_block(r.grad_back, owner, back_rows), r.back_near.at[slot], (r.near_s, r.near_r), 2 * slot + 1, peer
            )
    receive(back, range(p.experts))
    step_back, gain_two = norm_back(r.middle[...], r.gain_two[...], mm(r.comb[...], r.gret_in[...]))
    grad_middle = grad_first + step_back
    wide, lo_copies, hi_copies = {}, {}, {}

    def experts_wide():
        for k in range(p.local):
            to = turn(e, k + 1, p.local)
            total_in = row_block(r.grad_in, to * p.group + g, in_rows)[...].astype(F32)
            total_back = row_block(r.grad_back, to * p.group + g, back_rows)[...].astype(F32)
            for t in range(1, p.group):
                slot = k * (p.group - 1) + t - 1
                near[k, t, 0].wait_recv()
                near[k, t, 1].wait_recv()
                total_in = total_in + r.in_near[slot].astype(F32)
                total_back = total_back + r.back_near[slot].astype(F32)
            if k < p.local - 1:
                r.in_far_out[k] = total_in.astype(BF)
                r.back_far_out[k] = total_back.astype(BF)
                peer = (to * p.group + g, d)
                wide[k, 0] = send(r.in_far_out.at[k], r.in_far.at[k], (r.wide_s, r.wide_r), 2 * k, peer)
                wide[k, 1] = send(r.back_far_out.at[k], r.back_far.at[k], (r.wide_s, r.wide_r), 2 * k + 1, peer)
            else:
                r.out_in[e] = total_in.astype(BF)
                r.out_back[e] = total_back.astype(BF)

    parts = (slice(0, p.qkv), slice(p.qkv, p.all_cols))

    def sum_begin(part):
        for k in range(p.hi):
            to = turn(z, k + 1, p.hi)
            for t in range(1, p.lo):
                slot = k * (p.lo - 1) + t - 1
                xx = turn(x, t, p.lo)
                lo_copies[part, k, t] = send(
                    row_block(r.grad_w, to * p.lo + xx, rows, parts[part]),
                    r.w_lo.at[slot, :, parts[part]],
                    (r.lo_s, r.lo_r),
                    part * p.hi * (p.lo - 1) + slot,
                    (b, z * p.lo + xx),
                )

    def sum_pass(part):
        lanes = parts[part]
        for k in range(p.hi):
            to = turn(z, k + 1, p.hi)
            total = row_block(r.grad_w, to * p.lo + x, rows, lanes)[...].astype(F32)
            for t in range(1, p.lo):
                lo_copies[part, k, t].wait_recv()
                total = total + r.w_lo[k * (p.lo - 1) + t - 1, :, lanes].astype(F32)
            if k < p.hi - 1:
                r.w_hi_out[k, :, lanes] = total.astype(BF)
                hi_copies[part, k] = send(
                    r.w_hi_out.at[k, :, lanes],
                    r.w_hi.at[k, :, lanes],
                    (r.hi_s, r.hi_r),
                    part * (p.hi - 1) + k,
                    (b, to * p.lo + x),
                )
            else:
                r.out_w[:, lanes] = total

    def sum_finish(part):
        lanes = parts[part]
        total = r.out_w[:, lanes]
        for k in range(p.hi - 1):
            hi_copies[part, k].wait_recv()
            total = total + r.w_hi[k, :, lanes].astype(F32)
        r.out_w[:, lanes] = total

    def middle():
        experts_wide()
        attention_weight_grads(p, r, r.a, p.qkv, p.all_cols, True)
        sum_begin(1)

    def last():
        sum_pass(1)
        attention_weight_grads(p, r, r.a, 0, p.qkv, True)
        sum_begin(0)

    grad, gain_one, router = attention_backward(
        p, r, r.a, 0, r.x[...].astype(F32), grad_middle, lambda: None, middle, last
    )
    sum_pass(0)
    r.input_grad[...] = grad.astype(BF)
    small = r.out_small
    small[...] = jnp.zeros_like(small)
    small[0:1, :] = r.gain_one_before[...] + gain_one
    small[1:2, :] = r.gain_two_before[...] + gain_two
    small[2:3, :] = r.halt_before[...]
    small[8 : 8 + p.mixers, :] = r.mixer_before[...] + router
    small[8 + p.mixers :, :] = r.router_before[...] + r.grad_router[...]
    current = small[...]
    tiny = []
    sem = base = 0
    axes = (
        (2, c, lambda t: (2 * y + turn(c, t, 2), d)),
        (p.chips, y, lambda t: (2 * turn(y, t, p.chips) + c, d)),
        (p.lo, x, lambda t: (b, z * p.lo + turn(x, t, p.lo))),
        (p.hi, z, lambda t: (b, turn(z, t, p.hi) * p.lo + x)),
    )
    for size, index, peer in axes:
        r.all_small[base + index] = current
        at = r.all_small.at[base + index]
        copies = []
        for t in range(1, size):
            copies.append(send(at, at, (r.tiny_s, r.tiny_r), sem, peer(t)))
            sem += 1
        for copy in copies:
            copy.wait_recv()
        current = r.all_small[base]
        for k in range(1, size):
            current = current + r.all_small[base + k]
        base += size
        tiny += copies
    r.out_small[...] = current
    for k in range(p.local - 1):
        source = turn(e, -(k + 1), p.local)
        wide[k, 0].wait_recv()
        wide[k, 1].wait_recv()
        r.out_in[source] = r.in_far[k]
        r.out_back[source] = r.back_far[k]
    sum_finish(1)
    sum_finish(0)
    for copies in (there, back, near, wide, lo_copies, hi_copies, tiny):
        sent(copies)


def output_kernel(p, r):
    cols = p.cols
    r.result_out[...] = r.result[...]
    r.input_grad_out[...] = r.input_grad[...]
    r.in_out[...] = r.out_in[...].astype(F32)
    r.back_out[...] = r.out_back[...].astype(F32)
    for e in range(p.mixers):
        r.query_out[e] = r.out_w[:, e * cols : (e + 1) * cols]
        start = p.qkv + e * cols
        r.out_out[e] = r.out_w[:, start : start + cols].T
    r.key_out[...] = r.out_w[:, p.mixers * cols : (p.mixers + 1) * cols]
    r.value_out[...] = r.out_w[:, (p.mixers + 1) * cols : p.qkv]
    r.gains_out[...] = r.small[0:8, :]
    r.routers_out[...] = r.small[8:, :].T


SAVED = ("nt", "qs", "kt", "vt", "lse", "att", "mix", "gates")


def dma(name, size):
    sem = pltpu.SemaphoreType.DMA((max(1, size),))
    return {name + "_s": sem, name + "_r": sem}


def pack_sems(p, name):
    sizes = (p.chips - 1, p.chips - 1, p.chips, p.chips)
    return {f"{name}_{k}": pltpu.SemaphoreType.DMA((max(1, size),)) for k, size in enumerate(sizes)}


def sum_scratch(p):
    far = max(1, p.chips - 1)
    return {
        "part": pltpu.VMEM((p.chips, p.width, p.seq), BF),
        "near_in": pltpu.VMEM((p.chips, p.width, p.seq), BF),
        "far_out": pltpu.VMEM((far, p.width, p.seq), BF),
        "far_in": pltpu.VMEM((far, p.width, p.seq), BF),
    }


def saved_shapes(p):
    return {
        "nt": ((p.blk, p.width, p.seq), BF),
        "qs": ((p.blocks, p.cols, p.top * QROWS), BF),
        "kt": ((p.cols, p.length + MAXLEN), BF),
        "vt": ((p.cols, p.length + MAXLEN), BF),
        "lse": ((p.blocks, 8, p.top * QROWS), F32),
        "att": ((p.blocks, p.cols, p.top * QROWS), BF),
        "mix": ((p.mixers * p.cols, p.length), BF),
        "gates": ((p.blk, 8, p.seq), F32),
    }


def launch(body, name, number, ins, outs, scratch):
    def spec(vmem):
        return pl.BlockSpec(memory_space=pltpu.VMEM if vmem else pl.ANY)

    names = list(ins) + list(outs) + list(scratch)

    def kernel(*refs):
        r = SimpleNamespace(**dict(zip(names, refs, strict=True)))
        r.moved = 0
        r.a = SimpleNamespace(**{k[2:]: v for k, v in vars(r).items() if k.startswith("a_")})
        for key in ("gather", "sum", "back_gather", "back_sum", "picks"):
            sems = [getattr(r, f"{key}_{k}") for k in range(4) if hasattr(r, f"{key}_{k}")]
            setattr(r.a, key + "_sems", sems)
            setattr(r, key + "_sems", sems)
        body(r)

    results = pl.pallas_call(
        kernel,
        out_shape=tuple(jax.ShapeDtypeStruct(shape, dtype) for shape, dtype, _ in outs.values()),
        in_specs=[spec(vmem) for _, vmem in ins.values()],
        out_specs=tuple(spec(vmem) for _, _, vmem in outs.values()),
        scratch_shapes=list(scratch.values()),
        compiler_params=pltpu.CompilerParams(
            collective_id=number, has_side_effects=number is not None, vmem_limit_bytes=VMEM_BYTES
        ),
        name=name,
    )(*[array for array, _ in ins.values()])
    return SimpleNamespace(**dict(zip(outs, results, strict=True)))


def on_device(
    inputs,
    segments,
    attention_routes,
    expert_routes,
    gain_mixer,
    gain_expert,
    weight_query,
    weight_key,
    weight_value,
    weight_out,
    router_mixer,
    router_expert,
    weight_in,
    weight_back,
    halt_weight,
    cotangent,
):
    blk, dp = lax.axis_size("blk"), lax.axis_size("dp")
    seq, width = inputs.shape[1:]
    experts, local = router_expert.shape[1], weight_in.shape[0]
    slots_of = max(2, 3 * seq // experts)
    hi = 4
    p = Plan(
        blk=blk,
        dp=dp,
        lo=dp // hi,
        hi=hi,
        seq=seq,
        width=width,
        heads=HEADS // blk,
        mixers=weight_query.shape[0],
        top=attention_routes.shape[-1],
        experts=experts,
        local=local,
        group=blk // local,
        cap=-(-slots_of // 16) * 16,
        ff=weight_in.shape[2],
    )
    cols, length, top = p.cols, p.length, p.top
    share, in_rows, back_rows = weight_key.shape[0], weight_in.shape[1], weight_back.shape[1]

    wall = jnp.concatenate(
        [
            jnp.transpose(weight_query, (1, 0, 2)).reshape(share, p.mixers * cols),
            weight_key,
            weight_value,
            jnp.transpose(weight_out, (2, 0, 1)).reshape(share, p.mixers * cols),
        ],
        axis=1,
    )
    routes = jnp.concatenate(
        [attention_routes[:, 0], expert_routes[:, 0], jnp.zeros((2, seq, 8 - top - expert_routes.shape[-1]), jnp.int32)],
        axis=-1,
    )
    routes = jnp.transpose(routes, (0, 2, 1)).reshape(16, seq)
    gain_one = gain_mixer.astype(F32).reshape(1, width)
    gain_two = gain_expert.astype(F32).reshape(1, width)
    halt = halt_weight.astype(F32).reshape(1, width)
    router_row = router_mixer.T
    router = jnp.pad(router_expert, ((0, 0), (0, LANES - experts)))

    slots_bf = pltpu.VMEM((p.slots, width), BF)
    saved = saved_shapes(p)
    attention_scratch = {
        "seg_cols": pltpu.VMEM((length + MAXLEN, 8), F32),
        "k_heads": pltpu.VMEM((p.heads, length + MAXLEN, cols), BF),
        "all_w": pltpu.VMEM((width, p.all_cols), BF),
        **{"a_" + k: pltpu.VMEM(*v) for k, v in saved.items()},
    }
    forward_scratch = {
        "w_t": pltpu.VMEM((p.qkv, width), BF),
        **pack_sems(p, "gather"),
        **pack_sems(p, "sum"),
        **sum_scratch(p),
    }
    backward_scratch = {
        "gt": pltpu.VMEM((blk, width, seq), BF),
        "v_heads": pltpu.VMEM((p.heads, length + MAXLEN, cols), BF),
        "means": pltpu.VMEM((p.blocks, 8, top * QROWS), F32),
        "dlog": pltpu.VMEM((blk, p.mixers, seq), F32),
        "dkt": pltpu.VMEM((cols, length + MAXLEN), F32),
        "dvt": pltpu.VMEM((cols, length + MAXLEN), F32),
        "dall": pltpu.VMEM((p.qkv, length), BF),
        "grad_w": pltpu.VMEM((width, p.all_cols), BF),
        **pack_sems(p, "back_gather"),
        **pack_sems(p, "back_sum"),
        **sum_scratch(p),
    }
    expert_scratch = {
        "all_in": pltpu.VMEM((width, p.ff), BF),
        "all_back": pltpu.VMEM((p.ff, width), BF),
    }
    expert_back_scratch = {
        "act": pltpu.VMEM((p.slots, p.ff), BF),
        "slope": pltpu.VMEM((p.slots, p.ff), BF),
        "coeff": pltpu.VMEM((p.slots, LANES), BF),
        "arrived_t": pltpu.VMEM((width, p.slots), BF),
        "u_out": slots_bf,
        "u_in": slots_bf,
        "gret_in": slots_bf,
        "grad_in": pltpu.VMEM((width, p.ff), BF),
        "grad_back": pltpu.VMEM((p.ff, width), BF),
        **dma("u", p.experts),
        **dma("gret", p.experts),
    }

    one = launch(
        functools.partial(forward_kernel, p),
        "forward",
        0,
        {
            "x": (inputs[0], True),
            "segments": (segments, True),
            "routes": (routes, True),
            "gain_one": (gain_one, True),
            "gain_two": (gain_two, True),
            "router_row": (router_row, True),
            "router": (router, True),
            "wall": (wall, True),
            "weight_in": (weight_in, False),
            "weight_back": (weight_back, False),
        },
        {
            "first": ((seq, width), F32, True),
            "middle": ((seq, width), F32, True),
            "arrived": ((p.slots, width), BF, True),
            "produced": ((p.slots, width), BF, True),
            "all_picks": ((blk, 16, seq), jnp.int32, True),
            "disp_out": ((2, p.slots, seq), BF, False),
            "comb_out": ((2, seq, p.slots), BF, False),
            "pair_end": ((2, p.slots, LANES), BF, False),
            "all_w_out": ((width, p.all_cols), BF, False),
            "all_in_out": ((width, p.ff), BF, False),
            "all_back_out": ((p.ff, width), BF, False),
            **{k + "_out": (*v, False) for k, v in saved.items()},
        },
        {
            **attention_scratch,
            **forward_scratch,
            **expert_scratch,
            "disp": pltpu.VMEM((2, p.slots, seq), BF),
            "comb": pltpu.VMEM((2, seq, p.slots), BF),
            "pair": pltpu.VMEM((2, p.slots, LANES), BF),
            "pair_out": pltpu.VMEM((2, p.slots, LANES), BF),
            "outgoing": slots_bf,
            "ret_out": slots_bf,
            "ret_in": slots_bf,
            **pack_sems(p, "picks"),
            **dma("hi", 2 * (p.hi - 1)),
            **dma("lo", 2 * p.hi * (p.lo - 1)),
            **dma("wide", 2 * (p.local - 1)),
            **dma("near", 2 * p.local * (p.group - 1)),
            **dma("pair", 2 * p.experts),
            **dma("go", p.experts),
            **dma("ret", p.experts),
            "moves": pltpu.SemaphoreType.DMA((16,)),
        },
    )
    two = launch(
        functools.partial(turn_kernel, p),
        "turn",
        1,
        {
            "first": (one.first, True),
            "cot": (cotangent[0], True),
            "halt": (halt, True),
            "segments": (segments, True),
            "all_picks": (one.all_picks, True),
            "gain_one": (gain_one, True),
            "gain_two": (gain_two, True),
            "router_row": (router_row, True),
            "router_col": (router_mixer, True),
            "router": (router, True),
            "disp_in": (one.disp_out[1], False),
            "comb_in": (one.comb_out[1], False),
            "pair_in": (one.pair_end[1], False),
            "all_w_in": (one.all_w_out, False),
            "all_in_in": (one.all_in_out, False),
            "all_back_in": (one.all_back_out, False),
        },
        {
            "result": ((seq, width), BF, True),
            "grad_first": ((seq, width), F32, True),
            "grad_halt": ((1, width), F32, True),
            "grad_gain_one": ((1, width), F32, True),
            "grad_gain_two": ((1, width), F32, True),
            "grad_mixer": ((p.mixers, width), F32, True),
            "grad_router": ((experts, width), F32, True),
            "grad_in_out": ((width, p.ff), BF, False),
            "grad_back_out": ((p.ff, width), BF, False),
            "grad_w_out": ((width, p.all_cols), BF, False),
        },
        {
            **attention_scratch,
            **forward_scratch,
            **backward_scratch,
            **expert_scratch,
            **expert_back_scratch,
            "wo": pltpu.VMEM((p.mixers * cols, width), BF),
            "disp": pltpu.VMEM((p.slots, seq), BF),
            "comb": pltpu.VMEM((seq, p.slots), BF),
            "pair": pltpu.VMEM((p.slots, LANES), BF),
            "middle": pltpu.VMEM((seq, width), F32),
            "outgoing": slots_bf,
            "arrived": slots_bf,
            "gret_out": slots_bf,
            "ret_in": slots_bf,
            **dma("go", p.experts),
            **dma("ret", p.experts),
            "moves": pltpu.SemaphoreType.DMA((16,)),
        },
    )
    near, far = p.local * (p.group - 1), max(1, p.local - 1)
    small_rows = 8 + p.mixers + experts
    three = launch(
        functools.partial(backward_kernel, p),
        "backward",
        2,
        {
            "x": (inputs[0], True),
            "grad_first": (two.grad_first, True),
            "middle": (one.middle, True),
            "segments": (segments, True),
            "all_picks": (one.all_picks, True),
            "gain_one": (gain_one, True),
            "gain_two": (gain_two, True),
            "router_col": (router_mixer, True),
            "router": (router, True),
            "halt_before": (two.grad_halt, True),
            "gain_one_before": (two.grad_gain_one, True),
            "gain_two_before": (two.grad_gain_two, True),
            "mixer_before": (two.grad_mixer, True),
            "router_before": (two.grad_router, True),
            "disp_in": (one.disp_out[0], False),
            "comb_in": (one.comb_out[0], False),
            "pair_in": (one.pair_end[0], False),
            "arrived_in": (one.arrived, False),
            "produced_in": (one.produced, False),
            "all_w_in": (one.all_w_out, False),
            "all_in_in": (one.all_in_out, False),
            "all_back_in": (one.all_back_out, False),
            "grad_in_in": (two.grad_in_out, False),
            "grad_back_in": (two.grad_back_out, False),
            "grad_w_in": (two.grad_w_out, False),
            **{k + "_in": (getattr(one, k + "_out"), False) for k in SAVED},
        },
        {
            "input_grad": ((seq, width), BF, True),
            "out_w": ((share, p.all_cols), F32, True),
            "out_in": ((local, in_rows, p.ff), BF, True),
            "out_back": ((local, back_rows, width), BF, True),
            "out_small": ((small_rows, width), F32, True),
        },
        {
            **attention_scratch,
            **backward_scratch,
            **expert_scratch,
            **expert_back_scratch,
            "wo": pltpu.VMEM((p.mixers * cols, width), BF),
            "disp": pltpu.VMEM((p.slots, seq), BF),
            "comb": pltpu.VMEM((seq, p.slots), BF),
            "pair": pltpu.VMEM((p.slots, LANES), BF),
            "arrived": slots_bf,
            "produced": slots_bf,
            "in_near": pltpu.VMEM((near, in_rows, p.ff), BF),
            "back_near": pltpu.VMEM((near, back_rows, width), BF),
            "in_far_out": pltpu.VMEM((far, in_rows, p.ff), BF),
            "in_far": pltpu.VMEM((far, in_rows, p.ff), BF),
            "back_far_out": pltpu.VMEM((far, back_rows, width), BF),
            "back_far": pltpu.VMEM((far, back_rows, width), BF),
            "w_lo": pltpu.VMEM((hi * (p.lo - 1), share, p.all_cols), BF),
            "w_hi_out": pltpu.VMEM((hi - 1, share, p.all_cols), BF),
            "w_hi": pltpu.VMEM((hi - 1, share, p.all_cols), BF),
            "grad_router": pltpu.VMEM((experts, width), F32),
            "all_small": pltpu.VMEM((2 + p.chips + p.lo + hi, small_rows, width), F32),
            **dma("near", 2 * near),
            **dma("wide", 2 * (local - 1)),
            **dma("lo", 2 * hi * (p.lo - 1)),
            **dma("hi", 2 * (hi - 1)),
            **dma("tiny", 2 + p.chips + p.lo + hi),
            "moves": pltpu.SemaphoreType.DMA((24,)),
        },
    )
    four = launch(
        functools.partial(output_kernel, p),
        "outputs",
        None,
        {
            "result": (two.result, True),
            "input_grad": (three.input_grad, True),
            "out_w": (three.out_w, True),
            "out_in": (three.out_in, True),
            "out_back": (three.out_back, True),
            "small": (three.out_small, True),
        },
        {
            "result_out": ((seq, width), BF, True),
            "input_grad_out": ((seq, width), BF, True),
            "query_out": (weight_query.shape, F32, True),
            "key_out": (weight_key.shape, F32, True),
            "value_out": (weight_value.shape, F32, True),
            "out_out": (weight_out.shape, F32, True),
            "in_out": (weight_in.shape, F32, True),
            "back_out": (weight_back.shape, F32, True),
            "gains_out": ((8, width), F32, True),
            "routers_out": ((width, p.mixers + experts), F32, True),
        },
        {},
    )
    return (
        four.result_out[None],
        four.input_grad_out[None],
        four.gains_out[0],
        four.gains_out[1],
        four.query_out,
        four.key_out,
        four.value_out,
        four.out_out,
        four.routers_out[:, : p.mixers],
        four.routers_out[:, p.mixers :],
        four.in_out,
        four.back_out,
        four.gains_out[2],
    )


def solution(mesh):
    return jax.shard_map(
        on_device,
        mesh=mesh,
        in_specs=(
            P("dp", "blk", None),
            P("dp", None),
            P(None, "dp", "blk", None),
            P(None, "dp", "blk", None),
            P(),
            P(),
            P(None, "dp", "blk"),
            P("dp", "blk"),
            P("dp", "blk"),
            P(None, "blk", "dp"),
            P(),
            P(),
            P("dp", "blk", None),
            P("dp", "blk", None),
            P(),
            P("dp", "blk", None),
        ),
        out_specs=(
            P("dp", "blk", None),
            P("dp", "blk", None),
            P(),
            P(),
            P(None, "dp", "blk"),
            P("dp", "blk"),
            P("dp", "blk"),
            P(None, "blk", "dp"),
            P(),
            P(),
            P("dp", "blk", None),
            P("dp", "blk", None),
            P(),
        ),
        check_vma=False,
    )
```

```python
import functools
from types import SimpleNamespace
from typing import NamedTuple

import jax
import jax.numpy as jnp
from jax import lax
from jax.experimental import pallas as pl
from jax.experimental.pallas import tpu as pltpu
from jax.sharding import PartitionSpec as P

HEADS = 8
HD = 64
MAXLEN = 256
QROWS = 128
WINDOW = MAXLEN + QROWS
LANES = 128
EPSILON = 1e-06
MASKED_SCORE = -1e30
MESH = pl.DeviceIdType.MESH
BF = jnp.bfloat16
F32 = jnp.float32
VMEM_BYTES = 61 * 2**20


class Plan(NamedTuple):
    blk: int
    dp: int
    lo: int
    hi: int
    seq: int
    width: int
    heads: int
    mixers: int
    top: int
    experts: int
    local: int
    group: int
    cap: int
    ff: int

    @property
    def length(self):
        return self.blk * self.seq

    @property
    def cols(self):
        return self.heads * HD

    @property
    def qkv(self):
        return (self.mixers + 2) * self.cols

    @property
    def all_cols(self):
        return (2 * self.mixers + 2) * self.cols

    @property
    def blocks(self):
        return self.length // QROWS

    @property
    def slots(self):
        return self.experts * self.cap

    @property
    def tile(self):
        return 512 if self.slots <= 768 else 256

    @property
    def chips(self):
        return self.blk // 2


def mm(a, b):
    return lax.dot_general(a, b, (((1,), (0,)), ((), ())), preferred_element_type=F32)


def mm_nt(a, b):
    return lax.dot_general(a, b, (((1,), (1,)), ((), ())), preferred_element_type=F32)


def place():
    return lax.axis_index("blk"), lax.axis_index("dp")


def turn(index, by, size):
    return lax.rem(index + (by % size), size)


def greet(peers):
    barrier = pltpu.get_barrier_semaphore()
    for peer in peers:
        pl.semaphore_signal(barrier, inc=1, device_id=peer, device_id_type=MESH)
    pl.semaphore_wait(barrier, len(peers))


def send(src, dst, sems, slot, peer):
    copy = pltpu.make_async_remote_copy(
        src_ref=src,
        dst_ref=dst,
        send_sem=sems[0].at[slot],
        recv_sem=sems[1].at[slot],
        device_id=peer,
        device_id_type=MESH,
    )
    copy.start()
    return copy


def aligned(value, by):
    return pl.multiple_of(value, by)


def pack_peers(p):
    b, d = place()
    y, c = b // 2, lax.rem(b, 2)
    peers = [(2 * y + 1 - c, d)]
    return peers + [(2 * turn(y, s, p.chips) + c, d) for s in range(1, p.chips)]


def slot_peer(p, s):
    b, d = place()
    e, g = b // p.group, lax.rem(b, p.group)
    return (turn(e, s // p.dp, p.local) * p.group + g, turn(d, s % p.dp, p.dp))


def slot_peers(p):
    return [slot_peer(p, s) for s in range(1, p.experts)]


def slot_source(p, s):
    b, d = place()
    e, g = b // p.group, lax.rem(b, p.group)
    return (turn(e, -(s // p.dp), p.local) * p.group + g, turn(d, -(s % p.dp), p.dp))


def dp_peers(p):
    b, d = place()
    z, x = d // p.lo, lax.rem(d, p.lo)
    peers = [(b, turn(z, s, p.hi) * p.lo + x) for s in range(1, p.hi)]
    return peers + [(b, z * p.lo + turn(x, t, p.lo)) for t in range(1, p.lo)]


def expert_peers(p):
    b, d = place()
    e, g = b // p.group, lax.rem(b, p.group)
    peers = [(turn(e, s, p.local) * p.group + g, d) for s in range(1, p.local)]
    return peers + [(e * p.group + turn(g, t, p.group), d) for t in range(1, p.group)]


def link(src, dst, sems, slot, peer):
    return pltpu.make_async_remote_copy(
        src_ref=src,
        dst_ref=dst,
        send_sem=sems[0].at[slot],
        recv_sem=sems[1].at[slot],
        device_id=peer,
        device_id_type=MESH,
    )


class PackGather:
    def __init__(self, p, buf, sems):
        self.p, self.buf, self.far, self.near = p, buf, sems[0:2], sems[2:4]
        self.done_near = self.done_far = False

    def begin(self):
        p = self.p
        b, d = place()
        y, c = b // 2, lax.rem(b, 2)
        own = self.buf.at[b]
        self.first = [
            send(own, own, self.far, s - 1, (2 * turn(y, s, p.chips) + c, d))
            for s in range(1, p.chips)
        ]
        self.second = [send(own, own, self.near, 0, (2 * y + 1 - c, d))]

    def finish_near(self):
        if not self.done_near:
            self.second[0].wait_recv()
        self.done_near = True

    def finish_far(self):
        if self.done_far:
            return
        self.done_far = True
        p = self.p
        b, d = place()
        y, c = b // 2, lax.rem(b, 2)
        for s in range(1, p.chips):
            self.first[s - 1].wait_recv()
            block = self.buf.at[2 * turn(y, -s, p.chips) + c]
            self.second.append(send(block, block, self.near, s, (2 * y + 1 - c, d)))
        self.finish_near()
        for copy in self.second[1:]:
            copy.wait_recv()

    def end(self):
        for copy in self.first + self.second:
            copy.wait_send()


class PackSum:
    def __init__(self, p, bufs, sems):
        self.p, self.bufs = p, bufs
        self.far, self.near = sems[0:2], sems[2:4]
        self.first, self.second = {}, []

    def give(self, s, term):
        p, r = self.p, self.bufs
        b, d = place()
        y, c = b // 2, lax.rem(b, 2)
        r.part[s] = term.astype(BF)
        self.first[s] = send(r.part.at[s], r.near_in.at[s], self.near, s, (2 * y + 1 - c, d))

    def pass_on(self, s, term):
        p, r = self.p, self.bufs
        b, d = place()
        y, c = b // 2, lax.rem(b, 2)
        self.first[s].wait_recv()
        r.far_out[s - 1] = (term + r.near_in[s].astype(F32)).astype(BF)
        self.second.append(
            send(r.far_out.at[s - 1], r.far_in.at[s - 1], self.far, s - 1, (2 * turn(y, s, p.chips) + c, d))
        )

    def total(self, term):
        r = self.bufs
        self.first[0].wait_recv()
        term = term + r.near_in[0].astype(F32)
        for k, copy in enumerate(self.second):
            copy.wait_recv()
            term = term + r.far_in[k].astype(F32)
        for copy in list(self.first.values()) + self.second:
            copy.wait_send()
        return term


def slot_send(p, src, dst, sems, s, peer):
    rows = pl.ds(s * p.cap, p.cap)
    return send(src.at[rows], dst.at[rows], sems, s, peer)


def slot_sends(p, src, dst, sems, peer):
    dst[0 : p.cap, :] = src[0 : p.cap, :]
    return {s: slot_send(p, src, dst, sems, s, peer(p, s)) for s in range(1, p.experts)}


def receive(copies, sources):
    for s in sources:
        if s in copies:
            copies[s].wait_recv()


def sent(copies):
    for copy in copies.values() if isinstance(copies, dict) else copies:
        copy.wait_send()


def move(r, src, dst):
    copy = pltpu.make_async_copy(src, dst, r.moves.at[r.moved])
    r.moved += 1
    copy.start()
    return copy


def moves(r, pairs):
    return [move(r, src, dst) for src, dst in pairs]


def arrive(copies):
    for copy in copies:
        copy.wait()
    copies.clear()


def norm_parts(state):
    inverse = lax.rsqrt(jnp.mean(state * state, axis=-1, keepdims=True) + EPSILON)
    return inverse, state * inverse


def norm_back(state, gain, grad):
    inverse, unit = norm_parts(state)
    scaled = grad * gain
    back = inverse * scaled - state * (inverse * inverse * inverse) * jnp.mean(
        scaled * state, axis=-1, keepdims=True
    )
    return back, jnp.sum(grad * unit, axis=0, keepdims=True)


def segment_columns(p, segments, seg_cols):
    seg_cols[0:MAXLEN, :] = jnp.full((MAXLEN, 8), -1.0, F32)
    for start in range(0, p.length, QROWS):
        row = segments[:, start : start + QROWS].astype(F32)
        seg_cols[MAXLEN + start : MAXLEN + start + QROWS, :] = jnp.broadcast_to(row, (8, QROWS)).T


def attention_mask(r, start):
    keys = r.seg_cols[pl.ds(start, WINDOW), 0:1]
    queries = r.segments[:, pl.ds(start, QROWS)].astype(F32)
    key_at = lax.broadcasted_iota(jnp.int32, (WINDOW, QROWS), 0) - MAXLEN
    query_at = lax.broadcasted_iota(jnp.int32, (WINDOW, QROWS), 1)
    return jnp.where((key_at <= query_at) & (keys == queries), 0.0, MASKED_SCORE)


def head_rows(p, dst, at, values):
    flat = values.T
    lane = lax.broadcasted_iota(jnp.int32, flat.shape, 1) // HD
    for h in range(p.heads):
        dst[h, at, :] = jnp.where(lane == h, flat, 0.0).astype(BF)


def pick_rows(p, routes, terms):
    picked = []
    for j in range(p.top):
        row = routes[j : j + 1, :]
        total = None
        for e in range(p.mixers):
            term = jnp.where(row == e, terms(e), 0.0)
            total = term if total is None else total + term
        picked.append(total)
    return picked


def spread_rows(p, routes, values, e):
    total = None
    for j in range(p.top):
        term = jnp.where(routes[j : j + 1, :] == e, values[j], 0.0)
        total = term if total is None else total + term
    return total


def pick_table(p, r, step, bb):
    return r.all_picks[bb, 8 * step : 8 * step + p.top, :]


def transposed(dst, src, rows, first, tile):
    for start in range(0, rows, tile):
        dst[start : start + tile, :] = src[:, first + start : first + start + tile].astype(F32).T.astype(BF)


def project(p, r, a, step, bb):
    cols, sub = p.cols, p.seq // QROWS
    states = a.nt[bb]
    table = pick_table(p, r, step, bb)
    logits = mm(r.router_row[...], states)
    chosen = pick_rows(p, table, lambda e: logits[e : e + 1, :])
    peak = functools.reduce(jnp.maximum, chosen)
    chosen = [jnp.exp(row - peak) for row in chosen]
    scale = 1.0 / sum(chosen)
    for j in range(p.top):
        a.gates[bb, j : j + 1, :] = chosen[j] * scale
    values = mm(r.w_t[...], states)
    for k in range(sub):
        lanes = slice(k * QROWS, (k + 1) * QROWS)
        queries = pick_rows(p, table[:, lanes], lambda e: values[e * cols : (e + 1) * cols, lanes])
        for j in range(p.top):
            a.qs[bb * sub + k, :, j * QROWS : (j + 1) * QROWS] = (queries[j] * (HD**-0.5)).astype(BF)
    at = pl.ds(aligned(MAXLEN + bb * p.seq, QROWS), p.seq)
    keys = values[p.mixers * cols : (p.mixers + 1) * cols, :]
    a.kt[:, at] = keys.astype(BF)
    a.vt[:, at] = values[(p.mixers + 1) * cols :, :].astype(BF)
    head_rows(p, r.k_heads, at, keys)


def attend(p, r, a, step, bb):
    cols, sub = p.cols, p.seq // QROWS

    @pl.loop(0, sub)
    def _(k):
        i = bb * sub + k
        start = aligned(i * QROWS, QROWS)
        keys = pl.ds(start, WINDOW)
        bias = attention_mask(r, start)
        bias = jnp.concatenate([bias] * p.top, axis=1)
        queries = a.qs[i]
        for head in range(p.heads):
            scores = mm(r.k_heads[head, keys, :], queries) + bias
            peak = jnp.max(scores, axis=0, keepdims=True)
            scores = jnp.exp(scores - peak)
            total = jnp.sum(scores, axis=0, keepdims=True)
            a.lse[i, head : head + 1, :] = peak + jnp.log(total)
            probs = (scores * (1.0 / total)).astype(BF)
            rows = slice(head * HD, (head + 1) * HD)
            a.att[i, rows, :] = mm(a.vt[rows, keys], probs).astype(BF)
        at = pl.ds(aligned(k * QROWS, QROWS), QROWS)
        table = r.all_picks[bb, 8 * step : 8 * step + p.top, at]
        weights = a.gates[bb, 0 : p.top, at]
        values = [
            a.att[i, :, j * QROWS : (j + 1) * QROWS].astype(F32) * weights[j : j + 1, :] for j in range(p.top)
        ]
        for e in range(p.mixers):
            a.mix[e * cols : (e + 1) * cols, pl.ds(start, QROWS)] = spread_rows(p, table, values, e).astype(BF)


def attention_forward(p, r, a, step, state, before, out_ready, after):
    b, _ = place()
    y, c = b // 2, lax.rem(b, 2)
    a.nt[b] = (norm_parts(state)[1] * r.gain_one[...].astype(F32)).T.astype(BF)
    gather = PackGather(p, a.nt, a.gather_sems)
    gather.begin()
    r.k_heads[:, 0:MAXLEN, :] = jnp.zeros((p.heads, MAXLEN, p.cols), BF)
    a.kt[:, 0:MAXLEN] = jnp.zeros((p.cols, MAXLEN), BF)
    a.vt[:, 0:MAXLEN] = jnp.zeros((p.cols, MAXLEN), BF)
    before(gather)
    project(p, r, a, step, b)
    gather.finish_near()
    project(p, r, a, step, 2 * y + 1 - c)
    attend(p, r, a, step, 2 * y + 1)
    gather.finish_far()
    for s in range(1, p.chips):
        yy = turn(y, s, p.chips)

        @pl.loop(0, 2)
        def _(k):
            project(p, r, a, step, 2 * yy + k)

    def branch(bb):
        return mm(r.all_w[:, p.qkv :], a.mix[:, pl.ds(aligned(bb * p.seq, p.seq), p.seq)])

    shares = PackSum(p, r, a.sum_sems)
    for s in range(1, p.chips):
        yy = turn(y, s, p.chips)
        attend(p, r, a, step, 2 * yy + 1 - c)
        if s == 1:
            out_ready()
        shares.give(s, branch(2 * yy + 1 - c))
        attend(p, r, a, step, 2 * yy + c)
        shares.pass_on(s, branch(2 * yy + c))
    after()
    attend(p, r, a, step, 2 * y)
    shares.give(0, branch(2 * y + 1 - c))
    total = shares.total(branch(b))
    gather.end()
    return total


def attention_grads(p, r, a, step, bb):
    cols, sub = p.cols, p.seq // QROWS
    table = pick_table(p, r, step, bb)
    weights = a.gates[bb, 0 : p.top, :]
    values = mm(r.wo[...], r.gt[bb])
    for k in range(sub):
        lanes = slice(k * QROWS, (k + 1) * QROWS)
        here = table[:, lanes]
        picked = pick_rows(p, here, lambda e: values[e * cols : (e + 1) * cols, lanes])
        grads = []
        for j in range(p.top):
            slot = slice(j * QROWS, (j + 1) * QROWS)
            products = picked[j] * a.att[bb * sub + k, :, slot].astype(F32)
            grads.append(jnp.sum(products, axis=0, keepdims=True))
            for head in range(p.heads):
                mean = jnp.sum(products[head * HD : (head + 1) * HD], axis=0, keepdims=True)
                r.means[bb * sub + k, head : head + 1, slot] = mean * weights[j : j + 1, lanes]
            a.att[bb * sub + k, :, slot] = (picked[j] * weights[j : j + 1, lanes]).astype(BF)
        mean = sum(weights[j : j + 1, lanes] * grads[j] for j in range(p.top))
        back = [weights[j : j + 1, lanes] * (grads[j] - mean) for j in range(p.top)]
        for e in range(p.mixers):
            r.dlog[bb, e : e + 1, lanes] = spread_rows(p, here, back, e)


def attend_back(p, r, a, step, bb):
    cols, sub = p.cols, p.seq // QROWS

    @pl.loop(0, sub)
    def _(k):
        i = bb * sub + k
        start = aligned(i * QROWS, QROWS)
        keys = pl.ds(start, WINDOW)
        bias = attention_mask(r, start)
        bias = jnp.concatenate([bias] * p.top, axis=1)
        queries = a.qs[i]
        grads = a.att[i]
        query_grads = []
        for head in range(p.heads):
            rows = slice(head * HD, (head + 1) * HD)
            scores = mm(r.k_heads[head, keys, :], queries) + bias
            probs = jnp.exp(scores - a.lse[i, head : head + 1, :])
            mean = r.means[i, head : head + 1, :]
            dscores = (probs * (mm(r.v_heads[head, keys, :], grads) - mean)).astype(BF)
            r.dvt[rows, keys] += mm_nt(grads[rows], probs.astype(BF))
            r.dkt[rows, keys] += mm_nt(queries[rows], dscores)
            query_grads.append(mm(a.kt[rows, keys], dscores) * (HD**-0.5))
        at = pl.ds(aligned(k * QROWS, QROWS), QROWS)
        table = r.all_picks[bb, 8 * step : 8 * step + p.top, at]
        merged = jnp.concatenate(query_grads, axis=0)
        values = [merged[:, j * QROWS : (j + 1) * QROWS] for j in range(p.top)]
        for e in range(p.mixers):
            r.dall[e * cols : (e + 1) * cols, pl.ds(start, QROWS)] = spread_rows(p, table, values, e).astype(BF)


def attention_backward(p, r, a, step, state, grad, before, middle, last):
    b, _ = place()
    y, c = b // 2, lax.rem(b, 2)
    r.gt[b] = grad.T.astype(BF)
    gather = PackGather(p, r.gt, a.back_gather_sems)
    gather.begin()
    r.dkt[...] = jnp.zeros_like(r.dkt)
    r.dvt[...] = jnp.zeros_like(r.dvt)
    before()

    @pl.loop(0, (p.length + MAXLEN) // QROWS)
    def _(k):
        at = pl.ds(aligned(k * QROWS, QROWS), QROWS)
        head_rows(p, r.k_heads, at, a.kt[:, at].astype(F32))
        head_rows(p, r.v_heads, at, a.vt[:, at].astype(F32))

    attention_grads(p, r, a, step, b)
    gather.finish_near()
    attention_grads(p, r, a, step, 2 * y + 1 - c)
    attend_back(p, r, a, step, 2 * y)
    gather.finish_far()
    for s in range(1, p.chips):
        yy = turn(y, s, p.chips)

        @pl.loop(0, 2)
        def _(k):
            attention_grads(p, r, a, step, 2 * yy + k)

    middle()
    for s in range(1, p.chips):
        yy = turn(y, s, p.chips)

        @pl.loop(0, 2)
        def _(k):
            attend_back(p, r, a, step, 2 * yy + k)

    cols = p.cols
    router_col = r.router_row[...].astype(F32).T.astype(BF)

    def branch(bb):
        lanes = pl.ds(aligned(bb * p.seq, p.seq), p.seq)
        past = pl.ds(aligned(bb * p.seq + MAXLEN, QROWS), p.seq)
        r.dall[p.mixers * cols : (p.mixers + 1) * cols, lanes] = r.dkt[:, past].astype(BF)
        r.dall[(p.mixers + 1) * cols :, lanes] = r.dvt[:, past].astype(BF)
        return mm(r.all_w[:, : p.qkv], r.dall[:, lanes]) + mm(router_col, r.dlog[bb].astype(BF))

    shares = PackSum(p, r, a.back_sum_sems)
    for s in range(1, p.chips):
        yy = turn(y, s, p.chips)
        shares.give(s, branch(2 * yy + 1 - c))
        shares.pass_on(s, branch(2 * yy + c))
    attend_back(p, r, a, step, 2 * y + 1)
    shares.give(0, branch(2 * y + 1 - c))
    own = branch(b)
    last()
    router = sum(mm_nt(r.dlog[bb].astype(BF), a.nt[bb]) for bb in range(p.blk))
    grad_n = shares.total(own).T
    gather.end()
    back, gain = norm_back(state, r.gain_one[...].astype(F32), grad_n)
    return grad + back, gain, router


def attention_weight_grads(p, r, a, start, stop, add):
    tile = 2 * p.cols
    for first in range(start, stop, tile):
        total = None
        for bb in range(p.blk):
            lanes = slice(bb * p.seq, (bb + 1) * p.seq)
            if first < p.qkv:
                term = mm_nt(a.nt[bb], r.dall[first : first + tile, lanes])
            else:
                term = mm_nt(r.gt[bb], a.mix[first - p.qkv : first - p.qkv + tile, lanes])
            total = term if total is None else total + term
        at = slice(first, first + tile)
        r.grad_w[:, at] = (r.grad_w[:, at].astype(F32) + total if add else total).astype(BF)


def own_lane(p):
    b, d = place()
    mine = d * p.local + b // p.group
    return jnp.where(lax.broadcasted_iota(jnp.int32, (1, LANES), 1) == mine, 1.0, 0.0)


def slot_gates(p, r, rows, pair):
    own = own_lane(p)
    logits = mm_nt(rows, r.router[...])
    return 1.0 / (1.0 + jnp.exp(jnp.sum(logits * (pair - 2.0 * own), axis=-1, keepdims=True)))


def gelu_both(inner):
    half = 0.5 * (1.0 + lax.erf(inner * 0.7071067811865476))
    slope = half + inner * jnp.exp(-0.5 * inner * inner) * 0.3989422804014327
    return inner * half, slope


def fill_router(p, r):
    r.router[...] = jnp.zeros_like(r.router)
    r.router[0 : p.experts, :] = r.router_in[...]


def slot_groups(p):
    per = max(1, p.experts // 4)
    return [(pl.ds(first * p.cap, per * p.cap), range(first, first + per)) for first in range(0, p.experts, per)]


def expert_output(p, r, rows, at, keep):
    total = None
    for start in range(0, p.ff, p.tile):
        lanes = slice(start, start + p.tile)
        inner = mm(rows, r.all_in[:, lanes])
        if keep:
            act, slope = gelu_both(inner)
            act = act.astype(BF)
            r.act[at, lanes] = act
            r.slope[at, lanes] = slope.astype(BF)
        else:
            act = (inner * (0.5 * (1.0 + lax.erf(inner * 0.7071067811865476)))).astype(BF)
        term = mm(act, r.all_back[lanes, :])
        total = term if total is None else total + term
    return total


def expert_keep(p, r, rows, at):
    for start in range(0, p.ff, p.tile):
        lanes = slice(start, start + p.tile)
        act, slope = gelu_both(mm(rows, r.all_in[:, lanes]))
        r.act[at, lanes] = act.astype(BF)
        r.slope[at, lanes] = slope.astype(BF)


def expert_input_grad(p, r, at, u, rows, out, pair, dst):
    gate = slot_gates(p, r, rows, pair)
    grads = (u * gate).astype(BF)
    r.u_in[at, :] = grads
    coeff = gate * (1.0 - gate) * jnp.sum(u * out, axis=-1, keepdims=True) * (2.0 * own_lane(p) - pair)
    coeff = coeff.astype(BF)
    r.coeff[at, :] = coeff
    dst[at, :] = mm(coeff, r.router[...]).astype(BF)
    total = None
    for start in range(0, p.ff, p.tile):
        lanes = slice(start, start + p.tile)
        inner = (mm_nt(grads, r.all_back[lanes, :]) * r.slope[at, lanes].astype(F32)).astype(BF)
        r.slope[at, lanes] = inner
        term = mm_nt(inner, r.all_in[:, lanes])
        total = term if total is None else total + term
    dst[at, :] = (total + dst[at, :].astype(F32)).astype(BF)


def expert_weight_grads(p, r, arrived, add):
    r.arrived_t[...] = arrived[...].astype(F32).T.astype(BF)
    for start in range(0, p.ff, p.tile // 2):
        lanes = slice(start, start + p.tile // 2)
        term = mm(r.act[:, lanes].astype(F32).T.astype(BF), r.u_in[...])
        r.grad_back[lanes, :] = (r.grad_back[lanes, :].astype(F32) + term if add else term).astype(BF)
        term = mm(r.arrived_t[...], r.slope[:, lanes])
        r.grad_in[:, lanes] = (r.grad_in[:, lanes].astype(F32) + term if add else term).astype(BF)
    return mm(r.coeff[...].astype(F32).T.astype(BF)[0 : p.experts], arrived[...])


def slot_tables(p, r):
    b, d = place()
    e = b // p.group
    place_in = lax.broadcasted_iota(jnp.int32, (p.experts, 1), 0)
    ids = lax.rem(d + lax.rem(place_in, p.dp), p.dp) * p.local + lax.rem(e + place_in // p.dp, p.local)
    earlier = (
        lax.broadcasted_iota(jnp.int32, (p.seq, p.seq), 0) < lax.broadcasted_iota(jnp.int32, (p.seq, p.seq), 1)
    ).astype(BF)
    slot_ids = lax.broadcasted_iota(jnp.int32, (p.cap, p.seq), 0).astype(F32)
    r.pair_out[...] = jnp.zeros_like(r.pair_out)
    for step in range(2):
        one = r.routes[8 * step + p.top : 8 * step + p.top + 1, :]
        two = r.routes[8 * step + p.top + 1 : 8 * step + p.top + 2, :]
        member = jnp.where((one == ids) | (two == ids), 1.0, 0.0)
        rank = jnp.where(member > 0.5, mm(member.astype(BF), earlier), -1.0)
        both = jnp.broadcast_to((one + two).astype(F32), (8, p.seq)).astype(BF)
        for s in range(p.experts):
            table = jnp.where(rank[s : s + 1, :] == slot_ids, 1.0, 0.0).astype(BF)
            r.disp[step, pl.ds(s * p.cap, p.cap), :] = table
            r.pair_out[s, step : step + 1, 0 : p.cap] = mm_nt(both, table)[0:1]
        r.comb[step] = r.disp[step].astype(F32).T.astype(BF)
    r.pair_in[0] = r.pair_out[0]
    return [
        send(r.pair_out.at[s], r.pair_in.at[s], (r.pair_s, r.pair_r), s, slot_peer(p, s)) for s in range(1, p.experts)
    ]


def slot_pairs(p, r):
    b, d = place()
    mine = (d * p.local + b // p.group).astype(F32)
    lanes = lax.broadcasted_iota(jnp.int32, (p.cap, LANES), 1).astype(F32)
    for step in range(2):
        totals = r.pair_in[:, step, :].T
        for s in range(p.experts):
            other = totals[0 : p.cap, s : s + 1] - mine
            both = jnp.where(lanes == mine, 1.0, 0.0) + jnp.where(lanes == other, 1.0, 0.0)
            r.pair[step, pl.ds(s * p.cap, p.cap), :] = both.astype(BF)


def forward_kernel(p, r):
    b, d = place()
    z, x = d // p.lo, lax.rem(d, p.lo)
    e, g = b // p.group, lax.rem(b, p.group)
    own_rows = r.weight_key.shape[0]
    in_rows, back_rows = r.weight_in.shape[1], r.weight_back.shape[1]

    def w_at(index, part):
        lanes = slice(0, p.qkv) if part == 0 else slice(p.qkv, p.all_cols)
        return r.all_w.at[pl.ds(aligned(index * own_rows, own_rows), own_rows), lanes]

    def in_at(index):
        return r.all_in.at[pl.ds(aligned(index * in_rows, in_rows), in_rows)]

    def back_at(index):
        return r.all_back.at[pl.ds(aligned(index * back_rows, back_rows), back_rows)]

    own = pl.ds(aligned(d * own_rows, own_rows), own_rows)
    for k in range(p.mixers):
        r.all_w[own, k * p.cols : (k + 1) * p.cols] = r.weight_query[k]
        r.all_w[own, p.qkv + k * p.cols : p.qkv + (k + 1) * p.cols] = r.weight_out[k]
    r.all_w[own, p.mixers * p.cols : (p.mixers + 1) * p.cols] = r.weight_key[...]
    r.all_w[own, (p.mixers + 1) * p.cols : p.qkv] = r.weight_value[...]
    greet(pack_peers(p) + slot_peers(p) + dp_peers(p) + expert_peers(p))
    last = p.hi - 1

    def hop(part, k, up):
        rows = w_at((z - k if up else z + k) * p.lo + x, part)
        slot = (2 * part + (0 if up else 1)) * last + k
        return link(rows, rows, (r.hi_s, r.hi_r), slot, (b, (z + 1 if up else z - 1) * p.lo + x))

    def arrival(part, k, up):
        rows = w_at((z - 1 - k if up else z + 1 + k) * p.lo + x, part)
        return link(rows, rows, (r.hi_s, r.hi_r), (2 * part + (0 if up else 1)) * last + k, (b, d))

    def cross(part, source, t):
        rows = w_at(source * p.lo + x, part)
        slot = (part * p.hi + source) * (p.lo - 1) + t - 1
        return link(rows, rows, (r.lo_s, r.lo_r), slot, (b, z * p.lo + turn(x, t, p.lo)))

    def goes(k, up):
        return (z >= k) & (z < last) if up else (z + k <= last) & (z > 0)

    def comes(k, up):
        return z >= k + 1 if up else z + k + 1 <= last

    def w_begin(part):
        for up in (True, False):
            pl.when(goes(0, up))(lambda: hop(part, 0, up).start())
        for t in range(1, p.lo):
            cross(part, z, t).start()

    def w_pass(part):
        for k in range(last):
            for up in (True, False):

                @pl.when(comes(k, up))
                def _():
                    arrival(part, k, up).wait_recv()
                    if k + 1 < last:
                        pl.when(goes(k + 1, up))(lambda: hop(part, k + 1, up).start())
                    for t in range(1, p.lo):
                        cross(part, z - 1 - k if up else z + 1 + k, t).start()

    def w_finish(part):
        for source in range(p.hi):
            for t in range(1, p.lo):
                rows = w_at(source * p.lo + turn(x, -t, p.lo), part)
                slot = (part * p.hi + source) * (p.lo - 1) + t - 1
                link(rows, rows, (r.lo_s, r.lo_r), slot, (b, d)).wait_recv()

    def w_end():
        for part in range(2):
            for k in range(last):
                for up in (True, False):
                    pl.when(goes(k, up))(lambda: hop(part, k, up).wait_send())
            for source in range(p.hi):
                for t in range(1, p.lo):
                    cross(part, source, t).wait_send()

    local, over, beside = [], {}, []

    def experts_begin():
        for s in range(1, p.local):
            to = turn(e, s, p.local)
            peer = (to * p.group + g, d)
            over[s, 0] = send(r.weight_in.at[to], in_at(b), (r.wide_s, r.wide_r), 2 * s - 2, peer)
            over[s, 1] = send(r.weight_back.at[to], back_at(b), (r.wide_s, r.wide_r), 2 * s - 1, peer)
        for t in range(1, p.group):
            peer = (e * p.group + turn(g, t, p.group), d)
            beside.append(send(r.weight_in.at[e], in_at(b), (r.near_s, r.near_r), 2 * t - 2, peer))
            beside.append(send(r.weight_back.at[e], back_at(b), (r.near_s, r.near_r), 2 * t - 1, peer))

    def experts_pass():
        for s in range(1, p.local):
            source = turn(e, -s, p.local) * p.group + g
            for which, rows in ((0, in_at(source)), (1, back_at(source))):
                over[s, which].wait_recv()
                for t in range(1, p.group):
                    k = (s * (p.group - 1) + t - 1) * 2 + which
                    peer = (e * p.group + turn(g, t, p.group), d)
                    beside.append(send(rows, rows, (r.near_s, r.near_r), k, peer))

    tables = []
    saves = []

    w_begin(0)
    for step in range(2):
        r.routes[8 * step : 8 * step + p.top, :] = r.attention_routes[step]
        r.routes[8 * step + p.top : 8 * step + 6, :] = r.expert_routes[step]
        r.routes[8 * step + 6 : 8 * step + 8, :] = jnp.zeros((2, p.seq), jnp.int32)
    fill_router(p, r)
    r.all_picks[b] = r.routes[...]
    picks = PackGather(p, r.all_picks, r.picks_sems)
    picks.begin()
    state = r.x[...].astype(F32)

    def before(gather):
        local.extend(moves(r, [(r.weight_in.at[e], in_at(b)), (r.weight_back.at[e], back_at(b))]))
        segment_columns(p, r.segments, r.seg_cols)
        tables.extend(slot_tables(p, r))
        gather.finish_far()
        picks.finish_far()
        experts_begin()
        w_pass(0)
        w_begin(1)
        w_finish(0)
        transposed(r.w_t, r.all_w, p.qkv, 0, 2 * p.cols)

    def out_ready():
        w_pass(1)
        w_finish(1)

    def after():
        saves.extend(moves(r, [(r.all_w, r.all_w_out), (r.disp, r.disp_out), (r.comb, r.comb_out)]))
        experts_pass()

    total = attention_forward(p, r, r.a, 0, state, before, out_ready, after)
    middle = state + total.T
    r.middle[...] = middle
    m = (norm_parts(middle)[1] * r.gain_two[...].astype(F32)).astype(BF)
    r.outgoing[...] = mm(r.disp[0], m).astype(BF)
    there = slot_sends(p, r.outgoing, r.arrived, (r.go_s, r.go_r), slot_peer)
    saves.extend(moves(r, [(getattr(r.a, k), getattr(r, k + "_out")) for k in SAVED]))
    for copy in tables:
        copy.wait_recv()
    slot_pairs(p, r)
    for copy in beside:
        copy.wait_recv()
    arrive(local)
    saves.extend(moves(r, [(r.all_in, r.all_in_out), (r.all_back, r.all_back_out), (r.pair, r.pair_end)]))
    back = {}
    for at, sources in slot_groups(p):
        receive(there, sources)
        rows = r.arrived[at, :]
        out = expert_output(p, r, rows, at, False)
        r.produced[at, :] = out.astype(BF)
        r.ret_out[at, :] = (out * slot_gates(p, r, rows, r.pair[0, at, :].astype(F32))).astype(BF)
        for s in sources:
            if s:
                back[s] = slot_send(p, r.ret_out, r.ret_in, (r.ret_s, r.ret_r), s, slot_source(p, s))
    r.ret_in[0 : p.cap, :] = r.ret_out[0 : p.cap, :]
    receive(back, range(p.experts))
    r.first[...] = r.middle[...] + mm(r.comb[0], r.ret_in[...])
    sent(there)
    sent(back)
    sent(tables)
    sent(beside)
    w_end()
    sent(over)
    picks.end()
    arrive(saves)


def turn_kernel(p, r):
    greet(pack_peers(p) + slot_peers(p))
    early = moves(
        r, [(r.disp_in.at[1], r.disp), (r.all_w_in, r.all_w), (r.comb_in.at[1], r.comb), (r.pair_in.at[1], r.pair)]
    )
    fill_router(p, r)
    weights = moves(r, [(r.all_in_in, r.all_in), (r.all_back_in, r.all_back)])
    first = r.first[...]
    stop = 1.0 / (1.0 + jnp.exp(-jnp.sum(first * r.halt[...].astype(F32), axis=-1, keepdims=True)))
    cot = r.cot[...].astype(F32)
    there_u, saves = {}, []

    def before(gather):
        arrive(early)
        r.u_out[...] = mm(r.disp[...], ((1.0 - stop) * cot).astype(BF)).astype(BF)
        there_u.update(slot_sends(p, r.u_out, r.u_in, (r.u_s, r.u_r), slot_peer))
        segment_columns(p, r.segments, r.seg_cols)
        transposed(r.w_t, r.all_w, p.qkv, 0, 2 * p.cols)

    total = attention_forward(p, r, r.a, 1, first, before, lambda: None, lambda: None)
    middle = first + total.T
    r.middle[...] = middle
    m = (norm_parts(middle)[1] * r.gain_two[...].astype(F32)).astype(BF)
    r.outgoing[...] = mm(r.disp[...], m).astype(BF)
    there = slot_sends(p, r.outgoing, r.arrived, (r.go_s, r.go_r), slot_peer)
    transposed(r.wo, r.all_w, p.mixers * p.cols, p.qkv, 2 * p.cols)
    arrive(weights)
    sent(there_u)
    ret_out = r.u_out
    back, back_out = {}, {}
    for at, sources in slot_groups(p):
        receive(there_u, sources)
        receive(there, sources)
        rows = r.arrived[at, :]
        pair = r.pair[at, :].astype(F32)
        out = expert_output(p, r, rows, at, True)
        ret_out[at, :] = (out * slot_gates(p, r, rows, pair)).astype(BF)
        expert_input_grad(p, r, at, r.u_in[at, :].astype(F32), rows, out, pair, r.gret_out)
        for s in sources:
            if s:
                back[s] = slot_send(p, r.gret_out, r.gret_in, (r.gret_s, r.gret_r), s, slot_source(p, s))
    r.gret_in[0 : p.cap, :] = r.gret_out[0 : p.cap, :]
    r.ret_in[0 : p.cap, :] = ret_out[0 : p.cap, :]
    r.grad_router[...] = expert_weight_grads(p, r, r.arrived, False)
    saves.extend(moves(r, [(r.grad_in, r.grad_in_out), (r.grad_back, r.grad_back_out)]))
    receive(back, range(p.experts))
    step_back, gain_two = norm_back(r.middle[...], r.gain_two[...].astype(F32), mm(r.comb[...], r.gret_in[...]))
    r.grad_gain_two[...] = gain_two
    grad_middle = (1.0 - stop) * cot + step_back

    def before_back():
        for s in range(1, p.experts):
            back_out[s] = slot_send(p, ret_out, r.ret_in, (r.ret_s, r.ret_r), s, slot_source(p, s))

    def last():
        attention_weight_grads(p, r, r.a, 0, p.all_cols, False)

    grad, gain_one, router = attention_backward(
        p, r, r.a, 1, first, grad_middle, before_back, lambda: None, last
    )
    saves.extend(moves(r, [(r.grad_w, r.grad_w_out)]))
    r.grad_gain_one[...] = gain_one
    r.grad_mixer[...] = router
    receive(back_out, range(p.experts))
    second = r.middle[...] + mm(r.comb[...], r.ret_in[...])
    r.result[...] = (stop * first + (1.0 - stop) * second).astype(BF)
    grad_stop = jnp.sum(cot * (first - second), axis=-1, keepdims=True)
    coeff = grad_stop * stop * (1.0 - stop)
    r.grad_halt[...] = jnp.sum(coeff * first, axis=0, keepdims=True)
    r.grad_first[...] = stop * cot + coeff * r.halt[...].astype(F32) + grad
    for copies in (there, back, back_out):
        sent(copies)
    arrive(saves)


def backward_kernel(p, r):
    b, d = place()
    z, x = d // p.lo, lax.rem(d, p.lo)
    y, c = b // 2, lax.rem(b, 2)
    e, g = b // p.group, lax.rem(b, p.group)
    rows = r.out_w.shape[0]
    in_rows, back_rows = r.out_in.shape[1], r.out_back.shape[1]
    greet(pack_peers(p) + slot_peers(p) + dp_peers(p) + expert_peers(p))
    early = moves(
        r,
        [
            (r.disp_in.at[0], r.disp),
            (r.pair_in.at[0], r.pair),
            (r.arrived_in, r.arrived),
            (r.all_in_in, r.all_in),
            (r.all_back_in, r.all_back),
            (r.produced_in, r.produced),
        ],
    )
    later = moves(
        r, [(r.grad_in_in, r.grad_in), (r.grad_back_in, r.grad_back), (r.comb_in.at[0], r.comb), (r.all_w_in, r.all_w)]
    )
    later += moves(r, [(r.grad_w_in, r.grad_w)])
    later += moves(r, [(getattr(r, k + "_in"), getattr(r.a, k)) for k in SAVED])
    fill_router(p, r)
    grad_first = r.grad_first[...]
    arrive(early)
    r.u_out[...] = mm(r.disp[...], grad_first.astype(BF)).astype(BF)
    there = slot_sends(p, r.u_out, r.u_in, (r.u_s, r.u_r), slot_peer)
    for at, _ in slot_groups(p):
        expert_keep(p, r, r.arrived[at, :], at)
    segment_columns(p, r.segments, r.seg_cols)
    arrive(later)
    transposed(r.wo, r.all_w, p.mixers * p.cols, p.qkv, 2 * p.cols)
    back = {}
    for at, sources in slot_groups(p):
        receive(there, sources)
        pair = r.pair[at, :].astype(F32)
        out = r.produced[at, :].astype(F32)
        expert_input_grad(p, r, at, r.u_in[at, :].astype(F32), r.arrived[at, :], out, pair, r.produced)
        for s in sources:
            if s:
                back[s] = slot_send(p, r.produced, r.gret_in, (r.gret_s, r.gret_r), s, slot_source(p, s))
    r.gret_in[0 : p.cap, :] = r.produced[0 : p.cap, :]
    r.grad_router[...] = expert_weight_grads(p, r, r.arrived, True)

    def row_block(ref, index, size, lanes=slice(None)):
        return ref.at[pl.ds(aligned(index * size, size), size), lanes]

    near = {}
    for k in range(p.local):
        to = turn(e, k + 1, p.local)
        for t in range(1, p.group):
            member = turn(g, t, p.group)
            slot = k * (p.group - 1) + t - 1
            peer = (e * p.group + member, d)
            owner = to * p.group + member
            near[k, t, 0] = send(
                row_block(r.grad_in, owner, in_rows), r.in_near.at[slot], (r.near_s, r.near_r), 2 * slot, peer
            )
            near[k, t, 1] = send(
                row_block(r.grad_back, owner, back_rows), r.back_near.at[slot], (r.near_s, r.near_r), 2 * slot + 1, peer
            )
    receive(back, range(p.experts))
    step_back, gain_two = norm_back(r.middle[...], r.gain_two[...].astype(F32), mm(r.comb[...], r.gret_in[...]))
    grad_middle = grad_first + step_back
    wide, lo_copies, hi_copies = {}, {}, {}

    def experts_wide():
        for k in range(p.local):
            to = turn(e, k + 1, p.local)
            total_in = row_block(r.grad_in, to * p.group + g, in_rows)[...].astype(F32)
            total_back = row_block(r.grad_back, to * p.group + g, back_rows)[...].astype(F32)
            for t in range(1, p.group):
                slot = k * (p.group - 1) + t - 1
                near[k, t, 0].wait_recv()
                near[k, t, 1].wait_recv()
                total_in = total_in + r.in_near[slot].astype(F32)
                total_back = total_back + r.back_near[slot].astype(F32)
            if k < p.local - 1:
                r.in_far_out[k] = total_in.astype(BF)
                r.back_far_out[k] = total_back.astype(BF)
                peer = (to * p.group + g, d)
                wide[k, 0] = send(r.in_far_out.at[k], r.in_far.at[k], (r.wide_s, r.wide_r), 2 * k, peer)
                wide[k, 1] = send(r.back_far_out.at[k], r.back_far.at[k], (r.wide_s, r.wide_r), 2 * k + 1, peer)
            else:
                r.out_in[e] = total_in.astype(BF)
                r.out_back[e] = total_back.astype(BF)

    parts = (slice(0, p.qkv), slice(p.qkv, p.all_cols))

    def sum_begin(part):
        for k in range(p.hi):
            to = turn(z, k + 1, p.hi)
            for t in range(1, p.lo):
                slot = k * (p.lo - 1) + t - 1
                xx = turn(x, t, p.lo)
                lo_copies[part, k, t] = send(
                    row_block(r.grad_w, to * p.lo + xx, rows, parts[part]),
                    r.w_lo.at[slot, :, parts[part]],
                    (r.lo_s, r.lo_r),
                    part * p.hi * (p.lo - 1) + slot,
                    (b, z * p.lo + xx),
                )

    def sum_pass(part):
        lanes = parts[part]
        for k in range(p.hi):
            to = turn(z, k + 1, p.hi)
            total = row_block(r.grad_w, to * p.lo + x, rows, lanes)[...].astype(F32)
            for t in range(1, p.lo):
                lo_copies[part, k, t].wait_recv()
                total = total + r.w_lo[k * (p.lo - 1) + t - 1, :, lanes].astype(F32)
            if k < p.hi - 1:
                r.w_hi_out[k, :, lanes] = total.astype(BF)
                hi_copies[part, k] = send(
                    r.w_hi_out.at[k, :, lanes],
                    r.w_hi.at[k, :, lanes],
                    (r.hi_s, r.hi_r),
                    part * (p.hi - 1) + k,
                    (b, to * p.lo + x),
                )
            else:
                r.out_w[:, lanes] = total

    def sum_finish(part):
        lanes = parts[part]
        total = r.out_w[:, lanes]
        for k in range(p.hi - 1):
            hi_copies[part, k].wait_recv()
            total = total + r.w_hi[k, :, lanes].astype(F32)
        r.out_w[:, lanes] = total

    def middle():
        experts_wide()
        attention_weight_grads(p, r, r.a, p.qkv, p.all_cols, True)
        sum_begin(1)

    def last():
        sum_pass(1)
        attention_weight_grads(p, r, r.a, 0, p.qkv, True)
        sum_begin(0)

    grad, gain_one, router = attention_backward(
        p, r, r.a, 0, r.x[...].astype(F32), grad_middle, lambda: None, middle, last
    )
    sum_pass(0)
    r.input_grad[...] = grad.astype(BF)
    small = r.out_small
    small[...] = jnp.zeros_like(small)
    small[0:1, :] = r.gain_one_before[...] + gain_one
    small[1:2, :] = r.gain_two_before[...] + gain_two
    small[2:3, :] = r.halt_before[...]
    small[8 : 8 + p.mixers, :] = r.mixer_before[...] + router
    small[8 + p.mixers :, :] = r.router_before[...] + r.grad_router[...]
    current = small[...]
    tiny = []
    sem = base = 0
    axes = (
        (2, c, lambda t: (2 * y + turn(c, t, 2), d)),
        (p.chips, y, lambda t: (2 * turn(y, t, p.chips) + c, d)),
        (p.lo, x, lambda t: (b, z * p.lo + turn(x, t, p.lo))),
        (p.hi, z, lambda t: (b, turn(z, t, p.hi) * p.lo + x)),
    )
    for size, index, peer in axes:
        r.all_small[base + index] = current
        at = r.all_small.at[base + index]
        copies = []
        for t in range(1, size):
            copies.append(send(at, at, (r.tiny_s, r.tiny_r), sem, peer(t)))
            sem += 1
        for copy in copies:
            copy.wait_recv()
        current = r.all_small[base]
        for k in range(1, size):
            current = current + r.all_small[base + k]
        base += size
        tiny += copies
    r.out_small[...] = current
    for k in range(p.local - 1):
        source = turn(e, -(k + 1), p.local)
        wide[k, 0].wait_recv()
        wide[k, 1].wait_recv()
        r.out_in[source] = r.in_far[k]
        r.out_back[source] = r.back_far[k]
    sum_finish(1)
    sum_finish(0)
    for copies in (there, back, near, wide, lo_copies, hi_copies, tiny):
        sent(copies)


def output_kernel(p, r):
    cols = p.cols
    r.result_out[...] = r.result[...]
    r.input_grad_out[...] = r.input_grad[...]
    r.in_out[...] = r.out_in[...].astype(F32)
    r.back_out[...] = r.out_back[...].astype(F32)
    for e in range(p.mixers):
        r.query_out[e] = r.out_w[:, e * cols : (e + 1) * cols]
        start = p.qkv + e * cols
        r.out_out[e] = r.out_w[:, start : start + cols]
    r.key_out[...] = r.out_w[:, p.mixers * cols : (p.mixers + 1) * cols]
    r.value_out[...] = r.out_w[:, (p.mixers + 1) * cols : p.qkv]
    r.gain_one_out[...] = r.small[0:1, :]
    r.gain_two_out[...] = r.small[1:2, :]
    r.halt_out[...] = r.small[2:3, :]
    r.mixer_out[...] = r.small[8 : 8 + p.mixers, :]
    r.router_out[...] = r.small[8 + p.mixers :, :]


SAVED = ("nt", "qs", "kt", "vt", "lse", "att", "mix", "gates")


def dma(name, size):
    sem = pltpu.SemaphoreType.DMA((max(1, size),))
    return {name + "_s": sem, name + "_r": sem}


def pack_sems(p, name):
    sizes = (p.chips - 1, p.chips - 1, p.chips, p.chips)
    return {f"{name}_{k}": pltpu.SemaphoreType.DMA((max(1, size),)) for k, size in enumerate(sizes)}


def sum_scratch(p):
    far = max(1, p.chips - 1)
    return {
        "part": pltpu.VMEM((p.chips, p.width, p.seq), BF),
        "near_in": pltpu.VMEM((p.chips, p.width, p.seq), BF),
        "far_out": pltpu.VMEM((far, p.width, p.seq), BF),
        "far_in": pltpu.VMEM((far, p.width, p.seq), BF),
    }


def saved_shapes(p):
    return {
        "nt": ((p.blk, p.width, p.seq), BF),
        "qs": ((p.blocks, p.cols, p.top * QROWS), BF),
        "kt": ((p.cols, p.length + MAXLEN), BF),
        "vt": ((p.cols, p.length + MAXLEN), BF),
        "lse": ((p.blocks, 8, p.top * QROWS), F32),
        "att": ((p.blocks, p.cols, p.top * QROWS), BF),
        "mix": ((p.mixers * p.cols, p.length), BF),
        "gates": ((p.blk, 8, p.seq), F32),
    }


def launch(body, name, number, ins, outs, scratch):
    def spec(vmem):
        return pl.BlockSpec(memory_space=pltpu.VMEM if vmem else pl.ANY)

    names = list(ins) + list(outs) + list(scratch)

    def kernel(*refs):
        r = SimpleNamespace(**dict(zip(names, refs, strict=True)))
        r.moved = 0
        r.a = SimpleNamespace(**{k[2:]: v for k, v in vars(r).items() if k.startswith("a_")})
        for key in ("gather", "sum", "back_gather", "back_sum", "picks"):
            sems = [getattr(r, f"{key}_{k}") for k in range(4) if hasattr(r, f"{key}_{k}")]
            setattr(r.a, key + "_sems", sems)
            setattr(r, key + "_sems", sems)
        body(r)

    results = pl.pallas_call(
        kernel,
        out_shape=tuple(jax.ShapeDtypeStruct(shape, dtype) for shape, dtype, _ in outs.values()),
        in_specs=[spec(vmem) for _, vmem in ins.values()],
        out_specs=tuple(spec(vmem) for _, _, vmem in outs.values()),
        scratch_shapes=list(scratch.values()),
        compiler_params=pltpu.CompilerParams(
            collective_id=number, has_side_effects=number is not None, vmem_limit_bytes=VMEM_BYTES
        ),
        name=name,
    )(*[array for array, _ in ins.values()])
    return SimpleNamespace(**dict(zip(outs, results, strict=True)))


def on_device(
    inputs,
    segments,
    attention_routes,
    expert_routes,
    gain_mixer,
    gain_expert,
    weight_query,
    weight_key,
    weight_value,
    weight_out,
    router_mixer,
    router_expert,
    weight_in,
    weight_back,
    halt_weight,
    cotangent,
):
    blk, dp = lax.axis_size("blk"), lax.axis_size("dp")
    seq, width = inputs.shape[1:]
    experts, local = router_expert.shape[1], weight_in.shape[0]
    slots_of = max(2, 3 * seq // experts)
    hi = 4
    p = Plan(
        blk=blk,
        dp=dp,
        lo=dp // hi,
        hi=hi,
        seq=seq,
        width=width,
        heads=HEADS // blk,
        mixers=weight_query.shape[0],
        top=attention_routes.shape[-1],
        experts=experts,
        local=local,
        group=blk // local,
        cap=-(-slots_of // 16) * 16,
        ff=weight_in.shape[2],
    )
    cols, length, top = p.cols, p.length, p.top
    share, in_rows, back_rows = weight_key.shape[0], weight_in.shape[1], weight_back.shape[1]

    gain_one = gain_mixer.reshape(1, width)
    gain_two = gain_expert.reshape(1, width)
    halt = halt_weight.reshape(1, width)
    router_row, router = router_mixer.T, router_expert.T

    slots_bf = pltpu.VMEM((p.slots, width), BF)
    saved = saved_shapes(p)
    attention_scratch = {
        "seg_cols": pltpu.VMEM((length + MAXLEN, 8), F32),
        "k_heads": pltpu.VMEM((p.heads, length + MAXLEN, cols), BF),
        "all_w": pltpu.VMEM((width, p.all_cols), BF),
        **{"a_" + k: pltpu.VMEM(*v) for k, v in saved.items()},
    }
    forward_scratch = {
        "w_t": pltpu.VMEM((p.qkv, width), BF),
        **pack_sems(p, "gather"),
        **pack_sems(p, "sum"),
        **sum_scratch(p),
    }
    backward_scratch = {
        "gt": pltpu.VMEM((blk, width, seq), BF),
        "v_heads": pltpu.VMEM((p.heads, length + MAXLEN, cols), BF),
        "means": pltpu.VMEM((p.blocks, 8, top * QROWS), F32),
        "dlog": pltpu.VMEM((blk, p.mixers, seq), F32),
        "dkt": pltpu.VMEM((cols, length + MAXLEN), F32),
        "dvt": pltpu.VMEM((cols, length + MAXLEN), F32),
        "dall": pltpu.VMEM((p.qkv, length), BF),
        "grad_w": pltpu.VMEM((width, p.all_cols), BF),
        **pack_sems(p, "back_gather"),
        **pack_sems(p, "back_sum"),
        **sum_scratch(p),
    }
    expert_scratch = {
        "router": pltpu.VMEM((LANES, width), BF),
        "all_in": pltpu.VMEM((width, p.ff), BF),
        "all_back": pltpu.VMEM((p.ff, width), BF),
    }
    expert_back_scratch = {
        "act": pltpu.VMEM((p.slots, p.ff), BF),
        "slope": pltpu.VMEM((p.slots, p.ff), BF),
        "coeff": pltpu.VMEM((p.slots, LANES), BF),
        "arrived_t": pltpu.VMEM((width, p.slots), BF),
        "u_out": slots_bf,
        "u_in": slots_bf,
        "gret_in": slots_bf,
        "grad_in": pltpu.VMEM((width, p.ff), BF),
        "grad_back": pltpu.VMEM((p.ff, width), BF),
        **dma("u", p.experts),
        **dma("gret", p.experts),
    }

    one = launch(
        functools.partial(forward_kernel, p),
        "forward",
        0,
        {
            "x": (inputs[0], True),
            "segments": (segments, True),
            "attention_routes": (jnp.swapaxes(attention_routes[:, 0], 1, 2), True),
            "expert_routes": (jnp.swapaxes(expert_routes[:, 0], 1, 2), True),
            "gain_one": (gain_one, True),
            "gain_two": (gain_two, True),
            "router_row": (router_row, True),
            "router_in": (router, True),
            "weight_query": (weight_query, True),
            "weight_key": (weight_key, True),
            "weight_value": (weight_value, True),
            "weight_out": (jnp.swapaxes(weight_out, 1, 2), True),
            "weight_in": (weight_in, False),
            "weight_back": (weight_back, False),
        },
        {
            "first": ((seq, width), F32, True),
            "middle": ((seq, width), F32, True),
            "arrived": ((p.slots, width), BF, True),
            "produced": ((p.slots, width), BF, True),
            "all_picks": ((blk, 16, seq), jnp.int32, True),
            "disp_out": ((2, p.slots, seq), BF, False),
            "comb_out": ((2, seq, p.slots), BF, False),
            "pair_end": ((2, p.slots, LANES), BF, False),
            "all_w_out": ((width, p.all_cols), BF, False),
            "all_in_out": ((width, p.ff), BF, False),
            "all_back_out": ((p.ff, width), BF, False),
            **{k + "_out": (*v, False) for k, v in saved.items()},
        },
        {
            **attention_scratch,
            **forward_scratch,
            **expert_scratch,
            "disp": pltpu.VMEM((2, p.slots, seq), BF),
            "comb": pltpu.VMEM((2, seq, p.slots), BF),
            "pair": pltpu.VMEM((2, p.slots, LANES), BF),
            "pair_out": pltpu.VMEM((experts, 8, LANES), F32),
            "pair_in": pltpu.VMEM((experts, 8, LANES), F32),
            "routes": pltpu.VMEM((16, seq), jnp.int32),
            "outgoing": slots_bf,
            "ret_out": slots_bf,
            "ret_in": slots_bf,
            **pack_sems(p, "picks"),
            **dma("hi", 4 * (p.hi - 1)),
            **dma("lo", 2 * p.hi * (p.lo - 1)),
            **dma("wide", 2 * (p.local - 1)),
            **dma("near", 2 * p.local * (p.group - 1)),
            **dma("pair", p.experts),
            **dma("go", p.experts),
            **dma("ret", p.experts),
            "moves": pltpu.SemaphoreType.DMA((16,)),
        },
    )
    two = launch(
        functools.partial(turn_kernel, p),
        "turn",
        1,
        {
            "first": (one.first, True),
            "cot": (cotangent[0], True),
            "halt": (halt, True),
            "segments": (segments, True),
            "all_picks": (one.all_picks, True),
            "gain_one": (gain_one, True),
            "gain_two": (gain_two, True),
            "router_row": (router_row, True),
            "router_in": (router, True),
            "disp_in": (one.disp_out, False),
            "comb_in": (one.comb_out, False),
            "pair_in": (one.pair_end, False),
            "all_w_in": (one.all_w_out, False),
            "all_in_in": (one.all_in_out, False),
            "all_back_in": (one.all_back_out, False),
        },
        {
            "result": ((seq, width), BF, True),
            "grad_first": ((seq, width), F32, True),
            "grad_halt": ((1, width), F32, True),
            "grad_gain_one": ((1, width), F32, True),
            "grad_gain_two": ((1, width), F32, True),
            "grad_mixer": ((p.mixers, width), F32, True),
            "grad_router": ((experts, width), F32, True),
            "grad_in_out": ((width, p.ff), BF, False),
            "grad_back_out": ((p.ff, width), BF, False),
            "grad_w_out": ((width, p.all_cols), BF, False),
        },
        {
            **attention_scratch,
            **forward_scratch,
            **backward_scratch,
            **expert_scratch,
            **expert_back_scratch,
            "wo": pltpu.VMEM((p.mixers * cols, width), BF),
            "disp": pltpu.VMEM((p.slots, seq), BF),
            "comb": pltpu.VMEM((seq, p.slots), BF),
            "pair": pltpu.VMEM((p.slots, LANES), BF),
            "middle": pltpu.VMEM((seq, width), F32),
            "outgoing": slots_bf,
            "arrived": slots_bf,
            "gret_out": slots_bf,
            "ret_in": slots_bf,
            **dma("go", p.experts),
            **dma("ret", p.experts),
            "moves": pltpu.SemaphoreType.DMA((16,)),
        },
    )
    near, far = p.local * (p.group - 1), max(1, p.local - 1)
    small_rows = 8 + p.mixers + experts
    three = launch(
        functools.partial(backward_kernel, p),
        "backward",
        2,
        {
            "x": (inputs[0], True),
            "grad_first": (two.grad_first, True),
            "middle": (one.middle, True),
            "segments": (segments, True),
            "all_picks": (one.all_picks, True),
            "gain_one": (gain_one, True),
            "gain_two": (gain_two, True),
            "router_row": (router_row, True),
            "router_in": (router, True),
            "halt_before": (two.grad_halt, True),
            "gain_one_before": (two.grad_gain_one, True),
            "gain_two_before": (two.grad_gain_two, True),
            "mixer_before": (two.grad_mixer, True),
            "router_before": (two.grad_router, True),
            "disp_in": (one.disp_out, False),
            "comb_in": (one.comb_out, False),
            "pair_in": (one.pair_end, False),
            "arrived_in": (one.arrived, False),
            "produced_in": (one.produced, False),
            "all_w_in": (one.all_w_out, False),
            "all_in_in": (one.all_in_out, False),
            "all_back_in": (one.all_back_out, False),
            "grad_in_in": (two.grad_in_out, False),
            "grad_back_in": (two.grad_back_out, False),
            "grad_w_in": (two.grad_w_out, False),
            **{k + "_in": (getattr(one, k + "_out"), False) for k in SAVED},
        },
        {
            "input_grad": ((seq, width), BF, True),
            "out_w": ((share, p.all_cols), F32, True),
            "out_in": ((local, in_rows, p.ff), BF, True),
            "out_back": ((local, back_rows, width), BF, True),
            "out_small": ((small_rows, width), F32, True),
        },
        {
            **attention_scratch,
            **backward_scratch,
            **expert_scratch,
            **expert_back_scratch,
            "wo": pltpu.VMEM((p.mixers * cols, width), BF),
            "disp": pltpu.VMEM((p.slots, seq), BF),
            "comb": pltpu.VMEM((seq, p.slots), BF),
            "pair": pltpu.VMEM((p.slots, LANES), BF),
            "arrived": slots_bf,
            "produced": slots_bf,
            "in_near": pltpu.VMEM((near, in_rows, p.ff), BF),
            "back_near": pltpu.VMEM((near, back_rows, width), BF),
            "in_far_out": pltpu.VMEM((far, in_rows, p.ff), BF),
            "in_far": pltpu.VMEM((far, in_rows, p.ff), BF),
            "back_far_out": pltpu.VMEM((far, back_rows, width), BF),
            "back_far": pltpu.VMEM((far, back_rows, width), BF),
            "w_lo": pltpu.VMEM((hi * (p.lo - 1), share, p.all_cols), BF),
            "w_hi_out": pltpu.VMEM((hi - 1, share, p.all_cols), BF),
            "w_hi": pltpu.VMEM((hi - 1, share, p.all_cols), BF),
            "grad_router": pltpu.VMEM((experts, width), F32),
            "all_small": pltpu.VMEM((2 + p.chips + p.lo + hi, small_rows, width), F32),
            **dma("near", 2 * near),
            **dma("wide", 2 * (local - 1)),
            **dma("lo", 2 * hi * (p.lo - 1)),
            **dma("hi", 2 * (hi - 1)),
            **dma("tiny", 2 + p.chips + p.lo + hi),
            "moves": pltpu.SemaphoreType.DMA((24,)),
        },
    )
    four = launch(
        functools.partial(output_kernel, p),
        "outputs",
        None,
        {
            "result": (two.result, True),
            "input_grad": (three.input_grad, True),
            "out_w": (three.out_w, True),
            "out_in": (three.out_in, True),
            "out_back": (three.out_back, True),
            "small": (three.out_small, True),
        },
        {
            "result_out": ((seq, width), BF, True),
            "input_grad_out": ((seq, width), BF, True),
            "query_out": (weight_query.shape, F32, True),
            "key_out": (weight_key.shape, F32, True),
            "value_out": (weight_value.shape, F32, True),
            "out_out": ((p.mixers, share, cols), F32, True),
            "in_out": (weight_in.shape, F32, True),
            "back_out": (weight_back.shape, F32, True),
            "gain_one_out": ((1, width), F32, True),
            "gain_two_out": ((1, width), F32, True),
            "halt_out": ((1, width), F32, True),
            "mixer_out": ((p.mixers, width), F32, True),
            "router_out": ((experts, width), F32, True),
        },
        {},
    )
    return (
        four.result_out[None],
        four.input_grad_out[None],
        four.gain_one_out.reshape(width),
        four.gain_two_out.reshape(width),
        four.query_out,
        four.key_out,
        four.value_out,
        jnp.swapaxes(four.out_out, 1, 2),
        four.mixer_out.T,
        four.router_out.T,
        four.in_out,
        four.back_out,
        four.halt_out.reshape(width),
    )


def solution(mesh):
    return jax.shard_map(
        on_device,
        mesh=mesh,
        in_specs=(
            P("dp", "blk", None),
            P("dp", None),
            P(None, "dp", "blk", None),
            P(None, "dp", "blk", None),
            P(),
            P(),
            P(None, "dp", "blk"),
            P("dp", "blk"),
            P("dp", "blk"),
            P(None, "blk", "dp"),
            P(),
            P(),
            P("dp", "blk", None),
            P("dp", "blk", None),
            P(),
            P("dp", "blk", None),
        ),
        out_specs=(
            P("dp", "blk", None),
            P("dp", "blk", None),
            P(),
            P(),
            P(None, "dp", "blk"),
            P("dp", "blk"),
            P("dp", "blk"),
            P(None, "blk", "dp"),
            P(),
            P(),
            P("dp", "blk", None),
            P("dp", "blk", None),
            P(),
        ),
        check_vma=False,
    )
```

```python
import functools
from types import SimpleNamespace
from typing import NamedTuple

import jax
import jax.numpy as jnp
from jax import lax
from jax.experimental import pallas as pl
from jax.experimental.pallas import tpu as pltpu
from jax.sharding import PartitionSpec as P

HEADS = 8
HD = 64
MAXLEN = 256
QROWS = 128
WINDOW = MAXLEN + QROWS
LANES = 128
EPSILON = 1e-06
MASKED_SCORE = -1e30
MESH = pl.DeviceIdType.MESH
BF = jnp.bfloat16
F32 = jnp.float32
VMEM_BYTES = 61 * 2**20


class Plan(NamedTuple):
    blk: int
    dp: int
    lo: int
    hi: int
    seq: int
    width: int
    heads: int
    mixers: int
    top: int
    experts: int
    local: int
    group: int
    cap: int
    ff: int

    @property
    def length(self):
        return self.blk * self.seq

    @property
    def cols(self):
        return self.heads * HD

    @property
    def qkv(self):
        return (self.mixers + 2) * self.cols

    @property
    def all_cols(self):
        return (2 * self.mixers + 2) * self.cols

    @property
    def blocks(self):
        return self.length // QROWS

    @property
    def slots(self):
        return self.experts * self.cap

    @property
    def head_cols(self):
        return (self.mixers + 2) * HD

    @property
    def parts(self):
        heads = [slice(h * self.head_cols, (h + 1) * self.head_cols) for h in range(self.heads)]
        return (*heads, slice(self.qkv, self.all_cols))

    @property
    def tile(self):
        return 512 if self.slots <= 768 else 256

    @property
    def chips(self):
        return self.blk // 2


def mm(a, b):
    return lax.dot_general(a, b, (((1,), (0,)), ((), ())), preferred_element_type=F32)


def mm_nt(a, b):
    return lax.dot_general(a, b, (((1,), (1,)), ((), ())), preferred_element_type=F32)


def place():
    return lax.axis_index("blk"), lax.axis_index("dp")


def turn(index, by, size):
    return lax.rem(index + (by % size), size)


def greet(peers):
    barrier = pltpu.get_barrier_semaphore()
    for peer in peers:
        pl.semaphore_signal(barrier, inc=1, device_id=peer, device_id_type=MESH)


def answered(peers):
    pl.semaphore_wait(pltpu.get_barrier_semaphore(), len(peers))


def send(src, dst, sems, slot, peer):
    copy = pltpu.make_async_remote_copy(
        src_ref=src,
        dst_ref=dst,
        send_sem=sems[0].at[slot],
        recv_sem=sems[1].at[slot],
        device_id=peer,
        device_id_type=MESH,
    )
    copy.start()
    return copy


def aligned(value, by):
    return pl.multiple_of(value, by)


def pack_peers(p):
    b, d = place()
    y, c = b // 2, lax.rem(b, 2)
    peers = [(2 * y + 1 - c, d)]
    return peers + [(2 * turn(y, s, p.chips) + c, d) for s in range(1, p.chips)]


def slot_peer(p, s):
    b, d = place()
    e, g = b // p.group, lax.rem(b, p.group)
    return (turn(e, s // p.dp, p.local) * p.group + g, turn(d, s % p.dp, p.dp))


def slot_peers(p):
    return [slot_peer(p, s) for s in range(1, p.experts)]


def slot_source(p, s):
    b, d = place()
    e, g = b // p.group, lax.rem(b, p.group)
    return (turn(e, -(s // p.dp), p.local) * p.group + g, turn(d, -(s % p.dp), p.dp))


def dp_peers(p):
    b, d = place()
    z, x = d // p.lo, lax.rem(d, p.lo)
    peers = [(b, turn(z, s, p.hi) * p.lo + x) for s in range(1, p.hi)]
    return peers + [(b, z * p.lo + turn(x, t, p.lo)) for t in range(1, p.lo)]


def expert_peers(p):
    b, d = place()
    e, g = b // p.group, lax.rem(b, p.group)
    peers = [(turn(e, s, p.local) * p.group + g, d) for s in range(1, p.local)]
    return peers + [(e * p.group + turn(g, t, p.group), d) for t in range(1, p.group)]


def link(src, dst, sems, slot, peer):
    return pltpu.make_async_remote_copy(
        src_ref=src,
        dst_ref=dst,
        send_sem=sems[0].at[slot],
        recv_sem=sems[1].at[slot],
        device_id=peer,
        device_id_type=MESH,
    )


class PackGather:
    def __init__(self, p, buf, sems):
        self.p, self.buf, self.far, self.near = p, buf, sems[0:2], sems[2:4]
        self.done_near = self.done_far = False

    def begin(self):
        p = self.p
        b, d = place()
        y, c = b // 2, lax.rem(b, 2)
        own = self.buf.at[b]
        self.first = [
            send(own, own, self.far, s - 1, (2 * turn(y, s, p.chips) + c, d))
            for s in range(1, p.chips)
        ]
        self.second = [send(own, own, self.near, 0, (2 * y + 1 - c, d))]

    def finish_near(self):
        if not self.done_near:
            self.second[0].wait_recv()
        self.done_near = True

    def finish_far(self):
        if self.done_far:
            return
        self.done_far = True
        p = self.p
        b, d = place()
        y, c = b // 2, lax.rem(b, 2)
        for s in range(1, p.chips):
            self.first[s - 1].wait_recv()
            block = self.buf.at[2 * turn(y, -s, p.chips) + c]
            self.second.append(send(block, block, self.near, s, (2 * y + 1 - c, d)))
        self.finish_near()
        for copy in self.second[1:]:
            copy.wait_recv()

    def end(self):
        for copy in self.first + self.second:
            copy.wait_send()


class PackSum:
    def __init__(self, p, bufs, sems):
        self.p, self.bufs = p, bufs
        self.far, self.near = sems[0:2], sems[2:4]
        self.first, self.second = {}, []

    def give(self, s, term):
        p, r = self.p, self.bufs
        b, d = place()
        y, c = b // 2, lax.rem(b, 2)
        r.part[s] = term.astype(BF)
        self.first[s] = send(r.part.at[s], r.near_in.at[s], self.near, s, (2 * y + 1 - c, d))

    def pass_on(self, s, term):
        p, r = self.p, self.bufs
        b, d = place()
        y, c = b // 2, lax.rem(b, 2)
        self.first[s].wait_recv()
        r.far_out[s - 1] = (term + r.near_in[s].astype(F32)).astype(BF)
        self.second.append(
            send(r.far_out.at[s - 1], r.far_in.at[s - 1], self.far, s - 1, (2 * turn(y, s, p.chips) + c, d))
        )

    def total(self, term):
        r = self.bufs
        self.first[0].wait_recv()
        term = term + r.near_in[0].astype(F32)
        for k, copy in enumerate(self.second):
            copy.wait_recv()
            term = term + r.far_in[k].astype(F32)
        for copy in list(self.first.values()) + self.second:
            copy.wait_send()
        return term


def slot_send(p, src, dst, sems, s, peer):
    rows = pl.ds(s * p.cap, p.cap)
    return send(src.at[rows], dst.at[rows], sems, s, peer)


def slot_sends(p, src, dst, sems, peer):
    dst[0 : p.cap, :] = src[0 : p.cap, :]
    return {s: slot_send(p, src, dst, sems, s, peer(p, s)) for s in range(1, p.experts)}


def receive(copies, sources):
    for s in sources:
        if s in copies:
            copies[s].wait_recv()


def sent(copies):
    for copy in copies.values() if isinstance(copies, dict) else copies:
        copy.wait_send()


def move(r, src, dst):
    copy = pltpu.make_async_copy(src, dst, r.moves.at[r.moved])
    r.moved += 1
    copy.start()
    return copy


def moves(r, pairs):
    return [move(r, src, dst) for src, dst in pairs]


def arrive(copies):
    for copy in copies:
        copy.wait()
    copies.clear()


def norm_parts(state):
    inverse = lax.rsqrt(jnp.mean(state * state, axis=-1, keepdims=True) + EPSILON)
    return inverse, state * inverse


def norm_back(state, gain, grad):
    inverse, unit = norm_parts(state)
    scaled = grad * gain
    back = inverse * scaled - state * (inverse * inverse * inverse) * jnp.mean(
        scaled * state, axis=-1, keepdims=True
    )
    return back, jnp.sum(grad * unit, axis=0, keepdims=True)


def segment_columns(p, segments, seg_cols):
    seg_cols[0:MAXLEN, :] = jnp.full((MAXLEN, 8), -1.0, F32)
    for start in range(0, p.length, QROWS):
        row = segments[:, start : start + QROWS].astype(F32)
        seg_cols[MAXLEN + start : MAXLEN + start + QROWS, :] = jnp.broadcast_to(row, (8, QROWS)).T


def attention_mask(r, start):
    keys = r.seg_cols[pl.ds(start, WINDOW), 0:1]
    queries = r.segments[:, pl.ds(start, QROWS)].astype(F32)
    key_at = lax.broadcasted_iota(jnp.int32, (WINDOW, QROWS), 0) - MAXLEN
    query_at = lax.broadcasted_iota(jnp.int32, (WINDOW, QROWS), 1)
    return jnp.where((key_at <= query_at) & (keys == queries), 0.0, MASKED_SCORE)


def pick_rows(p, routes, terms):
    picked = []
    for j in range(p.top):
        row = routes[j : j + 1, :]
        total = None
        for e in range(p.mixers):
            term = jnp.where(row == e, terms(e), 0.0)
            total = term if total is None else total + term
        picked.append(total)
    return picked


def spread_rows(p, routes, values, e):
    total = None
    for j in range(p.top):
        term = jnp.where(routes[j : j + 1, :] == e, values[j], 0.0)
        total = term if total is None else total + term
    return total


def pick_table(p, r, step, bb):
    return r.all_picks[bb, 8 * step : 8 * step + p.top, :]


def transposed(dst, src, first, start, stop, tile):
    for at in range(0, stop - start, tile):
        piece = src[:, start + at : start + at + tile]
        dst[first + at : first + at + tile, :] = piece.astype(F32).T.astype(BF)


def project_rows(p, r, head):
    start, stop = head * p.head_cols, (head + 1) * p.head_cols
    transposed(r.w_t, r.all_w, start, start, stop, LANES)


def project_gates(p, r, a, step, bb):
    table = pick_table(p, r, step, bb)
    logits = mm(r.router_row[...], a.nt[bb])
    chosen = pick_rows(p, table, lambda e: logits[e : e + 1, :])
    peak = functools.reduce(jnp.maximum, chosen)
    chosen = [jnp.exp(row - peak) for row in chosen]
    scale = 1.0 / sum(chosen)
    for j in range(p.top):
        a.gates[bb, j : j + 1, :] = chosen[j] * scale


def project(p, r, a, step, bb, head):
    sub = p.seq // QROWS
    if head == 0:
        project_gates(p, r, a, step, bb)
    table = pick_table(p, r, step, bb)
    values = mm(r.w_t[head * p.head_cols : (head + 1) * p.head_cols, :], a.nt[bb])
    for k in range(sub):
        lanes = slice(k * QROWS, (k + 1) * QROWS)
        queries = pick_rows(p, table[:, lanes], lambda e: values[e * HD : (e + 1) * HD, lanes])
        for j in range(p.top):
            a.qs[head, bb * sub + k, :, j * QROWS : (j + 1) * QROWS] = (queries[j] * (HD**-0.5)).astype(BF)
    at = pl.ds(aligned(MAXLEN + bb * p.seq, QROWS), p.seq)
    keys = values[p.mixers * HD : (p.mixers + 1) * HD, :]
    a.kt[head, :, at] = keys.astype(BF)
    a.vt[head, :, at] = values[(p.mixers + 1) * HD :, :].astype(BF)
    r.k_rows[head, at, :] = keys.T.astype(BF)


def attend(p, r, a, step, bb, head):
    sub = p.seq // QROWS
    for k in range(sub):
        i = bb * sub + k
        start = aligned(i * QROWS, QROWS)
        keys = pl.ds(start, WINDOW)
        bias = attention_mask(r, start)
        bias = jnp.concatenate([bias] * p.top, axis=1)
        scores = mm(r.k_rows[head, keys, :], a.qs[head, i]) + bias
        peak = jnp.max(scores, axis=0, keepdims=True)
        scores = jnp.exp(scores - peak)
        total = jnp.sum(scores, axis=0, keepdims=True)
        a.lse[i, head : head + 1, :] = peak + jnp.log(total)
        probs = (scores * (1.0 / total)).astype(BF)
        past = mm(a.vt[head, :, keys], probs)
        a.att[head, i] = past.astype(BF)
        at = pl.ds(k * QROWS, QROWS)
        table = r.all_picks[bb, 8 * step : 8 * step + p.top, at]
        weights = a.gates[bb, 0 : p.top, at]
        values = [past[:, j * QROWS : (j + 1) * QROWS] * weights[j : j + 1, :] for j in range(p.top)]
        for e in range(p.mixers):
            rows = slice(e * p.cols + head * HD, e * p.cols + (head + 1) * HD)
            a.mix[rows, pl.ds(start, QROWS)] = spread_rows(p, table, values, e).astype(BF)


def each_block(work, first, count):
    @pl.loop(0, count)
    def _(k):
        work(first + k)


def attention_forward(p, r, a, step, state, before, ready, tick, out_ready, after):
    b, _ = place()
    y, c = b // 2, lax.rem(b, 2)
    a.nt[b] = (norm_parts(state)[1] * r.gain_one[...].astype(F32)).T.astype(BF)
    gather = PackGather(p, a.nt, a.gather_sems)
    gather.begin()
    r.k_rows[:, 0:MAXLEN, :] = jnp.zeros((p.heads, MAXLEN, HD), BF)
    a.kt[:, :, 0:MAXLEN] = jnp.zeros((p.heads, HD, MAXLEN), BF)
    a.vt[:, :, 0:MAXLEN] = jnp.zeros((p.heads, HD, MAXLEN), BF)
    before(gather)
    shares = PackSum(p, r, a.sum_sems)

    def branch(bb):
        return mm(r.all_w[:, p.qkv :], a.mix[:, pl.ds(aligned(bb * p.seq, p.seq), p.seq)])

    for head in range(p.heads):
        if head == 0:
            project(p, r, a, step, b, head)
            gather.finish_near()
            project(p, r, a, step, 2 * y + 1 - c, head)
            tick()
            attend(p, r, a, step, 2 * y + 1, head)
            gather.finish_far()
            tick()
            for s in range(1, p.chips):
                each_block(lambda bb: project(p, r, a, step, bb, 0), 2 * turn(y, s, p.chips), 2)
            tick()
        else:
            ready(head)
            each_block(lambda bb: project(p, r, a, step, bb, head), 0, p.blk)
            attend(p, r, a, step, 2 * y + 1, head)
            tick()
        for s in range(1, p.chips):
            yy = turn(y, s, p.chips)
            attend(p, r, a, step, 2 * yy + 1 - c, head)
            tick()
            if head == p.heads - 1:
                if s == 1:
                    out_ready()
                shares.give(s, branch(2 * yy + 1 - c))
            attend(p, r, a, step, 2 * yy + c, head)
            tick()
            if head == p.heads - 1:
                shares.pass_on(s, branch(2 * yy + c))
        if head == p.heads - 1:
            after()
        attend(p, r, a, step, 2 * y, head)
        tick()
    shares.give(0, branch(2 * y + 1 - c))
    total = shares.total(branch(b))
    gather.end()
    return total


def attention_grads(p, r, a, step, bb):
    sub = p.seq // QROWS
    table = pick_table(p, r, step, bb)
    weights = a.gates[bb, 0 : p.top, :]
    values = mm(r.wo[...], r.gt[bb])
    for k in range(sub):
        lanes = slice(k * QROWS, (k + 1) * QROWS)
        here = table[:, lanes]
        grads = [None] * p.top
        for head in range(p.heads):
            picked = pick_rows(
                p, here, lambda e: values[e * p.cols + head * HD : e * p.cols + (head + 1) * HD, lanes]
            )
            for j in range(p.top):
                slot = slice(j * QROWS, (j + 1) * QROWS)
                past = a.att[head, bb * sub + k, :, slot].astype(F32)
                dot = jnp.sum(picked[j] * past, axis=0, keepdims=True)
                grads[j] = dot if head == 0 else grads[j] + dot
                gate = weights[j : j + 1, lanes]
                r.means[bb * sub + k, head : head + 1, slot] = dot * gate
                a.att[head, bb * sub + k, :, slot] = (picked[j] * gate).astype(BF)
        mean = sum(weights[j : j + 1, lanes] * grads[j] for j in range(p.top))
        back = [weights[j : j + 1, lanes] * (grads[j] - mean) for j in range(p.top)]
        for e in range(p.mixers):
            r.dlog[bb, e : e + 1, lanes] = spread_rows(p, here, back, e)


def probs_at(p, i, head):
    across = p.ff // (p.top * QROWS)
    each = p.slots // WINDOW * across
    unit = i * p.heads + head
    rows = aligned(lax.rem(unit, each) // across * WINDOW, QROWS)
    lanes = aligned(lax.rem(unit, across) * (p.top * QROWS), QROWS)
    return unit // each, pl.ds(rows, WINDOW), pl.ds(lanes, p.top * QROWS)


def attention_probs(p, r, a):
    @pl.loop(0, p.blocks)
    def _(i):
        start = aligned(i * QROWS, QROWS)
        bias = attention_mask(r, start)
        bias = jnp.concatenate([bias] * p.top, axis=1)
        for head in range(p.heads):
            scores = mm(r.k_rows[head, pl.ds(start, WINDOW), :], a.qs[head, i]) + bias
            plane, rows, lanes = probs_at(p, i, head)
            r.keep[plane, rows, lanes] = jnp.exp(scores - a.lse[i, head : head + 1, :]).astype(BF)


def attention_rows(p, r, a, keys):
    @pl.loop(0, (p.length + MAXLEN) // QROWS)
    def _(k):
        at = pl.ds(aligned(k * QROWS, QROWS), QROWS)
        for head in range(p.heads):
            r.v_rows[head, at, :] = a.vt[head, :, at].astype(F32).T.astype(BF)
            if keys:
                r.k_rows[head, at, :] = a.kt[head, :, at].astype(F32).T.astype(BF)


def attend_back(p, r, a, step, bb, head):
    sub = p.seq // QROWS
    for k in range(sub):
        i = bb * sub + k
        start = aligned(i * QROWS, QROWS)
        keys = pl.ds(start, WINDOW)
        plane, rows, lanes = probs_at(p, i, head)
        probs = r.keep[plane, rows, lanes]
        grads = a.att[head, i]
        mean = r.means[i, head : head + 1, :]
        dscores = (probs.astype(F32) * (mm(r.v_rows[head, keys, :], grads) - mean)).astype(BF)
        r.dvt[head, :, keys] += mm_nt(grads, probs)
        r.dkt[head, :, keys] += mm_nt(a.qs[head, i], dscores)
        merged = mm(a.kt[head, :, keys], dscores) * (HD**-0.5)
        at = pl.ds(k * QROWS, QROWS)
        table = r.all_picks[bb, 8 * step : 8 * step + p.top, at]
        values = [merged[:, j * QROWS : (j + 1) * QROWS] for j in range(p.top)]
        for e in range(p.mixers):
            first = head * p.head_cols + e * HD
            r.dall[first : first + HD, pl.ds(start, QROWS)] = spread_rows(p, table, values, e).astype(BF)


def attention_backward(p, r, a, step, state, grad, before, middle, head_done):
    b, _ = place()
    y, c = b // 2, lax.rem(b, 2)
    r.gt[b] = grad.T.astype(BF)
    gather = PackGather(p, r.gt, a.back_gather_sems)
    gather.begin()
    r.dkt[...] = jnp.zeros_like(r.dkt)
    r.dvt[...] = jnp.zeros_like(r.dvt)
    before()
    router_col = r.router_row[...].astype(F32).T.astype(BF)

    def key_value_grads(lanes, past):
        for head in range(p.heads):
            first = head * p.head_cols + p.mixers * HD
            r.dall[first : first + HD, lanes] = r.dkt[head, :, past].astype(BF)
            r.dall[first + HD : first + 2 * HD, lanes] = r.dvt[head, :, past].astype(BF)

    def branch(bb):
        lanes = pl.ds(aligned(bb * p.seq, p.seq), p.seq)
        key_value_grads(lanes, pl.ds(aligned(bb * p.seq + MAXLEN, QROWS), p.seq))
        return mm(r.all_w[:, : p.qkv], r.dall[:, lanes]) + mm(router_col, r.dlog[bb].astype(BF))

    shares = PackSum(p, r, a.back_sum_sems)
    for head in range(p.heads):
        if head == 0:
            attention_grads(p, r, a, step, b)
            gather.finish_near()
            attention_grads(p, r, a, step, 2 * y + 1 - c)
            attend_back(p, r, a, step, 2 * y, head)
            gather.finish_far()
            for s in range(1, p.chips):
                each_block(lambda bb: attention_grads(p, r, a, step, bb), 2 * turn(y, s, p.chips), 2)
            middle()
        else:
            attend_back(p, r, a, step, 2 * y, head)
        for s in range(1, p.chips):
            each_block(lambda bb: attend_back(p, r, a, step, bb, head), 2 * turn(y, s, p.chips), 2)
        if head == p.heads - 1:
            for s in range(1, p.chips):
                yy = turn(y, s, p.chips)
                shares.give(s, branch(2 * yy + 1 - c))
                shares.pass_on(s, branch(2 * yy + c))
        attend_back(p, r, a, step, 2 * y + 1, head)
        if head < p.heads - 1:
            key_value_grads(slice(0, p.length), slice(MAXLEN, MAXLEN + p.length))
            head_done(head)
    shares.give(0, branch(2 * y + 1 - c))
    own = branch(b)
    head_done(p.heads - 1)
    router = sum(mm_nt(r.dlog[bb].astype(BF), a.nt[bb]) for bb in range(p.blk))
    grad_n = shares.total(own).T
    gather.end()
    back, gain = norm_back(state, r.gain_one[...].astype(F32), grad_n)
    return grad + back, gain, router


def attention_weight_grads(p, r, a, start, stop, add):
    for first in range(start, stop, 2 * LANES):
        tile = min(2 * LANES, stop - first)
        total = None
        for bb in range(p.blk):
            lanes = slice(bb * p.seq, (bb + 1) * p.seq)
            if first < p.qkv:
                term = mm_nt(a.nt[bb], r.dall[first : first + tile, lanes])
            else:
                term = mm_nt(r.gt[bb], a.mix[first - p.qkv : first - p.qkv + tile, lanes])
            total = term if total is None else total + term
        at = slice(first, first + tile)
        r.grad_w[:, at] = (r.grad_w[:, at].astype(F32) + total if add else total).astype(BF)


def own_lane(p):
    b, d = place()
    mine = d * p.local + b // p.group
    return jnp.where(lax.broadcasted_iota(jnp.int32, (1, LANES), 1) == mine, 1.0, 0.0)


def slot_gates(p, r, rows, pair):
    own = own_lane(p)
    logits = mm_nt(rows, r.router[...])
    return 1.0 / (1.0 + jnp.exp(jnp.sum(logits * (pair - 2.0 * own), axis=-1, keepdims=True)))


def gelu_both(inner):
    half = 0.5 * (1.0 + lax.erf(inner * 0.7071067811865476))
    slope = half + inner * jnp.exp(-0.5 * inner * inner) * 0.3989422804014327
    return inner * half, slope


def fill_router(p, r):
    r.router[...] = jnp.zeros_like(r.router)
    r.router[0 : p.experts, :] = r.router_in[...]


def slot_groups(p):
    per = max(1, p.experts // 4)
    return [(pl.ds(first * p.cap, per * p.cap), range(first, first + per)) for first in range(0, p.experts, per)]


def expert_output(p, r, rows, at, keep):
    total = None
    for start in range(0, p.ff, p.tile):
        lanes = slice(start, start + p.tile)
        inner = mm(rows, r.all_in[:, lanes])
        if keep:
            act, slope = gelu_both(inner)
            act = act.astype(BF)
            r.keep[0, at, lanes] = act
            r.keep[1, at, lanes] = slope.astype(BF)
        else:
            act = (inner * (0.5 * (1.0 + lax.erf(inner * 0.7071067811865476)))).astype(BF)
        term = mm(act, r.all_back[lanes, :])
        total = term if total is None else total + term
    return total


def expert_keep(p, r, rows, at):
    for start in range(0, p.ff, p.tile):
        lanes = slice(start, start + p.tile)
        act, slope = gelu_both(mm(rows, r.all_in[:, lanes]))
        r.keep[0, at, lanes] = act.astype(BF)
        r.keep[1, at, lanes] = slope.astype(BF)


def expert_input_grad(p, r, at, u, rows, out, pair, dst):
    gate = slot_gates(p, r, rows, pair)
    grads = (u * gate).astype(BF)
    r.u_in[at, :] = grads
    coeff = gate * (1.0 - gate) * jnp.sum(u * out, axis=-1, keepdims=True) * (2.0 * own_lane(p) - pair)
    coeff = coeff.astype(BF)
    r.coeff[at, :] = coeff
    dst[at, :] = mm(coeff, r.router[...]).astype(BF)
    total = None
    for start in range(0, p.ff, p.tile):
        lanes = slice(start, start + p.tile)
        inner = (mm_nt(grads, r.all_back[lanes, :]) * r.keep[1, at, lanes].astype(F32)).astype(BF)
        r.keep[1, at, lanes] = inner
        term = mm_nt(inner, r.all_in[:, lanes])
        total = term if total is None else total + term
    dst[at, :] = (total + dst[at, :].astype(F32)).astype(BF)


def expert_weight_grads(p, r, arrived, add):
    r.arrived_t[...] = arrived[...].astype(F32).T.astype(BF)
    for start in range(0, p.ff, p.tile // 2):
        lanes = slice(start, start + p.tile // 2)
        term = mm(r.keep[0, :, lanes].astype(F32).T.astype(BF), r.u_in[...])
        r.grad_back[lanes, :] = (r.grad_back[lanes, :].astype(F32) + term if add else term).astype(BF)
        term = mm(r.arrived_t[...], r.keep[1, :, lanes])
        r.grad_in[:, lanes] = (r.grad_in[:, lanes].astype(F32) + term if add else term).astype(BF)
    return mm(r.coeff[...].astype(F32).T.astype(BF)[0 : p.experts], arrived[...])


def slot_tables(p, r):
    b, d = place()
    e = b // p.group
    place_in = lax.broadcasted_iota(jnp.int32, (p.experts, 1), 0)
    ids = lax.rem(d + lax.rem(place_in, p.dp), p.dp) * p.local + lax.rem(e + place_in // p.dp, p.local)
    earlier = (
        lax.broadcasted_iota(jnp.int32, (p.seq, p.seq), 0) < lax.broadcasted_iota(jnp.int32, (p.seq, p.seq), 1)
    ).astype(BF)
    slot_ids = lax.broadcasted_iota(jnp.int32, (p.cap, p.seq), 0).astype(F32)
    r.pair_out[...] = jnp.zeros_like(r.pair_out)
    for step in range(2):
        one = r.routes[8 * step + p.top : 8 * step + p.top + 1, :]
        two = r.routes[8 * step + p.top + 1 : 8 * step + p.top + 2, :]
        member = jnp.where((one == ids) | (two == ids), 1.0, 0.0)
        rank = jnp.where(member > 0.5, mm(member.astype(BF), earlier), -1.0)
        both = jnp.broadcast_to((one + two).astype(F32), (8, p.seq)).astype(BF)
        for s in range(p.experts):
            table = jnp.where(rank[s : s + 1, :] == slot_ids, 1.0, 0.0).astype(BF)
            r.disp[step, pl.ds(s * p.cap, p.cap), :] = table
            r.pair_out[s, step : step + 1, 0 : p.cap] = mm_nt(both, table)[0:1]
        r.comb[step] = r.disp[step].astype(F32).T.astype(BF)
    r.pair_in[0] = r.pair_out[0]
    return [
        send(r.pair_out.at[s], r.pair_in.at[s], (r.pair_s, r.pair_r), s, slot_peer(p, s)) for s in range(1, p.experts)
    ]


def slot_pairs(p, r):
    b, d = place()
    mine = (d * p.local + b // p.group).astype(F32)
    lanes = lax.broadcasted_iota(jnp.int32, (p.cap, LANES), 1).astype(F32)
    for step in range(2):
        totals = r.pair_in[:, step, :].T
        for s in range(p.experts):
            other = totals[0 : p.cap, s : s + 1] - mine
            both = jnp.where(lanes == mine, 1.0, 0.0) + jnp.where(lanes == other, 1.0, 0.0)
            r.pair[step, pl.ds(s * p.cap, p.cap), :] = both.astype(BF)


def forward_kernel(p, r):
    b, d = place()
    z, x = d // p.lo, lax.rem(d, p.lo)
    e, g = b // p.group, lax.rem(b, p.group)
    own_rows = r.weight_key.shape[0]
    in_rows, back_rows = r.weight_in.shape[1], r.weight_back.shape[1]

    def w_at(index, part):
        return r.all_w.at[pl.ds(aligned(index * own_rows, own_rows), own_rows), p.parts[part]]

    def in_at(index):
        return r.all_in.at[pl.ds(aligned(index * in_rows, in_rows), in_rows)]

    def back_at(index):
        return r.all_back.at[pl.ds(aligned(index * back_rows, back_rows), back_rows)]

    peers = pack_peers(p) + slot_peers(p) + dp_peers(p) + expert_peers(p)
    greet(peers)
    own = pl.ds(aligned(d * own_rows, own_rows), own_rows)
    for head in range(p.heads):
        mine = slice(head * HD, (head + 1) * HD)
        shares = [r.weight_query[k, :, mine] for k in range(p.mixers)]
        shares += [r.weight_key[:, mine], r.weight_value[:, mine]]
        r.all_w[own, p.parts[head]] = jnp.concatenate(shares, axis=1)
    for k in range(p.mixers):
        r.all_w[own, p.qkv + k * p.cols : p.qkv + (k + 1) * p.cols] = r.weight_out[k]
    fill_router(p, r)
    segment_columns(p, r.segments, r.seg_cols)
    answered(peers)
    last = p.hi - 1

    def hop(part, k, up):
        rows = w_at((z - k if up else z + k) * p.lo + x, part)
        slot = (2 * part + (0 if up else 1)) * last + k
        return link(rows, rows, (r.hi_s, r.hi_r), slot, (b, (z + 1 if up else z - 1) * p.lo + x))

    def arrival(part, k, up):
        rows = w_at((z - 1 - k if up else z + 1 + k) * p.lo + x, part)
        return link(rows, rows, (r.hi_s, r.hi_r), (2 * part + (0 if up else 1)) * last + k, (b, d))

    def cross(part, source, t):
        rows = w_at(source * p.lo + x, part)
        slot = (part * p.hi + source) * (p.lo - 1) + t - 1
        return link(rows, rows, (r.lo_s, r.lo_r), slot, (b, z * p.lo + turn(x, t, p.lo)))

    def goes(k, up):
        return (z >= k) & (z < last) if up else (z + k <= last) & (z > 0)

    def comes(k, up):
        return z >= k + 1 if up else z + k + 1 <= last

    def w_begin(part):
        for up in (True, False):
            pl.when(goes(0, up))(lambda: hop(part, 0, up).start())
        for t in range(1, p.lo):
            cross(part, z, t).start()

    def w_pass(part, k):
        for up in (True, False):

            @pl.when(comes(k, up))
            def _():
                arrival(part, k, up).wait_recv()
                if k + 1 < last:
                    pl.when(goes(k + 1, up))(lambda: hop(part, k + 1, up).start())
                for t in range(1, p.lo):
                    cross(part, z - 1 - k if up else z + 1 + k, t).start()

    def w_finish(part):
        for source in range(p.hi):
            for t in range(1, p.lo):
                rows = w_at(source * p.lo + turn(x, -t, p.lo), part)
                slot = (part * p.hi + source) * (p.lo - 1) + t - 1
                link(rows, rows, (r.lo_s, r.lo_r), slot, (b, d)).wait_recv()

    def w_end():
        for part in range(p.heads + 1):
            for k in range(last):
                for up in (True, False):
                    pl.when(goes(k, up))(lambda: hop(part, k, up).wait_send())
            for source in range(p.hi):
                for t in range(1, p.lo):
                    cross(part, source, t).wait_send()

    local, over, beside = [], {}, []

    def experts_begin():
        for s in range(1, p.local):
            to = turn(e, s, p.local)
            peer = (to * p.group + g, d)
            over[s, 0] = send(r.weight_in.at[to], in_at(b), (r.wide_s, r.wide_r), 2 * s - 2, peer)
            over[s, 1] = send(r.weight_back.at[to], back_at(b), (r.wide_s, r.wide_r), 2 * s - 1, peer)
        for t in range(1, p.group):
            peer = (e * p.group + turn(g, t, p.group), d)
            beside.append(send(r.weight_in.at[e], in_at(b), (r.near_s, r.near_r), 2 * t - 2, peer))
            beside.append(send(r.weight_back.at[e], back_at(b), (r.near_s, r.near_r), 2 * t - 1, peer))

    def experts_pass():
        for s in range(1, p.local):
            source = turn(e, -s, p.local) * p.group + g
            for which, rows in ((0, in_at(source)), (1, back_at(source))):
                over[s, which].wait_recv()
                for t in range(1, p.group):
                    k = (s * (p.group - 1) + t - 1) * 2 + which
                    peer = (e * p.group + turn(g, t, p.group), d)
                    beside.append(send(rows, rows, (r.near_s, r.near_r), k, peer))

    tables = []
    saves = []

    w_begin(0)
    for step in range(2):
        r.routes[8 * step : 8 * step + p.top, :] = r.attention_routes[step]
        r.routes[8 * step + p.top : 8 * step + 6, :] = r.expert_routes[step]
        r.routes[8 * step + 6 : 8 * step + 8, :] = jnp.zeros((2, p.seq), jnp.int32)
    r.all_picks[b] = r.routes[...]
    picks = PackGather(p, r.all_picks, r.picks_sems)
    picks.begin()
    state = r.x[...].astype(F32)

    def before(gather):
        local.extend(moves(r, [(r.weight_in.at[e], in_at(b)), (r.weight_back.at[e], back_at(b))]))
        tables.extend(slot_tables(p, r))
        w_pass(0, 0)
        w_pass(0, 1)
        gather.finish_far()
        picks.finish_far()
        experts_begin()
        for k in range(2, last):
            w_pass(0, k)
        w_begin(1)
        w_finish(0)
        project_rows(p, r, 0)
        for part in range(1, p.heads + 1):
            for k in range(last):
                waiting.append((part, k))

    waiting = []

    def tick():
        if waiting:
            part, k = waiting.pop(0)
            w_pass(part, k)
            if k == last - 1 and part < p.heads:
                w_begin(part + 1)

    def drain(part):
        while waiting and waiting[0][0] <= part:
            tick()
        w_finish(part)

    def ready(head):
        drain(head)
        project_rows(p, r, head)

    def out_ready():
        drain(p.heads)

    def after():
        saves.extend(moves(r, [(r.all_w, r.all_w_out), (r.disp, r.disp_out), (r.comb, r.comb_out)]))
        experts_pass()

    total = attention_forward(p, r, r.a, 0, state, before, ready, tick, out_ready, after)
    middle = state + total.T
    r.middle[...] = middle
    m = (norm_parts(middle)[1] * r.gain_two[...].astype(F32)).astype(BF)
    r.outgoing[...] = mm(r.disp[0], m).astype(BF)
    there = slot_sends(p, r.outgoing, r.arrived, (r.go_s, r.go_r), slot_peer)
    saves.extend(moves(r, [(getattr(r.a, k), getattr(r, k + "_out")) for k in SAVED]))
    for copy in tables:
        copy.wait_recv()
    slot_pairs(p, r)
    for copy in beside:
        copy.wait_recv()
    arrive(local)
    saves.extend(moves(r, [(r.all_in, r.all_in_out), (r.all_back, r.all_back_out), (r.pair, r.pair_end)]))
    back = {}
    for at, sources in slot_groups(p):
        receive(there, sources)
        rows = r.arrived[at, :]
        out = expert_output(p, r, rows, at, False)
        r.produced[at, :] = out.astype(BF)
        r.ret_out[at, :] = (out * slot_gates(p, r, rows, r.pair[0, at, :].astype(F32))).astype(BF)
        for s in sources:
            if s:
                back[s] = slot_send(p, r.ret_out, r.ret_in, (r.ret_s, r.ret_r), s, slot_source(p, s))
    r.ret_in[0 : p.cap, :] = r.ret_out[0 : p.cap, :]
    receive(back, range(p.experts))
    r.first[...] = r.middle[...] + mm(r.comb[0], r.ret_in[...])
    sent(there)
    sent(back)
    sent(tables)
    sent(beside)
    w_end()
    sent(over)
    picks.end()
    arrive(saves)


def turn_kernel(p, r):
    peers = pack_peers(p) + slot_peers(p)
    greet(peers)
    early = moves(
        r, [(r.disp_in.at[1], r.disp), (r.all_w_in, r.all_w), (r.comb_in.at[1], r.comb), (r.pair_in.at[1], r.pair)]
    )
    fill_router(p, r)
    weights = moves(r, [(r.all_in_in, r.all_in), (r.all_back_in, r.all_back)])
    first = r.first[...]
    stop = 1.0 / (1.0 + jnp.exp(-jnp.sum(first * r.halt[...].astype(F32), axis=-1, keepdims=True)))
    cot = r.cot[...].astype(F32)
    segment_columns(p, r.segments, r.seg_cols)
    answered(peers)
    there_u, saves = {}, []

    def before(gather):
        arrive(early)
        r.u_out[...] = mm(r.disp[...], ((1.0 - stop) * cot).astype(BF)).astype(BF)
        there_u.update(slot_sends(p, r.u_out, r.u_in, (r.u_s, r.u_r), slot_peer))
        for head in range(p.heads):
            project_rows(p, r, head)

    def nothing(*_):
        pass

    total = attention_forward(p, r, r.a, 1, first, before, nothing, nothing, nothing, nothing)
    middle = first + total.T
    r.middle[...] = middle
    m = (norm_parts(middle)[1] * r.gain_two[...].astype(F32)).astype(BF)
    r.outgoing[...] = mm(r.disp[...], m).astype(BF)
    there = slot_sends(p, r.outgoing, r.arrived, (r.go_s, r.go_r), slot_peer)
    transposed(r.wo, r.all_w, 0, p.qkv, p.all_cols, LANES)
    attention_rows(p, r, r.a, False)
    arrive(weights)
    sent(there_u)
    ret_out = r.u_out
    back, back_out = {}, {}
    for at, sources in slot_groups(p):
        receive(there_u, sources)
        receive(there, sources)
        rows = r.arrived[at, :]
        pair = r.pair[at, :].astype(F32)
        out = expert_output(p, r, rows, at, True)
        ret_out[at, :] = (out * slot_gates(p, r, rows, pair)).astype(BF)
        expert_input_grad(p, r, at, r.u_in[at, :].astype(F32), rows, out, pair, r.gret_out)
        for s in sources:
            if s:
                back[s] = slot_send(p, r.gret_out, r.gret_in, (r.gret_s, r.gret_r), s, slot_source(p, s))
    r.gret_in[0 : p.cap, :] = r.gret_out[0 : p.cap, :]
    r.ret_in[0 : p.cap, :] = ret_out[0 : p.cap, :]
    r.grad_router[...] = expert_weight_grads(p, r, r.arrived, False)
    saves.extend(moves(r, [(r.grad_in, r.grad_in_out), (r.grad_back, r.grad_back_out)]))
    attention_probs(p, r, r.a)
    receive(back, range(p.experts))
    step_back, gain_two = norm_back(r.middle[...], r.gain_two[...].astype(F32), mm(r.comb[...], r.gret_in[...]))
    r.grad_gain_two[...] = gain_two
    grad_middle = (1.0 - stop) * cot + step_back

    def before_back():
        for s in range(1, p.experts):
            back_out[s] = slot_send(p, ret_out, r.ret_in, (r.ret_s, r.ret_r), s, slot_source(p, s))

    def head_done(head):
        if head == p.heads - 1:
            for part in p.parts:
                attention_weight_grads(p, r, r.a, part.start, part.stop, False)

    grad, gain_one, router = attention_backward(
        p, r, r.a, 1, first, grad_middle, before_back, lambda: None, head_done
    )
    saves.extend(moves(r, [(r.grad_w, r.grad_w_out)]))
    r.grad_gain_one[...] = gain_one
    r.grad_mixer[...] = router
    receive(back_out, range(p.experts))
    second = r.middle[...] + mm(r.comb[...], r.ret_in[...])
    r.result[...] = (stop * first + (1.0 - stop) * second).astype(BF)
    grad_stop = jnp.sum(cot * (first - second), axis=-1, keepdims=True)
    coeff = grad_stop * stop * (1.0 - stop)
    r.grad_halt[...] = jnp.sum(coeff * first, axis=0, keepdims=True)
    r.grad_first[...] = stop * cot + coeff * r.halt[...].astype(F32) + grad
    for copies in (there, back, back_out):
        sent(copies)
    arrive(saves)


def backward_kernel(p, r):
    b, d = place()
    z, x = d // p.lo, lax.rem(d, p.lo)
    y, c = b // 2, lax.rem(b, 2)
    e, g = b // p.group, lax.rem(b, p.group)
    rows = r.out_w.shape[0]
    in_rows, back_rows = r.out_in.shape[1], r.out_back.shape[1]
    peers = pack_peers(p) + slot_peers(p) + dp_peers(p) + expert_peers(p)
    greet(peers)
    early = moves(
        r,
        [
            (r.disp_in.at[0], r.disp),
            (r.pair_in.at[0], r.pair),
            (r.arrived_in, r.arrived),
            (r.all_in_in, r.all_in),
            (r.all_back_in, r.all_back),
            (r.produced_in, r.produced),
        ],
    )
    later = moves(
        r, [(r.grad_in_in, r.grad_in), (r.grad_back_in, r.grad_back), (r.comb_in.at[0], r.comb), (r.all_w_in, r.all_w)]
    )
    later += moves(r, [(r.grad_w_in, r.grad_w)])
    later += moves(r, [(getattr(r, k + "_in"), getattr(r.a, k)) for k in SAVED])
    fill_router(p, r)
    grad_first = r.grad_first[...]
    early[0].wait()
    r.u_out[...] = mm(r.disp[...], grad_first.astype(BF)).astype(BF)
    answered(peers)
    there = slot_sends(p, r.u_out, r.u_in, (r.u_s, r.u_r), slot_peer)
    arrive(early[1:])
    for at, _ in slot_groups(p):
        expert_keep(p, r, r.arrived[at, :], at)
    segment_columns(p, r.segments, r.seg_cols)
    arrive(later)
    attention_rows(p, r, r.a, True)
    transposed(r.wo, r.all_w, 0, p.qkv, p.all_cols, LANES)
    back = {}
    for at, sources in slot_groups(p):
        receive(there, sources)
        pair = r.pair[at, :].astype(F32)
        out = r.produced[at, :].astype(F32)
        expert_input_grad(p, r, at, r.u_in[at, :].astype(F32), r.arrived[at, :], out, pair, r.produced)
        for s in sources:
            if s:
                back[s] = slot_send(p, r.produced, r.gret_in, (r.gret_s, r.gret_r), s, slot_source(p, s))
    r.gret_in[0 : p.cap, :] = r.produced[0 : p.cap, :]
    r.grad_router[...] = expert_weight_grads(p, r, r.arrived, True)

    def row_block(ref, index, size, lanes=slice(None)):
        return ref.at[pl.ds(aligned(index * size, size), size), lanes]

    near = {}
    for k in range(p.local):
        to = turn(e, k + 1, p.local)
        for t in range(1, p.group):
            member = turn(g, t, p.group)
            slot = k * (p.group - 1) + t - 1
            peer = (e * p.group + member, d)
            owner = to * p.group + member
            near[k, t, 0] = send(
                row_block(r.grad_in, owner, in_rows), r.in_near.at[slot], (r.near_s, r.near_r), 2 * slot, peer
            )
            near[k, t, 1] = send(
                row_block(r.grad_back, owner, back_rows), r.back_near.at[slot], (r.near_s, r.near_r), 2 * slot + 1, peer
            )
    attention_probs(p, r, r.a)
    receive(back, range(p.experts))
    step_back, gain_two = norm_back(r.middle[...], r.gain_two[...].astype(F32), mm(r.comb[...], r.gret_in[...]))
    grad_middle = grad_first + step_back
    wide, lo_copies, hi_copies = {}, {}, {}

    def experts_wide():
        for k in range(p.local):
            to = turn(e, k + 1, p.local)
            total_in = row_block(r.grad_in, to * p.group + g, in_rows)[...].astype(F32)
            total_back = row_block(r.grad_back, to * p.group + g, back_rows)[...].astype(F32)
            for t in range(1, p.group):
                slot = k * (p.group - 1) + t - 1
                near[k, t, 0].wait_recv()
                near[k, t, 1].wait_recv()
                total_in = total_in + r.in_near[slot].astype(F32)
                total_back = total_back + r.back_near[slot].astype(F32)
            if k < p.local - 1:
                r.in_far_out[k] = total_in.astype(BF)
                r.back_far_out[k] = total_back.astype(BF)
                peer = (to * p.group + g, d)
                wide[k, 0] = send(r.in_far_out.at[k], r.in_far.at[k], (r.wide_s, r.wide_r), 2 * k, peer)
                wide[k, 1] = send(r.back_far_out.at[k], r.back_far.at[k], (r.wide_s, r.wide_r), 2 * k + 1, peer)
            else:
                r.out_in[e] = total_in.astype(BF)
                r.out_back[e] = total_back.astype(BF)

    parts = p.parts

    def sum_begin(part):
        for k in range(p.hi):
            to = turn(z, k + 1, p.hi)
            for t in range(1, p.lo):
                slot = k * (p.lo - 1) + t - 1
                xx = turn(x, t, p.lo)
                lo_copies[part, k, t] = send(
                    row_block(r.grad_w, to * p.lo + xx, rows, parts[part]),
                    r.w_lo.at[slot, :, parts[part]],
                    (r.lo_s, r.lo_r),
                    part * p.hi * (p.lo - 1) + slot,
                    (b, z * p.lo + xx),
                )

    def sum_pass(part):
        lanes = parts[part]
        for k in range(p.hi):
            to = turn(z, k + 1, p.hi)
            total = row_block(r.grad_w, to * p.lo + x, rows, lanes)[...].astype(F32)
            for t in range(1, p.lo):
                lo_copies[part, k, t].wait_recv()
                total = total + r.w_lo[k * (p.lo - 1) + t - 1, :, lanes].astype(F32)
            if k < p.hi - 1:
                r.w_hi_out[k, :, lanes] = total.astype(BF)
                hi_copies[part, k] = send(
                    r.w_hi_out.at[k, :, lanes],
                    r.w_hi.at[k, :, lanes],
                    (r.hi_s, r.hi_r),
                    part * (p.hi - 1) + k,
                    (b, to * p.lo + x),
                )
            else:
                r.out_w[:, lanes] = total

    def sum_finish(part):
        lanes = parts[part]
        total = r.out_w[:, lanes]
        for k in range(p.hi - 1):
            hi_copies[part, k].wait_recv()
            total = total + r.w_hi[k, :, lanes].astype(F32)
        r.out_w[:, lanes] = total

    def middle():
        experts_wide()
        attention_weight_grads(p, r, r.a, p.qkv, p.all_cols, True)
        sum_begin(p.heads)

    def head_done(head):
        attention_weight_grads(p, r, r.a, parts[head].start, parts[head].stop, True)
        sum_begin(head)
        sum_pass(p.heads if head == 0 else head - 1)

    grad, gain_one, router = attention_backward(
        p, r, r.a, 0, r.x[...].astype(F32), grad_middle, lambda: None, middle, head_done
    )
    small = r.out_small
    small[...] = jnp.zeros_like(small)
    small[0:1, :] = r.gain_one_before[...] + gain_one
    small[1:2, :] = r.gain_two_before[...] + gain_two
    small[2:3, :] = r.halt_before[...]
    small[8 : 8 + p.mixers, :] = r.mixer_before[...] + router
    small[8 + p.mixers :, :] = r.router_before[...] + r.grad_router[...]
    tiny = []
    axes = (
        (2, c, lambda t: (2 * y + turn(c, t, 2), d)),
        (p.chips, y, lambda t: (2 * turn(y, t, p.chips) + c, d)),
        (p.lo, x, lambda t: (b, z * p.lo + turn(x, t, p.lo))),
        (p.hi, z, lambda t: (b, turn(z, t, p.hi) * p.lo + x)),
    )

    def tiny_begin(axis):
        size, index, peer = axes[axis]
        base = sum(entry[0] for entry in axes[:axis])
        r.all_small[base + index] = small[...]
        at = r.all_small.at[base + index]
        for t in range(1, size):
            tiny.append(send(at, at, (r.tiny_s, r.tiny_r), base + t - 1, peer(t)))

    def tiny_finish(axis):
        size = axes[axis][0]
        base = sum(entry[0] for entry in axes[:axis])
        for copy in tiny[len(tiny) - (size - 1) :]:
            copy.wait_recv()
        total = r.all_small[base]
        for k in range(1, size):
            total = total + r.all_small[base + k]
        small[...] = total

    tiny_begin(0)
    r.input_grad[...] = grad.astype(BF)
    tiny_finish(0)
    tiny_begin(1)
    sum_pass(p.heads - 1)
    tiny_finish(1)
    tiny_begin(2)
    for k in range(p.local - 1):
        source = turn(e, -(k + 1), p.local)
        wide[k, 0].wait_recv()
        wide[k, 1].wait_recv()
        r.out_in[source] = r.in_far[k]
        r.out_back[source] = r.back_far[k]
    tiny_finish(2)
    tiny_begin(3)
    sum_finish(p.heads)
    for part in range(p.heads - 1):
        sum_finish(part)
    tiny_finish(3)
    sum_finish(p.heads - 1)
    for copies in (there, back, near, wide, lo_copies, hi_copies, tiny):
        sent(copies)


def output_kernel(p, r):
    cols = p.cols
    r.result_out[...] = r.result[...]
    r.input_grad_out[...] = r.input_grad[...]
    r.in_out[...] = r.out_in[...].astype(F32)
    r.back_out[...] = r.out_back[...].astype(F32)
    for e in range(p.mixers):
        heads = [h * p.head_cols + e * HD for h in range(p.heads)]
        r.query_out[e] = jnp.concatenate([r.out_w[:, at : at + HD] for at in heads], axis=1)
        start = p.qkv + e * cols
        r.out_out[e] = r.out_w[:, start : start + cols]
    heads = [h * p.head_cols + p.mixers * HD for h in range(p.heads)]
    r.key_out[...] = jnp.concatenate([r.out_w[:, at : at + HD] for at in heads], axis=1)
    r.value_out[...] = jnp.concatenate([r.out_w[:, at + HD : at + 2 * HD] for at in heads], axis=1)
    r.gain_one_out[...] = r.small[0:1, :]
    r.gain_two_out[...] = r.small[1:2, :]
    r.halt_out[...] = r.small[2:3, :]
    r.mixer_out[...] = r.small[8 : 8 + p.mixers, :]
    r.router_out[...] = r.small[8 + p.mixers :, :]


SAVED = ("nt", "qs", "kt", "vt", "lse", "att", "mix", "gates")


def dma(name, size):
    sem = pltpu.SemaphoreType.DMA((max(1, size),))
    return {name + "_s": sem, name + "_r": sem}


def pack_sems(p, name):
    sizes = (p.chips - 1, p.chips - 1, p.chips, p.chips)
    return {f"{name}_{k}": pltpu.SemaphoreType.DMA((max(1, size),)) for k, size in enumerate(sizes)}


def sum_scratch(p):
    far = max(1, p.chips - 1)
    return {
        "part": pltpu.VMEM((p.chips, p.width, p.seq), BF),
        "near_in": pltpu.VMEM((p.chips, p.width, p.seq), BF),
        "far_out": pltpu.VMEM((far, p.width, p.seq), BF),
        "far_in": pltpu.VMEM((far, p.width, p.seq), BF),
    }


def saved_shapes(p):
    return {
        "nt": ((p.blk, p.width, p.seq), BF),
        "qs": ((p.heads, p.blocks, HD, p.top * QROWS), BF),
        "kt": ((p.heads, HD, p.length + MAXLEN), BF),
        "vt": ((p.heads, HD, p.length + MAXLEN), BF),
        "lse": ((p.blocks, 8, p.top * QROWS), F32),
        "att": ((p.heads, p.blocks, HD, p.top * QROWS), BF),
        "mix": ((p.mixers * p.cols, p.length), BF),
        "gates": ((p.blk, 8, p.seq), F32),
    }


def launch(body, name, number, ins, outs, scratch):
    def spec(vmem):
        return pl.BlockSpec(memory_space=pltpu.VMEM if vmem else pl.ANY)

    names = list(ins) + list(outs) + list(scratch)

    def kernel(*refs):
        r = SimpleNamespace(**dict(zip(names, refs, strict=True)))
        r.moved = 0
        r.a = SimpleNamespace(**{k[2:]: v for k, v in vars(r).items() if k.startswith("a_")})
        for key in ("gather", "sum", "back_gather", "back_sum", "picks"):
            sems = [getattr(r, f"{key}_{k}") for k in range(4) if hasattr(r, f"{key}_{k}")]
            setattr(r.a, key + "_sems", sems)
            setattr(r, key + "_sems", sems)
        body(r)

    results = pl.pallas_call(
        kernel,
        out_shape=tuple(jax.ShapeDtypeStruct(shape, dtype) for shape, dtype, _ in outs.values()),
        in_specs=[spec(vmem) for _, vmem in ins.values()],
        out_specs=tuple(spec(vmem) for _, _, vmem in outs.values()),
        scratch_shapes=list(scratch.values()),
        compiler_params=pltpu.CompilerParams(
            collective_id=number, has_side_effects=number is not None, vmem_limit_bytes=VMEM_BYTES
        ),
        name=name,
    )(*[array for array, _ in ins.values()])
    return SimpleNamespace(**dict(zip(outs, results, strict=True)))


def on_device(
    inputs,
    segments,
    attention_routes,
    expert_routes,
    gain_mixer,
    gain_expert,
    weight_query,
    weight_key,
    weight_value,
    weight_out,
    router_mixer,
    router_expert,
    weight_in,
    weight_back,
    halt_weight,
    cotangent,
):
    blk, dp = lax.axis_size("blk"), lax.axis_size("dp")
    seq, width = inputs.shape[1:]
    experts, local = router_expert.shape[1], weight_in.shape[0]
    slots_of = max(2, 3 * seq // experts)
    hi = 4
    p = Plan(
        blk=blk,
        dp=dp,
        lo=dp // hi,
        hi=hi,
        seq=seq,
        width=width,
        heads=HEADS // blk,
        mixers=weight_query.shape[0],
        top=attention_routes.shape[-1],
        experts=experts,
        local=local,
        group=blk // local,
        cap=-(-slots_of // 16) * 16,
        ff=weight_in.shape[2],
    )
    cols, length, top = p.cols, p.length, p.top
    share, in_rows, back_rows = weight_key.shape[0], weight_in.shape[1], weight_back.shape[1]

    gain_one = gain_mixer.reshape(1, width)
    gain_two = gain_expert.reshape(1, width)
    halt = halt_weight.reshape(1, width)
    router_row, router = router_mixer.T, router_expert.T

    slots_bf = pltpu.VMEM((p.slots, width), BF)
    saved = saved_shapes(p)
    attention_scratch = {
        "seg_cols": pltpu.VMEM((length + MAXLEN, 8), F32),
        "k_rows": pltpu.VMEM((p.heads, length + MAXLEN, HD), BF),
        "all_w": pltpu.VMEM((width, p.all_cols), BF),
        **{"a_" + k: pltpu.VMEM(*v) for k, v in saved.items()},
    }
    forward_scratch = {
        "w_t": pltpu.VMEM((p.qkv, width), BF),
        **pack_sems(p, "gather"),
        **pack_sems(p, "sum"),
        **sum_scratch(p),
    }
    backward_scratch = {
        "gt": pltpu.VMEM((blk, width, seq), BF),
        "v_rows": pltpu.VMEM((p.heads, length + MAXLEN, HD), BF),
        "means": pltpu.VMEM((p.blocks, 8, top * QROWS), F32),
        "dlog": pltpu.VMEM((blk, p.mixers, seq), F32),
        "dkt": pltpu.VMEM((p.heads, HD, length + MAXLEN), F32),
        "dvt": pltpu.VMEM((p.heads, HD, length + MAXLEN), F32),
        "dall": pltpu.VMEM((p.qkv, length), BF),
        "grad_w": pltpu.VMEM((width, p.all_cols), BF),
        **pack_sems(p, "back_gather"),
        **pack_sems(p, "back_sum"),
        **sum_scratch(p),
    }
    expert_scratch = {
        "router": pltpu.VMEM((LANES, width), BF),
        "all_in": pltpu.VMEM((width, p.ff), BF),
        "all_back": pltpu.VMEM((p.ff, width), BF),
    }
    expert_back_scratch = {
        "keep": pltpu.VMEM((2, p.slots, p.ff), BF),
        "coeff": pltpu.VMEM((p.slots, LANES), BF),
        "arrived_t": pltpu.VMEM((width, p.slots), BF),
        "u_out": slots_bf,
        "u_in": slots_bf,
        "gret_in": slots_bf,
        "grad_in": pltpu.VMEM((width, p.ff), BF),
        "grad_back": pltpu.VMEM((p.ff, width), BF),
        **dma("u", p.experts),
        **dma("gret", p.experts),
    }

    one = launch(
        functools.partial(forward_kernel, p),
        "forward",
        0,
        {
            "x": (inputs[0], True),
            "segments": (segments, True),
            "attention_routes": (jnp.swapaxes(attention_routes[:, 0], 1, 2), True),
            "expert_routes": (jnp.swapaxes(expert_routes[:, 0], 1, 2), True),
            "gain_one": (gain_one, True),
            "gain_two": (gain_two, True),
            "router_row": (router_row, True),
            "router_in": (router, True),
            "weight_query": (weight_query, True),
            "weight_key": (weight_key, True),
            "weight_value": (weight_value, True),
            "weight_out": (jnp.swapaxes(weight_out, 1, 2), True),
            "weight_in": (weight_in, False),
            "weight_back": (weight_back, False),
        },
        {
            "first": ((seq, width), F32, True),
            "middle": ((seq, width), F32, True),
            "arrived": ((p.slots, width), BF, True),
            "produced": ((p.slots, width), BF, True),
            "all_picks": ((blk, 16, seq), jnp.int32, True),
            "disp_out": ((2, p.slots, seq), BF, False),
            "comb_out": ((2, seq, p.slots), BF, False),
            "pair_end": ((2, p.slots, LANES), BF, False),
            "all_w_out": ((width, p.all_cols), BF, False),
            "all_in_out": ((width, p.ff), BF, False),
            "all_back_out": ((p.ff, width), BF, False),
            **{k + "_out": (*v, False) for k, v in saved.items()},
        },
        {
            **attention_scratch,
            **forward_scratch,
            **expert_scratch,
            "disp": pltpu.VMEM((2, p.slots, seq), BF),
            "comb": pltpu.VMEM((2, seq, p.slots), BF),
            "pair": pltpu.VMEM((2, p.slots, LANES), BF),
            "pair_out": pltpu.VMEM((experts, 8, LANES), F32),
            "pair_in": pltpu.VMEM((experts, 8, LANES), F32),
            "routes": pltpu.VMEM((16, seq), jnp.int32),
            "outgoing": slots_bf,
            "ret_out": slots_bf,
            "ret_in": slots_bf,
            **pack_sems(p, "picks"),
            **dma("hi", 2 * (p.heads + 1) * (p.hi - 1)),
            **dma("lo", (p.heads + 1) * p.hi * (p.lo - 1)),
            **dma("wide", 2 * (p.local - 1)),
            **dma("near", 2 * p.local * (p.group - 1)),
            **dma("pair", p.experts),
            **dma("go", p.experts),
            **dma("ret", p.experts),
            "moves": pltpu.SemaphoreType.DMA((16,)),
        },
    )
    two = launch(
        functools.partial(turn_kernel, p),
        "turn",
        1,
        {
            "first": (one.first, True),
            "cot": (cotangent[0], True),
            "halt": (halt, True),
            "segments": (segments, True),
            "all_picks": (one.all_picks, True),
            "gain_one": (gain_one, True),
            "gain_two": (gain_two, True),
            "router_row": (router_row, True),
            "router_in": (router, True),
            "disp_in": (one.disp_out, False),
            "comb_in": (one.comb_out, False),
            "pair_in": (one.pair_end, False),
            "all_w_in": (one.all_w_out, False),
            "all_in_in": (one.all_in_out, False),
            "all_back_in": (one.all_back_out, False),
        },
        {
            "result": ((seq, width), BF, True),
            "grad_first": ((seq, width), F32, True),
            "grad_halt": ((1, width), F32, True),
            "grad_gain_one": ((1, width), F32, True),
            "grad_gain_two": ((1, width), F32, True),
            "grad_mixer": ((p.mixers, width), F32, True),
            "grad_router": ((experts, width), F32, True),
            "grad_in_out": ((width, p.ff), BF, False),
            "grad_back_out": ((p.ff, width), BF, False),
            "grad_w_out": ((width, p.all_cols), BF, False),
        },
        {
            **attention_scratch,
            **forward_scratch,
            **backward_scratch,
            **expert_scratch,
            **expert_back_scratch,
            "wo": pltpu.VMEM((p.mixers * cols, width), BF),
            "disp": pltpu.VMEM((p.slots, seq), BF),
            "comb": pltpu.VMEM((seq, p.slots), BF),
            "pair": pltpu.VMEM((p.slots, LANES), BF),
            "middle": pltpu.VMEM((seq, width), F32),
            "outgoing": slots_bf,
            "arrived": slots_bf,
            "gret_out": slots_bf,
            "ret_in": slots_bf,
            **dma("go", p.experts),
            **dma("ret", p.experts),
            "moves": pltpu.SemaphoreType.DMA((16,)),
        },
    )
    near, far = p.local * (p.group - 1), max(1, p.local - 1)
    small_rows = 8 + p.mixers + experts
    three = launch(
        functools.partial(backward_kernel, p),
        "backward",
        2,
        {
            "x": (inputs[0], True),
            "grad_first": (two.grad_first, True),
            "middle": (one.middle, True),
            "segments": (segments, True),
            "all_picks": (one.all_picks, True),
            "gain_one": (gain_one, True),
            "gain_two": (gain_two, True),
            "router_row": (router_row, True),
            "router_in": (router, True),
            "halt_before": (two.grad_halt, True),
            "gain_one_before": (two.grad_gain_one, True),
            "gain_two_before": (two.grad_gain_two, True),
            "mixer_before": (two.grad_mixer, True),
            "router_before": (two.grad_router, True),
            "disp_in": (one.disp_out, False),
            "comb_in": (one.comb_out, False),
            "pair_in": (one.pair_end, False),
            "arrived_in": (one.arrived, False),
            "produced_in": (one.produced, False),
            "all_w_in": (one.all_w_out, False),
            "all_in_in": (one.all_in_out, False),
            "all_back_in": (one.all_back_out, False),
            "grad_in_in": (two.grad_in_out, False),
            "grad_back_in": (two.grad_back_out, False),
            "grad_w_in": (two.grad_w_out, False),
            **{k + "_in": (getattr(one, k + "_out"), False) for k in SAVED},
        },
        {
            "input_grad": ((seq, width), BF, True),
            "out_w": ((share, p.all_cols), F32, True),
            "out_in": ((local, in_rows, p.ff), BF, True),
            "out_back": ((local, back_rows, width), BF, True),
            "out_small": ((small_rows, width), F32, True),
        },
        {
            **attention_scratch,
            **backward_scratch,
            **expert_scratch,
            **expert_back_scratch,
            "wo": pltpu.VMEM((p.mixers * cols, width), BF),
            "disp": pltpu.VMEM((p.slots, seq), BF),
            "comb": pltpu.VMEM((seq, p.slots), BF),
            "pair": pltpu.VMEM((p.slots, LANES), BF),
            "arrived": slots_bf,
            "produced": slots_bf,
            "in_near": pltpu.VMEM((near, in_rows, p.ff), BF),
            "back_near": pltpu.VMEM((near, back_rows, width), BF),
            "in_far_out": pltpu.VMEM((far, in_rows, p.ff), BF),
            "in_far": pltpu.VMEM((far, in_rows, p.ff), BF),
            "back_far_out": pltpu.VMEM((far, back_rows, width), BF),
            "back_far": pltpu.VMEM((far, back_rows, width), BF),
            "w_lo": pltpu.VMEM((hi * (p.lo - 1), share, p.all_cols), BF),
            "w_hi_out": pltpu.VMEM((hi - 1, share, p.all_cols), BF),
            "w_hi": pltpu.VMEM((hi - 1, share, p.all_cols), BF),
            "grad_router": pltpu.VMEM((experts, width), F32),
            "all_small": pltpu.VMEM((2 + p.chips + p.lo + hi, small_rows, width), F32),
            **dma("near", 2 * near),
            **dma("wide", 2 * (local - 1)),
            **dma("lo", (p.heads + 1) * hi * (p.lo - 1)),
            **dma("hi", (p.heads + 1) * (hi - 1)),
            **dma("tiny", 2 + p.chips + p.lo + hi),
            "moves": pltpu.SemaphoreType.DMA((24,)),
        },
    )
    four = launch(
        functools.partial(output_kernel, p),
        "outputs",
        None,
        {
            "result": (two.result, True),
            "input_grad": (three.input_grad, True),
            "out_w": (three.out_w, True),
            "out_in": (three.out_in, True),
            "out_back": (three.out_back, True),
            "small": (three.out_small, True),
        },
        {
            "result_out": ((seq, width), BF, True),
            "input_grad_out": ((seq, width), BF, True),
            "query_out": (weight_query.shape, F32, True),
            "key_out": (weight_key.shape, F32, True),
            "value_out": (weight_value.shape, F32, True),
            "out_out": ((p.mixers, share, cols), F32, True),
            "in_out": (weight_in.shape, F32, True),
            "back_out": (weight_back.shape, F32, True),
            "gain_one_out": ((1, width), F32, True),
            "gain_two_out": ((1, width), F32, True),
            "halt_out": ((1, width), F32, True),
            "mixer_out": ((p.mixers, width), F32, True),
            "router_out": ((experts, width), F32, True),
        },
        {},
    )
    return (
        four.result_out[None],
        four.input_grad_out[None],
        four.gain_one_out.reshape(width),
        four.gain_two_out.reshape(width),
        four.query_out,
        four.key_out,
        four.value_out,
        jnp.swapaxes(four.out_out, 1, 2),
        four.mixer_out.T,
        four.router_out.T,
        four.in_out,
        four.back_out,
        four.halt_out.reshape(width),
    )


def solution(mesh):
    return jax.shard_map(
        on_device,
        mesh=mesh,
        in_specs=(
            P("dp", "blk", None),
            P("dp", None),
            P(None, "dp", "blk", None),
            P(None, "dp", "blk", None),
            P(),
            P(),
            P(None, "dp", "blk"),
            P("dp", "blk"),
            P("dp", "blk"),
            P(None, "blk", "dp"),
            P(),
            P(),
            P("dp", "blk", None),
            P("dp", "blk", None),
            P(),
            P("dp", "blk", None),
        ),
        out_specs=(
            P("dp", "blk", None),
            P("dp", "blk", None),
            P(),
            P(),
            P(None, "dp", "blk"),
            P("dp", "blk"),
            P("dp", "blk"),
            P(None, "blk", "dp"),
            P(),
            P(),
            P("dp", "blk", None),
            P("dp", "blk", None),
            P(),
        ),
        check_vma=False,
    )
```

```python
import functools
from types import SimpleNamespace
from typing import NamedTuple

import jax
import jax.numpy as jnp
from jax import lax
from jax.experimental import pallas as pl
from jax.experimental.pallas import tpu as pltpu
from jax.sharding import PartitionSpec as P

HEADS = 8
HD = 64
MAXLEN = 256
QROWS = 128
WINDOW = MAXLEN + QROWS
LANES = 128
EPSILON = 1e-06
MASKED_SCORE = -1e30
MESH = pl.DeviceIdType.MESH
BF = jnp.bfloat16
F32 = jnp.float32
VMEM_BYTES = 61 * 2**20


class Plan(NamedTuple):
    blk: int
    dp: int
    lo: int
    hi: int
    seq: int
    width: int
    heads: int
    mixers: int
    top: int
    experts: int
    local: int
    group: int
    cap: int
    ff: int

    @property
    def length(self):
        return self.blk * self.seq

    @property
    def cols(self):
        return self.heads * HD

    @property
    def qkv(self):
        return (self.mixers + 2) * self.cols

    @property
    def all_cols(self):
        return (2 * self.mixers + 2) * self.cols

    @property
    def blocks(self):
        return self.length // QROWS

    @property
    def slots(self):
        return self.experts * self.cap

    @property
    def head_cols(self):
        return (self.mixers + 2) * HD

    @property
    def parts(self):
        heads = [slice(h * self.head_cols, (h + 1) * self.head_cols) for h in range(self.heads)]
        return (*heads, slice(self.qkv, self.all_cols))

    @property
    def tile(self):
        return 512 if self.slots <= 768 else 256

    @property
    def chips(self):
        return self.blk // 2


def mm(a, b):
    return lax.dot_general(a, b, (((1,), (0,)), ((), ())), preferred_element_type=F32)


def mm_nt(a, b):
    return lax.dot_general(a, b, (((1,), (1,)), ((), ())), preferred_element_type=F32)


def place():
    return lax.axis_index("blk"), lax.axis_index("dp")


def turn(index, by, size):
    return lax.rem(index + (by % size), size)


def greet(peers):
    barrier = pltpu.get_barrier_semaphore()
    for peer in peers:
        pl.semaphore_signal(barrier, inc=1, device_id=peer, device_id_type=MESH)


def answered(peers):
    pl.semaphore_wait(pltpu.get_barrier_semaphore(), len(peers))


def send(src, dst, sems, slot, peer):
    copy = pltpu.make_async_remote_copy(
        src_ref=src,
        dst_ref=dst,
        send_sem=sems[0].at[slot],
        recv_sem=sems[1].at[slot],
        device_id=peer,
        device_id_type=MESH,
    )
    copy.start()
    return copy


def aligned(value, by):
    return pl.multiple_of(value, by)


def pack_peers(p):
    b, d = place()
    y, c = b // 2, lax.rem(b, 2)
    peers = [(2 * y + 1 - c, d)]
    return peers + [(2 * turn(y, s, p.chips) + c, d) for s in range(1, p.chips)]


def slot_peer(p, s):
    b, d = place()
    e, g = b // p.group, lax.rem(b, p.group)
    return (turn(e, s // p.dp, p.local) * p.group + g, turn(d, s % p.dp, p.dp))


def slot_peers(p):
    return [slot_peer(p, s) for s in range(1, p.experts)]


def slot_source(p, s):
    b, d = place()
    e, g = b // p.group, lax.rem(b, p.group)
    return (turn(e, -(s // p.dp), p.local) * p.group + g, turn(d, -(s % p.dp), p.dp))


def dp_peers(p):
    b, d = place()
    z, x = d // p.lo, lax.rem(d, p.lo)
    peers = [(b, turn(z, s, p.hi) * p.lo + x) for s in range(1, p.hi)]
    return peers + [(b, z * p.lo + turn(x, t, p.lo)) for t in range(1, p.lo)]


def expert_peers(p):
    b, d = place()
    e, g = b // p.group, lax.rem(b, p.group)
    peers = [(turn(e, s, p.local) * p.group + g, d) for s in range(1, p.local)]
    return peers + [(e * p.group + turn(g, t, p.group), d) for t in range(1, p.group)]


def link(src, dst, sems, slot, peer):
    return pltpu.make_async_remote_copy(
        src_ref=src,
        dst_ref=dst,
        send_sem=sems[0].at[slot],
        recv_sem=sems[1].at[slot],
        device_id=peer,
        device_id_type=MESH,
    )


class PackGather:
    def __init__(self, p, buf, sems):
        self.p, self.buf, self.far, self.near = p, buf, sems[0:2], sems[2:4]
        self.done_near = self.done_far = False

    def begin(self):
        p = self.p
        b, d = place()
        y, c = b // 2, lax.rem(b, 2)
        own = self.buf.at[b]
        self.first = [
            send(own, own, self.far, s - 1, (2 * turn(y, s, p.chips) + c, d))
            for s in range(1, p.chips)
        ]
        self.second = [send(own, own, self.near, 0, (2 * y + 1 - c, d))]

    def finish_near(self):
        if not self.done_near:
            self.second[0].wait_recv()
        self.done_near = True

    def finish_far(self):
        if self.done_far:
            return
        self.done_far = True
        p = self.p
        b, d = place()
        y, c = b // 2, lax.rem(b, 2)
        for s in range(1, p.chips):
            self.first[s - 1].wait_recv()
            block = self.buf.at[2 * turn(y, -s, p.chips) + c]
            self.second.append(send(block, block, self.near, s, (2 * y + 1 - c, d)))
        self.finish_near()
        for copy in self.second[1:]:
            copy.wait_recv()

    def end(self):
        for copy in self.first + self.second:
            copy.wait_send()


class PackSum:
    def __init__(self, p, bufs, sems):
        self.p, self.bufs = p, bufs
        self.far, self.near = sems[0:2], sems[2:4]
        self.first, self.second = {}, []

    def give(self, s, term):
        p, r = self.p, self.bufs
        b, d = place()
        y, c = b // 2, lax.rem(b, 2)
        r.part[s] = term.astype(BF)
        self.first[s] = send(r.part.at[s], r.near_in.at[s], self.near, s, (2 * y + 1 - c, d))

    def pass_on(self, s, term):
        p, r = self.p, self.bufs
        b, d = place()
        y, c = b // 2, lax.rem(b, 2)
        self.first[s].wait_recv()
        r.far_out[s - 1] = (term + r.near_in[s].astype(F32)).astype(BF)
        self.second.append(
            send(r.far_out.at[s - 1], r.far_in.at[s - 1], self.far, s - 1, (2 * turn(y, s, p.chips) + c, d))
        )

    def total(self, term):
        r = self.bufs
        self.first[0].wait_recv()
        term = term + r.near_in[0].astype(F32)
        for k, copy in enumerate(self.second):
            copy.wait_recv()
            term = term + r.far_in[k].astype(F32)
        for copy in list(self.first.values()) + self.second:
            copy.wait_send()
        return term


def slot_send(p, src, dst, sems, s, peer):
    rows = pl.ds(s * p.cap, p.cap)
    return send(src.at[rows], dst.at[rows], sems, s, peer)


def slot_sends(p, src, dst, sems, peer):
    dst[0 : p.cap, :] = src[0 : p.cap, :]
    return {s: slot_send(p, src, dst, sems, s, peer(p, s)) for s in range(1, p.experts)}


def receive(copies, sources):
    for s in sources:
        if s in copies:
            copies[s].wait_recv()


def sent(copies):
    for copy in copies.values() if isinstance(copies, dict) else copies:
        copy.wait_send()


def move(r, src, dst):
    copy = pltpu.make_async_copy(src, dst, r.moves.at[r.moved])
    r.moved += 1
    copy.start()
    return copy


def moves(r, pairs):
    return [move(r, src, dst) for src, dst in pairs]


def arrive(copies):
    for copy in copies:
        copy.wait()
    copies.clear()


def norm_parts(state):
    inverse = lax.rsqrt(jnp.mean(state * state, axis=-1, keepdims=True) + EPSILON)
    return inverse, state * inverse


def norm_back(state, gain, grad):
    inverse, unit = norm_parts(state)
    scaled = grad * gain
    back = inverse * scaled - state * (inverse * inverse * inverse) * jnp.mean(
        scaled * state, axis=-1, keepdims=True
    )
    return back, jnp.sum(grad * unit, axis=0, keepdims=True)


def segment_columns(p, segments, seg_cols):
    seg_cols[0:MAXLEN, :] = jnp.full((MAXLEN, 8), -1.0, F32)
    for start in range(0, p.length, QROWS):
        row = segments[:, start : start + QROWS].astype(F32)
        seg_cols[MAXLEN + start : MAXLEN + start + QROWS, :] = jnp.broadcast_to(row, (8, QROWS)).T


def attention_mask(r, start):
    keys = r.seg_cols[pl.ds(start, WINDOW), 0:1]
    queries = r.segments[:, pl.ds(start, QROWS)].astype(F32)
    key_at = lax.broadcasted_iota(jnp.int32, (WINDOW, QROWS), 0) - MAXLEN
    query_at = lax.broadcasted_iota(jnp.int32, (WINDOW, QROWS), 1)
    return jnp.where((key_at <= query_at) & (keys == queries), 0.0, MASKED_SCORE)


def pick_rows(p, routes, terms):
    picked = []
    for j in range(p.top):
        row = routes[j : j + 1, :]
        total = None
        for e in range(p.mixers):
            term = jnp.where(row == e, terms(e), 0.0)
            total = term if total is None else total + term
        picked.append(total)
    return picked


def spread_rows(p, routes, values, e):
    total = None
    for j in range(p.top):
        term = jnp.where(routes[j : j + 1, :] == e, values[j], 0.0)
        total = term if total is None else total + term
    return total


def pick_table(p, r, step, bb):
    return r.all_picks[bb, 8 * step : 8 * step + p.top, :]


def transposed(dst, src, first, start, stop, tile):
    for at in range(0, stop - start, tile):
        piece = src[:, start + at : start + at + tile]
        dst[first + at : first + at + tile, :] = piece.astype(F32).T.astype(BF)


def project_rows(p, r, head):
    start, stop = head * p.head_cols, (head + 1) * p.head_cols
    transposed(r.w_t, r.all_w, start, start, stop, LANES)


def project_gates(p, r, a, step, bb):
    table = pick_table(p, r, step, bb)
    logits = mm(r.router_row[...], a.nt[bb])
    chosen = pick_rows(p, table, lambda e: logits[e : e + 1, :])
    peak = functools.reduce(jnp.maximum, chosen)
    chosen = [jnp.exp(row - peak) for row in chosen]
    scale = 1.0 / sum(chosen)
    for j in range(p.top):
        a.gates[bb, j : j + 1, :] = chosen[j] * scale


def project(p, r, a, step, bb, head):
    sub = p.seq // QROWS
    if head == 0:
        project_gates(p, r, a, step, bb)
    table = pick_table(p, r, step, bb)
    values = mm(r.w_t[head * p.head_cols : (head + 1) * p.head_cols, :], a.nt[bb])
    for k in range(sub):
        lanes = slice(k * QROWS, (k + 1) * QROWS)
        queries = pick_rows(p, table[:, lanes], lambda e: values[e * HD : (e + 1) * HD, lanes])
        for j in range(p.top):
            a.qs[head, bb * sub + k, :, j * QROWS : (j + 1) * QROWS] = (queries[j] * (HD**-0.5)).astype(BF)
    at = pl.ds(aligned(MAXLEN + bb * p.seq, QROWS), p.seq)
    keys = values[p.mixers * HD : (p.mixers + 1) * HD, :]
    a.kt[head, :, at] = keys.astype(BF)
    a.vt[head, :, at] = values[(p.mixers + 1) * HD :, :].astype(BF)
    r.k_rows[head, at, :] = keys.T.astype(BF)


def attend(p, r, a, step, bb, head):
    sub = p.seq // QROWS
    for k in range(sub):
        i = bb * sub + k
        start = aligned(i * QROWS, QROWS)
        keys = pl.ds(start, WINDOW)
        bias = attention_mask(r, start)
        bias = jnp.concatenate([bias] * p.top, axis=1)
        scores = mm(r.k_rows[head, keys, :], a.qs[head, i]) + bias
        peak = jnp.max(scores, axis=0, keepdims=True)
        scores = jnp.exp(scores - peak)
        total = jnp.sum(scores, axis=0, keepdims=True)
        a.lse[i, head : head + 1, :] = peak + jnp.log(total)
        probs = (scores * (1.0 / total)).astype(BF)
        past = mm(a.vt[head, :, keys], probs)
        a.att[head, i] = past.astype(BF)
        at = pl.ds(k * QROWS, QROWS)
        table = r.all_picks[bb, 8 * step : 8 * step + p.top, at]
        weights = a.gates[bb, 0 : p.top, at]
        values = [past[:, j * QROWS : (j + 1) * QROWS] * weights[j : j + 1, :] for j in range(p.top)]
        for e in range(p.mixers):
            rows = slice(e * p.cols + head * HD, e * p.cols + (head + 1) * HD)
            a.mix[rows, pl.ds(start, QROWS)] = spread_rows(p, table, values, e).astype(BF)


def by_head(p):
    return [[head] for head in range(p.heads)]


def each_block(work, first, count):
    @pl.loop(0, count)
    def _(k):
        work(first + k)


def attention_forward(p, r, a, step, state, passes, before, ready, tick, out_ready, after):
    b, _ = place()
    y, c = b // 2, lax.rem(b, 2)
    a.nt[b] = (norm_parts(state)[1] * r.vectors[0:1, :].astype(F32)).T.astype(BF)
    gather = PackGather(p, a.nt, a.gather_sems)
    gather.begin()
    r.k_rows[:, 0:MAXLEN, :] = jnp.zeros((p.heads, MAXLEN, HD), BF)
    a.kt[:, :, 0:MAXLEN] = jnp.zeros((p.heads, HD, MAXLEN), BF)
    a.vt[:, :, 0:MAXLEN] = jnp.zeros((p.heads, HD, MAXLEN), BF)
    before(gather)
    shares = PackSum(p, r, a.sum_sems)

    def branch(bb):
        return mm(r.all_w[:, p.qkv :], a.mix[:, pl.ds(aligned(bb * p.seq, p.seq), p.seq)])

    def attends(bb, heads):
        for head in heads:
            attend(p, r, a, step, bb, head)
        tick()

    def projects(bb, heads):
        for head in heads:
            project(p, r, a, step, bb, head)

    for heads in passes:
        final = heads[-1] == p.heads - 1
        if heads[0] == 0:
            projects(b, heads)
            gather.finish_near()
            projects(2 * y + 1 - c, heads)
            tick()
            attends(2 * y + 1, heads)
            gather.finish_far()
            for s in range(1, p.chips):
                each_block(lambda bb: projects(bb, heads), 2 * turn(y, s, p.chips), 2)
            tick()
        else:
            ready(heads[0])
            each_block(lambda bb: projects(bb, heads), 0, p.blk)
            attends(2 * y + 1, heads)
        for s in range(1, p.chips):
            yy = turn(y, s, p.chips)
            attends(2 * yy + 1 - c, heads)
            if final:
                if s == 1:
                    out_ready()
                shares.give(s, branch(2 * yy + 1 - c))
            attends(2 * yy + c, heads)
            if final:
                shares.pass_on(s, branch(2 * yy + c))
        if final:
            after()
        attends(2 * y, heads)
    shares.give(0, branch(2 * y + 1 - c))
    total = shares.total(branch(b))
    gather.end()
    return total


def attention_grads(p, r, a, step, bb):
    sub = p.seq // QROWS
    table = pick_table(p, r, step, bb)
    weights = a.gates[bb, 0 : p.top, :]
    values = mm(r.wo[...], r.gt[bb])
    for k in range(sub):
        lanes = slice(k * QROWS, (k + 1) * QROWS)
        here = table[:, lanes]
        grads = [None] * p.top
        for head in range(p.heads):
            picked = pick_rows(
                p, here, lambda e: values[e * p.cols + head * HD : e * p.cols + (head + 1) * HD, lanes]
            )
            for j in range(p.top):
                slot = slice(j * QROWS, (j + 1) * QROWS)
                past = a.att[head, bb * sub + k, :, slot].astype(F32)
                dot = jnp.sum(picked[j] * past, axis=0, keepdims=True)
                grads[j] = dot if head == 0 else grads[j] + dot
                gate = weights[j : j + 1, lanes]
                r.means[bb * sub + k, head : head + 1, slot] = dot * gate
                a.att[head, bb * sub + k, :, slot] = (picked[j] * gate).astype(BF)
        mean = sum(weights[j : j + 1, lanes] * grads[j] for j in range(p.top))
        back = [weights[j : j + 1, lanes] * (grads[j] - mean) for j in range(p.top)]
        for e in range(p.mixers):
            r.dlog[bb, e : e + 1, lanes] = spread_rows(p, here, back, e)


def probs_at(p, i, head):
    across = p.ff // (p.top * QROWS)
    each = p.slots // WINDOW * across
    unit = i * p.heads + head
    rows = aligned(lax.rem(unit, each) // across * WINDOW, QROWS)
    lanes = aligned(lax.rem(unit, across) * (p.top * QROWS), QROWS)
    return unit // each, pl.ds(rows, WINDOW), pl.ds(lanes, p.top * QROWS)


def attention_probs(p, r, a):
    @pl.loop(0, p.blocks)
    def _(i):
        start = aligned(i * QROWS, QROWS)
        bias = attention_mask(r, start)
        bias = jnp.concatenate([bias] * p.top, axis=1)
        for head in range(p.heads):
            scores = mm(r.k_rows[head, pl.ds(start, WINDOW), :], a.qs[head, i]) + bias
            plane, rows, lanes = probs_at(p, i, head)
            r.keep[plane, rows, lanes] = jnp.exp(scores - a.lse[i, head : head + 1, :]).astype(BF)


def attention_rows(p, r, a, keys):
    @pl.loop(0, (p.length + MAXLEN) // QROWS)
    def _(k):
        at = pl.ds(aligned(k * QROWS, QROWS), QROWS)
        for head in range(p.heads):
            r.v_rows[head, at, :] = a.vt[head, :, at].astype(F32).T.astype(BF)
            if keys:
                r.k_rows[head, at, :] = a.kt[head, :, at].astype(F32).T.astype(BF)


def attend_back(p, r, a, step, bb, head):
    sub = p.seq // QROWS
    for k in range(sub):
        i = bb * sub + k
        start = aligned(i * QROWS, QROWS)
        keys = pl.ds(start, WINDOW)
        plane, rows, lanes = probs_at(p, i, head)
        probs = r.keep[plane, rows, lanes]
        grads = a.att[head, i]
        mean = r.means[i, head : head + 1, :]
        dscores = (probs.astype(F32) * (mm(r.v_rows[head, keys, :], grads) - mean)).astype(BF)
        r.dvt[head, :, keys] += mm_nt(grads, probs)
        r.dkt[head, :, keys] += mm_nt(a.qs[head, i], dscores)
        merged = mm(a.kt[head, :, keys], dscores) * (HD**-0.5)
        at = pl.ds(k * QROWS, QROWS)
        table = r.all_picks[bb, 8 * step : 8 * step + p.top, at]
        values = [merged[:, j * QROWS : (j + 1) * QROWS] for j in range(p.top)]
        for e in range(p.mixers):
            first = head * p.head_cols + e * HD
            r.dall[first : first + HD, pl.ds(start, QROWS)] = spread_rows(p, table, values, e).astype(BF)


def attention_backward(p, r, a, step, state, grad, passes, before, middle, head_done):
    b, _ = place()
    y, c = b // 2, lax.rem(b, 2)
    r.gt[b] = grad.T.astype(BF)
    gather = PackGather(p, r.gt, a.back_gather_sems)
    gather.begin()
    r.dkt[...] = jnp.zeros_like(r.dkt)
    r.dvt[...] = jnp.zeros_like(r.dvt)
    before()
    router_col = r.router_row[...].astype(F32).T.astype(BF)

    def key_value_grads(lanes, past):
        for head in range(p.heads):
            first = head * p.head_cols + p.mixers * HD
            r.dall[first : first + HD, lanes] = r.dkt[head, :, past].astype(BF)
            r.dall[first + HD : first + 2 * HD, lanes] = r.dvt[head, :, past].astype(BF)

    def branch(bb):
        lanes = pl.ds(aligned(bb * p.seq, p.seq), p.seq)
        key_value_grads(lanes, pl.ds(aligned(bb * p.seq + MAXLEN, QROWS), p.seq))
        return mm(r.all_w[:, : p.qkv], r.dall[:, lanes]) + mm(router_col, r.dlog[bb].astype(BF))

    shares = PackSum(p, r, a.back_sum_sems)
    def backs(bb, heads):
        for head in heads:
            attend_back(p, r, a, step, bb, head)

    attention_grads(p, r, a, step, b)
    gather.finish_near()
    attention_grads(p, r, a, step, 2 * y + 1 - c)
    backs(2 * y, range(p.heads))
    gather.finish_far()
    for s in range(1, p.chips):
        each_block(lambda bb: attention_grads(p, r, a, step, bb), 2 * turn(y, s, p.chips), 2)
    middle()
    for heads in passes:
        final = heads[-1] == p.heads - 1
        for s in range(1, p.chips):
            each_block(lambda bb: backs(bb, heads), 2 * turn(y, s, p.chips), 2)
        if final:
            for s in range(1, p.chips):
                yy = turn(y, s, p.chips)
                shares.give(s, branch(2 * yy + 1 - c))
                shares.pass_on(s, branch(2 * yy + c))
        backs(2 * y + 1, heads)
        if not final:
            key_value_grads(slice(0, p.length), slice(MAXLEN, MAXLEN + p.length))
            head_done(heads[-1])
    shares.give(0, branch(2 * y + 1 - c))
    own = branch(b)
    head_done(p.heads - 1)
    router = sum(mm_nt(r.dlog[bb].astype(BF), a.nt[bb]) for bb in range(p.blk))
    grad_n = shares.total(own).T
    gather.end()
    back, gain = norm_back(state, r.vectors[0:1, :].astype(F32), grad_n)
    return grad + back, gain, router


def attention_weight_grads(p, r, a, start, stop, add):
    for first in range(start, stop, 2 * LANES):
        tile = min(2 * LANES, stop - first)
        total = None
        for bb in range(p.blk):
            lanes = slice(bb * p.seq, (bb + 1) * p.seq)
            if first < p.qkv:
                term = mm_nt(a.nt[bb], r.dall[first : first + tile, lanes])
            else:
                term = mm_nt(r.gt[bb], a.mix[first - p.qkv : first - p.qkv + tile, lanes])
            total = term if total is None else total + term
        at = slice(first, first + tile)
        r.grad_w[:, at] = (r.grad_w[:, at].astype(F32) + total if add else total).astype(BF)


def own_lane(p):
    b, d = place()
    mine = d * p.local + b // p.group
    return jnp.where(lax.broadcasted_iota(jnp.int32, (1, LANES), 1) == mine, 1.0, 0.0)


def slot_gates(p, r, rows, pair):
    own = own_lane(p)
    logits = mm_nt(rows, r.router[...])
    return 1.0 / (1.0 + jnp.exp(jnp.sum(logits * (pair - 2.0 * own), axis=-1, keepdims=True)))


def gelu_both(inner):
    half = 0.5 * (1.0 + lax.erf(inner * 0.7071067811865476))
    slope = half + inner * jnp.exp(-0.5 * inner * inner) * 0.3989422804014327
    return inner * half, slope


def fill_router(p, r):
    r.router[...] = jnp.zeros_like(r.router)
    r.router[0 : p.experts, :] = r.router_in[...]


def slot_groups(p):
    per = max(1, p.experts // (2 if p.slots <= 768 else 4))
    return [(pl.ds(first * p.cap, per * p.cap), range(first, first + per)) for first in range(0, p.experts, per)]


def expert_output(p, r, rows, at, keep):
    total = None
    for start in range(0, p.ff, p.tile):
        lanes = slice(start, start + p.tile)
        inner = mm(rows, r.all_in[:, lanes])
        if keep:
            act, slope = gelu_both(inner)
            act = act.astype(BF)
            r.keep[0, at, lanes] = act
            r.keep[1, at, lanes] = slope.astype(BF)
        else:
            act = (inner * (0.5 * (1.0 + lax.erf(inner * 0.7071067811865476)))).astype(BF)
        term = mm(act, r.all_back[lanes, :])
        total = term if total is None else total + term
    return total


def expert_keep(p, r, rows, at):
    for start in range(0, p.ff, p.tile):
        lanes = slice(start, start + p.tile)
        act, slope = gelu_both(mm(rows, r.all_in[:, lanes]))
        r.keep[0, at, lanes] = act.astype(BF)
        r.keep[1, at, lanes] = slope.astype(BF)


def expert_input_grad(p, r, at, u, rows, out, pair, dst):
    gate = slot_gates(p, r, rows, pair)
    grads = (u * gate).astype(BF)
    r.u_in[at, :] = grads
    coeff = gate * (1.0 - gate) * jnp.sum(u * out, axis=-1, keepdims=True) * (2.0 * own_lane(p) - pair)
    coeff = coeff.astype(BF)
    r.coeff[at, :] = coeff
    dst[at, :] = mm(coeff, r.router[...]).astype(BF)
    total = None
    for start in range(0, p.ff, p.tile):
        lanes = slice(start, start + p.tile)
        inner = (mm_nt(grads, r.all_back[lanes, :]) * r.keep[1, at, lanes].astype(F32)).astype(BF)
        r.keep[1, at, lanes] = inner
        term = mm_nt(inner, r.all_in[:, lanes])
        total = term if total is None else total + term
    dst[at, :] = (total + dst[at, :].astype(F32)).astype(BF)


def expert_weight_grads(p, r, arrived, add):
    r.arrived_t[...] = arrived[...].astype(F32).T.astype(BF)
    for start in range(0, p.ff, p.tile // 2):
        lanes = slice(start, start + p.tile // 2)
        term = mm(r.keep[0, :, lanes].astype(F32).T.astype(BF), r.u_in[...])
        r.grad_back[lanes, :] = (r.grad_back[lanes, :].astype(F32) + term if add else term).astype(BF)
        term = mm(r.arrived_t[...], r.keep[1, :, lanes])
        r.grad_in[:, lanes] = (r.grad_in[:, lanes].astype(F32) + term if add else term).astype(BF)
    return mm(r.coeff[...].astype(F32).T.astype(BF)[0 : p.experts], arrived[...])


def slot_tables(p, r):
    b, d = place()
    e = b // p.group
    place_in = lax.broadcasted_iota(jnp.int32, (p.experts, 1), 0)
    ids = lax.rem(d + lax.rem(place_in, p.dp), p.dp) * p.local + lax.rem(e + place_in // p.dp, p.local)
    earlier = (
        lax.broadcasted_iota(jnp.int32, (p.seq, p.seq), 0) < lax.broadcasted_iota(jnp.int32, (p.seq, p.seq), 1)
    ).astype(BF)
    slot_ids = lax.broadcasted_iota(jnp.int32, (p.cap, p.seq), 0).astype(F32)
    r.pair_out[...] = jnp.zeros_like(r.pair_out)
    for step in range(2):
        one = r.routes[8 * step + p.top : 8 * step + p.top + 1, :]
        two = r.routes[8 * step + p.top + 1 : 8 * step + p.top + 2, :]
        member = jnp.where((one == ids) | (two == ids), 1.0, 0.0)
        rank = jnp.where(member > 0.5, mm(member.astype(BF), earlier), -1.0)
        both = jnp.broadcast_to((one + two).astype(F32), (8, p.seq)).astype(BF)
        for s in range(p.experts):
            table = jnp.where(rank[s : s + 1, :] == slot_ids, 1.0, 0.0).astype(BF)
            r.disp[step, pl.ds(s * p.cap, p.cap), :] = table
            r.pair_out[s, step : step + 1, 0 : p.cap] = mm_nt(both, table)[0:1]
        r.comb[step] = r.disp[step].astype(F32).T.astype(BF)
    r.pair_in[0] = r.pair_out[0]
    return [
        send(r.pair_out.at[s], r.pair_in.at[s], (r.pair_s, r.pair_r), s, slot_peer(p, s)) for s in range(1, p.experts)
    ]


def slot_pairs(p, r):
    b, d = place()
    mine = (d * p.local + b // p.group).astype(F32)
    lanes = lax.broadcasted_iota(jnp.int32, (p.cap, LANES), 1).astype(F32)
    for step in range(2):
        totals = r.pair_in[:, step, :].T
        for s in range(p.experts):
            other = totals[0 : p.cap, s : s + 1] - mine
            both = jnp.where(lanes == mine, 1.0, 0.0) + jnp.where(lanes == other, 1.0, 0.0)
            r.pair[step, pl.ds(s * p.cap, p.cap), :] = both.astype(BF)


def forward_kernel(p, r):
    b, d = place()
    z, x = d // p.lo, lax.rem(d, p.lo)
    e, g = b // p.group, lax.rem(b, p.group)
    own_rows = r.weight_key.shape[0]
    in_rows, back_rows = r.weight_in.shape[1], r.weight_back.shape[1]

    def w_at(index, part):
        return r.all_w.at[pl.ds(aligned(index * own_rows, own_rows), own_rows), p.parts[part]]

    def in_at(index):
        return r.all_in.at[pl.ds(aligned(index * in_rows, in_rows), in_rows)]

    def back_at(index):
        return r.all_back.at[pl.ds(aligned(index * back_rows, back_rows), back_rows)]

    peers = pack_peers(p) + slot_peers(p) + dp_peers(p) + expert_peers(p)
    greet(peers)
    own = pl.ds(aligned(d * own_rows, own_rows), own_rows)
    for head in range(p.heads):
        mine = slice(head * HD, (head + 1) * HD)
        shares = [r.weight_query[k, :, mine] for k in range(p.mixers)]
        shares += [r.weight_key[:, mine], r.weight_value[:, mine]]
        r.all_w[own, p.parts[head]] = jnp.concatenate(shares, axis=1)
    for k in range(p.mixers):
        r.all_w[own, p.qkv + k * p.cols : p.qkv + (k + 1) * p.cols] = r.weight_out[k]
    fill_router(p, r)
    segment_columns(p, r.segments, r.seg_cols)
    answered(peers)
    last = p.hi - 1

    def hop(part, k, up):
        rows = w_at((z - k if up else z + k) * p.lo + x, part)
        slot = (2 * part + (0 if up else 1)) * last + k
        return link(rows, rows, (r.hi_s, r.hi_r), slot, (b, (z + 1 if up else z - 1) * p.lo + x))

    def arrival(part, k, up):
        rows = w_at((z - 1 - k if up else z + 1 + k) * p.lo + x, part)
        return link(rows, rows, (r.hi_s, r.hi_r), (2 * part + (0 if up else 1)) * last + k, (b, d))

    def cross(part, source, t):
        rows = w_at(source * p.lo + x, part)
        slot = (part * p.hi + source) * (p.lo - 1) + t - 1
        return link(rows, rows, (r.lo_s, r.lo_r), slot, (b, z * p.lo + turn(x, t, p.lo)))

    def goes(k, up):
        return (z >= k) & (z < last) if up else (z + k <= last) & (z > 0)

    def comes(k, up):
        return z >= k + 1 if up else z + k + 1 <= last

    def w_begin(part):
        for up in (True, False):
            pl.when(goes(0, up))(lambda: hop(part, 0, up).start())
        for t in range(1, p.lo):
            cross(part, z, t).start()

    def w_pass(part, k):
        for up in (True, False):

            @pl.when(comes(k, up))
            def _():
                arrival(part, k, up).wait_recv()
                if k + 1 < last:
                    pl.when(goes(k + 1, up))(lambda: hop(part, k + 1, up).start())
                for t in range(1, p.lo):
                    cross(part, z - 1 - k if up else z + 1 + k, t).start()

    def w_finish(part):
        for source in range(p.hi):
            for t in range(1, p.lo):
                rows = w_at(source * p.lo + turn(x, -t, p.lo), part)
                slot = (part * p.hi + source) * (p.lo - 1) + t - 1
                link(rows, rows, (r.lo_s, r.lo_r), slot, (b, d)).wait_recv()

    def w_end():
        for part in range(p.heads + 1):
            for k in range(last):
                for up in (True, False):
                    pl.when(goes(k, up))(lambda: hop(part, k, up).wait_send())
            for source in range(p.hi):
                for t in range(1, p.lo):
                    cross(part, source, t).wait_send()

    local, over, beside = [], {}, []

    def experts_begin():
        for s in range(1, p.local):
            to = turn(e, s, p.local)
            peer = (to * p.group + g, d)
            over[s, 0] = send(r.weight_in.at[to], in_at(b), (r.wide_s, r.wide_r), 2 * s - 2, peer)
            over[s, 1] = send(r.weight_back.at[to], back_at(b), (r.wide_s, r.wide_r), 2 * s - 1, peer)
        for t in range(1, p.group):
            peer = (e * p.group + turn(g, t, p.group), d)
            beside.append(send(r.weight_in.at[e], in_at(b), (r.near_s, r.near_r), 2 * t - 2, peer))
            beside.append(send(r.weight_back.at[e], back_at(b), (r.near_s, r.near_r), 2 * t - 1, peer))

    def experts_pass():
        for s in range(1, p.local):
            source = turn(e, -s, p.local) * p.group + g
            for which, rows in ((0, in_at(source)), (1, back_at(source))):
                over[s, which].wait_recv()
                for t in range(1, p.group):
                    k = (s * (p.group - 1) + t - 1) * 2 + which
                    peer = (e * p.group + turn(g, t, p.group), d)
                    beside.append(send(rows, rows, (r.near_s, r.near_r), k, peer))

    tables = []
    saves = []

    w_begin(0)
    for step in range(2):
        r.routes[8 * step : 8 * step + p.top, :] = r.attention_routes[step]
        r.routes[8 * step + p.top : 8 * step + 6, :] = r.expert_routes[step]
        r.routes[8 * step + 6 : 8 * step + 8, :] = jnp.zeros((2, p.seq), jnp.int32)
    r.all_picks[b] = r.routes[...]
    picks = PackGather(p, r.all_picks, r.picks_sems)
    picks.begin()
    state = r.x[...].astype(F32)

    def before(gather):
        local.extend(moves(r, [(r.weight_in.at[e], in_at(b)), (r.weight_back.at[e], back_at(b))]))
        tables.extend(slot_tables(p, r))
        w_pass(0, 0)
        w_pass(0, 1)
        gather.finish_far()
        picks.finish_far()
        experts_begin()
        for k in range(2, last):
            w_pass(0, k)
        w_begin(1)
        w_finish(0)
        project_rows(p, r, 0)
        for part in range(1, p.heads + 1):
            for k in range(last):
                waiting.append((part, k))

    waiting = []

    def tick():
        if waiting:
            part, k = waiting.pop(0)
            w_pass(part, k)
            if k == last - 1 and part < p.heads:
                w_begin(part + 1)

    def drain(part):
        while waiting and waiting[0][0] <= part:
            tick()
        w_finish(part)

    def ready(head):
        drain(head)
        project_rows(p, r, head)

    def out_ready():
        drain(p.heads)

    def after():
        saves.extend(moves(r, [(r.all_w, r.all_w_out), (r.disp, r.disp_out), (r.comb, r.comb_out)]))
        experts_pass()

    total = attention_forward(p, r, r.a, 0, state, by_head(p), before, ready, tick, out_ready, after)
    middle = state + total.T
    r.middle[...] = middle
    m = (norm_parts(middle)[1] * r.vectors[1:2, :].astype(F32)).astype(BF)
    r.outgoing[...] = mm(r.disp[0], m).astype(BF)
    there = slot_sends(p, r.outgoing, r.arrived, (r.go_s, r.go_r), slot_peer)
    saves.extend(moves(r, [(getattr(r.a, k), getattr(r, k + "_out")) for k in SAVED]))
    for copy in tables:
        copy.wait_recv()
    slot_pairs(p, r)
    for copy in beside:
        copy.wait_recv()
    arrive(local)
    saves.extend(moves(r, [(r.all_in, r.all_in_out), (r.all_back, r.all_back_out), (r.pair, r.pair_end)]))
    back = {}
    for at, sources in slot_groups(p):
        receive(there, sources)
        rows = r.arrived[at, :]
        out = expert_output(p, r, rows, at, False)
        r.produced[at, :] = out.astype(BF)
        r.ret_out[at, :] = (out * slot_gates(p, r, rows, r.pair[0, at, :].astype(F32))).astype(BF)
        for s in sources:
            if s:
                back[s] = slot_send(p, r.ret_out, r.ret_in, (r.ret_s, r.ret_r), s, slot_source(p, s))
    r.ret_in[0 : p.cap, :] = r.ret_out[0 : p.cap, :]
    receive(back, range(p.experts))
    r.first[...] = r.middle[...] + mm(r.comb[0], r.ret_in[...])
    sent(there)
    sent(back)
    sent(tables)
    sent(beside)
    w_end()
    sent(over)
    picks.end()
    arrive(saves)


def turn_kernel(p, r):
    peers = pack_peers(p) + slot_peers(p)
    greet(peers)
    early = moves(
        r, [(r.disp_in.at[1], r.disp), (r.all_w_in, r.all_w), (r.comb_in.at[1], r.comb), (r.pair_in.at[1], r.pair)]
    )
    fill_router(p, r)
    weights = moves(r, [(r.all_in_in, r.all_in), (r.all_back_in, r.all_back)])
    first = r.first[...]
    stop = 1.0 / (1.0 + jnp.exp(-jnp.sum(first * r.vectors[2:3, :].astype(F32), axis=-1, keepdims=True)))
    cot = r.cot[...].astype(F32)
    segment_columns(p, r.segments, r.seg_cols)
    answered(peers)
    there_u, saves = {}, []

    def before(gather):
        arrive(early)
        r.u_out[...] = mm(r.disp[...], ((1.0 - stop) * cot).astype(BF)).astype(BF)
        there_u.update(slot_sends(p, r.u_out, r.u_in, (r.u_s, r.u_r), slot_peer))
        for head in range(p.heads):
            project_rows(p, r, head)

    def nothing(*_):
        pass

    total = attention_forward(p, r, r.a, 1, first, [range(p.heads)], before, nothing, nothing, nothing, nothing)
    middle = first + total.T
    r.middle[...] = middle
    m = (norm_parts(middle)[1] * r.vectors[1:2, :].astype(F32)).astype(BF)
    r.outgoing[...] = mm(r.disp[...], m).astype(BF)
    there = slot_sends(p, r.outgoing, r.arrived, (r.go_s, r.go_r), slot_peer)
    transposed(r.wo, r.all_w, 0, p.qkv, p.all_cols, LANES)
    attention_rows(p, r, r.a, False)
    arrive(weights)
    sent(there_u)
    ret_out = r.u_out
    back, back_out = {}, {}
    for at, sources in slot_groups(p):
        receive(there_u, sources)
        receive(there, sources)
        rows = r.arrived[at, :]
        pair = r.pair[at, :].astype(F32)
        out = expert_output(p, r, rows, at, True)
        ret_out[at, :] = (out * slot_gates(p, r, rows, pair)).astype(BF)
        expert_input_grad(p, r, at, r.u_in[at, :].astype(F32), rows, out, pair, r.gret_out)
        for s in sources:
            if s:
                back[s] = slot_send(p, r.gret_out, r.gret_in, (r.gret_s, r.gret_r), s, slot_source(p, s))
    r.gret_in[0 : p.cap, :] = r.gret_out[0 : p.cap, :]
    r.ret_in[0 : p.cap, :] = ret_out[0 : p.cap, :]
    r.grad_router[...] = expert_weight_grads(p, r, r.arrived, False)
    saves.extend(moves(r, [(r.grad_in, r.grad_in_out), (r.grad_back, r.grad_back_out)]))
    attention_probs(p, r, r.a)
    receive(back, range(p.experts))
    step_back, gain_two = norm_back(r.middle[...], r.vectors[1:2, :].astype(F32), mm(r.comb[...], r.gret_in[...]))
    r.grad_gain_two[...] = gain_two
    grad_middle = (1.0 - stop) * cot + step_back

    def before_back():
        for s in range(1, p.experts):
            back_out[s] = slot_send(p, ret_out, r.ret_in, (r.ret_s, r.ret_r), s, slot_source(p, s))

    def head_done(head):
        if head == p.heads - 1:
            for part in p.parts:
                attention_weight_grads(p, r, r.a, part.start, part.stop, False)

    grad, gain_one, router = attention_backward(
        p, r, r.a, 1, first, grad_middle, [range(p.heads)], before_back, lambda: None, head_done
    )
    saves.extend(moves(r, [(r.grad_w, r.grad_w_out)]))
    r.grad_gain_one[...] = gain_one
    r.grad_mixer[...] = router
    receive(back_out, range(p.experts))
    second = r.middle[...] + mm(r.comb[...], r.ret_in[...])
    r.result[...] = (stop * first + (1.0 - stop) * second).astype(BF)
    grad_stop = jnp.sum(cot * (first - second), axis=-1, keepdims=True)
    coeff = grad_stop * stop * (1.0 - stop)
    r.grad_halt[...] = jnp.sum(coeff * first, axis=0, keepdims=True)
    r.grad_first[...] = stop * cot + coeff * r.vectors[2:3, :].astype(F32) + grad
    for copies in (there, back, back_out):
        sent(copies)
    arrive(saves)


def backward_kernel(p, r):
    b, d = place()
    z, x = d // p.lo, lax.rem(d, p.lo)
    y, c = b // 2, lax.rem(b, 2)
    e, g = b // p.group, lax.rem(b, p.group)
    rows = r.out_w.shape[0]
    in_rows, back_rows = r.out_in.shape[1], r.out_back.shape[1]
    peers = pack_peers(p) + slot_peers(p) + dp_peers(p) + expert_peers(p)
    greet(peers)
    early = moves(
        r,
        [
            (r.disp_in.at[0], r.disp),
            (r.pair_in.at[0], r.pair),
            (r.arrived_in, r.arrived),
            (r.all_in_in, r.all_in),
            (r.all_back_in, r.all_back),
            (r.produced_in, r.produced),
        ],
    )
    later = moves(
        r, [(r.grad_in_in, r.grad_in), (r.grad_back_in, r.grad_back), (r.comb_in.at[0], r.comb), (r.all_w_in, r.all_w)]
    )
    later += moves(r, [(r.grad_w_in, r.grad_w)])
    later += moves(r, [(getattr(r, k + "_in"), getattr(r.a, k)) for k in SAVED])
    fill_router(p, r)
    grad_first = r.grad_first[...]
    early[0].wait()
    r.u_out[...] = mm(r.disp[...], grad_first.astype(BF)).astype(BF)
    answered(peers)
    there = slot_sends(p, r.u_out, r.u_in, (r.u_s, r.u_r), slot_peer)
    arrive(early[1:])
    for at, _ in slot_groups(p):
        expert_keep(p, r, r.arrived[at, :], at)
    segment_columns(p, r.segments, r.seg_cols)
    arrive(later)
    attention_rows(p, r, r.a, True)
    transposed(r.wo, r.all_w, 0, p.qkv, p.all_cols, LANES)
    back = {}
    for at, sources in slot_groups(p):
        receive(there, sources)
        pair = r.pair[at, :].astype(F32)
        out = r.produced[at, :].astype(F32)
        expert_input_grad(p, r, at, r.u_in[at, :].astype(F32), r.arrived[at, :], out, pair, r.produced)
        for s in sources:
            if s:
                back[s] = slot_send(p, r.produced, r.gret_in, (r.gret_s, r.gret_r), s, slot_source(p, s))
    r.gret_in[0 : p.cap, :] = r.produced[0 : p.cap, :]
    r.grad_router[...] = expert_weight_grads(p, r, r.arrived, True)

    def row_block(ref, index, size, lanes=slice(None)):
        return ref.at[pl.ds(aligned(index * size, size), size), lanes]

    near = {}
    for k in range(p.local):
        to = turn(e, k + 1, p.local)
        for t in range(1, p.group):
            member = turn(g, t, p.group)
            slot = k * (p.group - 1) + t - 1
            peer = (e * p.group + member, d)
            owner = to * p.group + member
            near[k, t, 0] = send(
                row_block(r.grad_in, owner, in_rows), r.in_near.at[slot], (r.near_s, r.near_r), 2 * slot, peer
            )
            near[k, t, 1] = send(
                row_block(r.grad_back, owner, back_rows), r.back_near.at[slot], (r.near_s, r.near_r), 2 * slot + 1, peer
            )
    attention_probs(p, r, r.a)
    receive(back, range(p.experts))
    step_back, gain_two = norm_back(r.middle[...], r.vectors[1:2, :].astype(F32), mm(r.comb[...], r.gret_in[...]))
    grad_middle = grad_first + step_back
    wide, lo_copies, hi_copies = {}, {}, {}

    def experts_wide():
        for k in range(p.local):
            to = turn(e, k + 1, p.local)
            total_in = row_block(r.grad_in, to * p.group + g, in_rows)[...].astype(F32)
            total_back = row_block(r.grad_back, to * p.group + g, back_rows)[...].astype(F32)
            for t in range(1, p.group):
                slot = k * (p.group - 1) + t - 1
                near[k, t, 0].wait_recv()
                near[k, t, 1].wait_recv()
                total_in = total_in + r.in_near[slot].astype(F32)
                total_back = total_back + r.back_near[slot].astype(F32)
            if k < p.local - 1:
                r.in_far_out[k] = total_in.astype(BF)
                r.back_far_out[k] = total_back.astype(BF)
                peer = (to * p.group + g, d)
                wide[k, 0] = send(r.in_far_out.at[k], r.in_far.at[k], (r.wide_s, r.wide_r), 2 * k, peer)
                wide[k, 1] = send(r.back_far_out.at[k], r.back_far.at[k], (r.wide_s, r.wide_r), 2 * k + 1, peer)
            else:
                r.out_in[e] = total_in.astype(BF)
                r.out_back[e] = total_back.astype(BF)

    parts = p.parts

    def sum_begin(part):
        for k in range(p.hi):
            to = turn(z, k + 1, p.hi)
            for t in range(1, p.lo):
                slot = k * (p.lo - 1) + t - 1
                xx = turn(x, t, p.lo)
                lo_copies[part, k, t] = send(
                    row_block(r.grad_w, to * p.lo + xx, rows, parts[part]),
                    r.w_lo.at[slot, :, parts[part]],
                    (r.lo_s, r.lo_r),
                    part * p.hi * (p.lo - 1) + slot,
                    (b, z * p.lo + xx),
                )

    def sum_pass(part):
        lanes = parts[part]
        for k in range(p.hi):
            to = turn(z, k + 1, p.hi)
            total = row_block(r.grad_w, to * p.lo + x, rows, lanes)[...].astype(F32)
            for t in range(1, p.lo):
                lo_copies[part, k, t].wait_recv()
                total = total + r.w_lo[k * (p.lo - 1) + t - 1, :, lanes].astype(F32)
            if k < p.hi - 1:
                r.w_hi_out[k, :, lanes] = total.astype(BF)
                hi_copies[part, k] = send(
                    r.w_hi_out.at[k, :, lanes],
                    r.w_hi.at[k, :, lanes],
                    (r.hi_s, r.hi_r),
                    part * (p.hi - 1) + k,
                    (b, to * p.lo + x),
                )
            else:
                r.out_w[:, lanes] = total

    def sum_finish(part):
        lanes = parts[part]
        total = r.out_w[:, lanes]
        for k in range(p.hi - 1):
            hi_copies[part, k].wait_recv()
            total = total + r.w_hi[k, :, lanes].astype(F32)
        r.out_w[:, lanes] = total

    def middle():
        experts_wide()
        attention_weight_grads(p, r, r.a, p.qkv, p.all_cols, True)
        sum_begin(p.heads)

    def head_done(head):
        attention_weight_grads(p, r, r.a, parts[head].start, parts[head].stop, True)
        sum_begin(head)
        sum_pass(p.heads if head == 0 else head - 1)

    grad, gain_one, router = attention_backward(
        p, r, r.a, 0, r.x[...].astype(F32), grad_middle, by_head(p), lambda: None, middle, head_done
    )
    small = r.out_small
    small[...] = jnp.zeros_like(small)
    small[0:1, :] = r.gain_one_before[...] + gain_one
    small[1:2, :] = r.gain_two_before[...] + gain_two
    small[2:3, :] = r.halt_before[...]
    small[8 : 8 + p.mixers, :] = r.mixer_before[...] + router
    small[8 + p.mixers :, :] = r.router_before[...] + r.grad_router[...]
    tiny = []
    axes = (
        (2, c, lambda t: (2 * y + turn(c, t, 2), d)),
        (p.chips, y, lambda t: (2 * turn(y, t, p.chips) + c, d)),
        (p.lo, x, lambda t: (b, z * p.lo + turn(x, t, p.lo))),
        (p.hi, z, lambda t: (b, turn(z, t, p.hi) * p.lo + x)),
    )

    def tiny_begin(axis):
        size, index, peer = axes[axis]
        base = sum(entry[0] for entry in axes[:axis])
        r.all_small[base + index] = small[...]
        at = r.all_small.at[base + index]
        for t in range(1, size):
            tiny.append(send(at, at, (r.tiny_s, r.tiny_r), base + t - 1, peer(t)))

    def tiny_finish(axis):
        size = axes[axis][0]
        base = sum(entry[0] for entry in axes[:axis])
        for copy in tiny[len(tiny) - (size - 1) :]:
            copy.wait_recv()
        total = r.all_small[base]
        for k in range(1, size):
            total = total + r.all_small[base + k]
        small[...] = total

    tiny_begin(0)
    r.input_grad[...] = grad.astype(BF)
    tiny_finish(0)
    tiny_begin(1)
    sum_pass(p.heads - 1)
    tiny_finish(1)
    tiny_begin(2)
    for k in range(p.local - 1):
        source = turn(e, -(k + 1), p.local)
        wide[k, 0].wait_recv()
        wide[k, 1].wait_recv()
        r.out_in[source] = r.in_far[k]
        r.out_back[source] = r.back_far[k]
    tiny_finish(2)
    tiny_begin(3)
    sum_finish(p.heads)
    for part in range(p.heads - 1):
        sum_finish(part)
    tiny_finish(3)
    sum_finish(p.heads - 1)
    for copies in (there, back, near, wide, lo_copies, hi_copies, tiny):
        sent(copies)


def output_kernel(p, r):
    cols = p.cols
    r.result_out[...] = r.result[...]
    r.input_grad_out[...] = r.input_grad[...]
    r.in_out[...] = r.out_in[...].astype(F32)
    r.back_out[...] = r.out_back[...].astype(F32)
    for e in range(p.mixers):
        heads = [h * p.head_cols + e * HD for h in range(p.heads)]
        r.query_out[e] = jnp.concatenate([r.out_w[:, at : at + HD] for at in heads], axis=1)
        start = p.qkv + e * cols
        r.out_out[e] = r.out_w[:, start : start + cols]
    heads = [h * p.head_cols + p.mixers * HD for h in range(p.heads)]
    r.key_out[...] = jnp.concatenate([r.out_w[:, at : at + HD] for at in heads], axis=1)
    r.value_out[...] = jnp.concatenate([r.out_w[:, at + HD : at + 2 * HD] for at in heads], axis=1)
    r.gain_one_out[...] = r.small[0:1, :]
    r.gain_two_out[...] = r.small[1:2, :]
    r.halt_out[...] = r.small[2:3, :]
    r.mixer_out[...] = r.small[8 : 8 + p.mixers, :]
    r.router_out[...] = r.small[8 + p.mixers :, :]


SAVED = ("nt", "qs", "kt", "vt", "lse", "att", "mix", "gates")


def dma(name, size):
    sem = pltpu.SemaphoreType.DMA((max(1, size),))
    return {name + "_s": sem, name + "_r": sem}


def pack_sems(p, name):
    sizes = (p.chips - 1, p.chips - 1, p.chips, p.chips)
    return {f"{name}_{k}": pltpu.SemaphoreType.DMA((max(1, size),)) for k, size in enumerate(sizes)}


def sum_scratch(p):
    far = max(1, p.chips - 1)
    return {
        "part": pltpu.VMEM((p.chips, p.width, p.seq), BF),
        "near_in": pltpu.VMEM((p.chips, p.width, p.seq), BF),
        "far_out": pltpu.VMEM((far, p.width, p.seq), BF),
        "far_in": pltpu.VMEM((far, p.width, p.seq), BF),
    }


def saved_shapes(p):
    return {
        "nt": ((p.blk, p.width, p.seq), BF),
        "qs": ((p.heads, p.blocks, HD, p.top * QROWS), BF),
        "kt": ((p.heads, HD, p.length + MAXLEN), BF),
        "vt": ((p.heads, HD, p.length + MAXLEN), BF),
        "lse": ((p.blocks, 8, p.top * QROWS), F32),
        "att": ((p.heads, p.blocks, HD, p.top * QROWS), BF),
        "mix": ((p.mixers * p.cols, p.length), BF),
        "gates": ((p.blk, 8, p.seq), F32),
    }


def launch(body, name, number, ins, outs, scratch):
    def spec(vmem):
        return pl.BlockSpec(memory_space=pltpu.VMEM if vmem else pl.ANY)

    names = list(ins) + list(outs) + list(scratch)

    def kernel(*refs):
        r = SimpleNamespace(**dict(zip(names, refs, strict=True)))
        r.moved = 0
        r.a = SimpleNamespace(**{k[2:]: v for k, v in vars(r).items() if k.startswith("a_")})
        for key in ("gather", "sum", "back_gather", "back_sum", "picks"):
            sems = [getattr(r, f"{key}_{k}") for k in range(4) if hasattr(r, f"{key}_{k}")]
            setattr(r.a, key + "_sems", sems)
            setattr(r, key + "_sems", sems)
        body(r)

    results = pl.pallas_call(
        kernel,
        out_shape=tuple(jax.ShapeDtypeStruct(shape, dtype) for shape, dtype, _ in outs.values()),
        in_specs=[spec(vmem) for _, vmem in ins.values()],
        out_specs=tuple(spec(vmem) for _, _, vmem in outs.values()),
        scratch_shapes=list(scratch.values()),
        compiler_params=pltpu.CompilerParams(
            collective_id=number, has_side_effects=number is not None, vmem_limit_bytes=VMEM_BYTES
        ),
        name=name,
    )(*[array for array, _ in ins.values()])
    return SimpleNamespace(**dict(zip(outs, results, strict=True)))


def on_device(
    inputs,
    segments,
    attention_routes,
    expert_routes,
    gain_mixer,
    gain_expert,
    weight_query,
    weight_key,
    weight_value,
    weight_out,
    router_mixer,
    router_expert,
    weight_in,
    weight_back,
    halt_weight,
    cotangent,
):
    blk, dp = lax.axis_size("blk"), lax.axis_size("dp")
    seq, width = inputs.shape[1:]
    experts, local = router_expert.shape[1], weight_in.shape[0]
    slots_of = max(2, 3 * seq // experts)
    hi = 4
    p = Plan(
        blk=blk,
        dp=dp,
        lo=dp // hi,
        hi=hi,
        seq=seq,
        width=width,
        heads=HEADS // blk,
        mixers=weight_query.shape[0],
        top=attention_routes.shape[-1],
        experts=experts,
        local=local,
        group=blk // local,
        cap=-(-slots_of // 16) * 16,
        ff=weight_in.shape[2],
    )
    cols, length, top = p.cols, p.length, p.top
    share, in_rows, back_rows = weight_key.shape[0], weight_in.shape[1], weight_back.shape[1]

    vectors = jnp.stack([gain_mixer, gain_expert, halt_weight])
    router_row, router = router_mixer.T, router_expert.T

    slots_bf = pltpu.VMEM((p.slots, width), BF)
    saved = saved_shapes(p)
    attention_scratch = {
        "seg_cols": pltpu.VMEM((length + MAXLEN, 8), F32),
        "k_rows": pltpu.VMEM((p.heads, length + MAXLEN, HD), BF),
        "all_w": pltpu.VMEM((width, p.all_cols), BF),
        **{"a_" + k: pltpu.VMEM(*v) for k, v in saved.items()},
    }
    forward_scratch = {
        "w_t": pltpu.VMEM((p.qkv, width), BF),
        **pack_sems(p, "gather"),
        **pack_sems(p, "sum"),
        **sum_scratch(p),
    }
    backward_scratch = {
        "gt": pltpu.VMEM((blk, width, seq), BF),
        "v_rows": pltpu.VMEM((p.heads, length + MAXLEN, HD), BF),
        "means": pltpu.VMEM((p.blocks, 8, top * QROWS), F32),
        "dlog": pltpu.VMEM((blk, p.mixers, seq), F32),
        "dkt": pltpu.VMEM((p.heads, HD, length + MAXLEN), F32),
        "dvt": pltpu.VMEM((p.heads, HD, length + MAXLEN), F32),
        "dall": pltpu.VMEM((p.qkv, length), BF),
        "grad_w": pltpu.VMEM((width, p.all_cols), BF),
        **pack_sems(p, "back_gather"),
        **pack_sems(p, "back_sum"),
        **sum_scratch(p),
    }
    expert_scratch = {
        "router": pltpu.VMEM((LANES, width), BF),
        "all_in": pltpu.VMEM((width, p.ff), BF),
        "all_back": pltpu.VMEM((p.ff, width), BF),
    }
    expert_back_scratch = {
        "keep": pltpu.VMEM((2, p.slots, p.ff), BF),
        "coeff": pltpu.VMEM((p.slots, LANES), BF),
        "arrived_t": pltpu.VMEM((width, p.slots), BF),
        "u_out": slots_bf,
        "u_in": slots_bf,
        "gret_in": slots_bf,
        "grad_in": pltpu.VMEM((width, p.ff), BF),
        "grad_back": pltpu.VMEM((p.ff, width), BF),
        **dma("u", p.experts),
        **dma("gret", p.experts),
    }

    one = launch(
        functools.partial(forward_kernel, p),
        "forward",
        0,
        {
            "x": (inputs[0], True),
            "segments": (segments, True),
            "attention_routes": (jnp.swapaxes(attention_routes[:, 0], 1, 2), True),
            "expert_routes": (jnp.swapaxes(expert_routes[:, 0], 1, 2), True),
            "vectors": (vectors, True),
            "router_row": (router_row, True),
            "router_in": (router, True),
            "weight_query": (weight_query, True),
            "weight_key": (weight_key, True),
            "weight_value": (weight_value, True),
            "weight_out": (jnp.swapaxes(weight_out, 1, 2), True),
            "weight_in": (weight_in, False),
            "weight_back": (weight_back, False),
        },
        {
            "first": ((seq, width), F32, True),
            "middle": ((seq, width), F32, True),
            "arrived": ((p.slots, width), BF, True),
            "produced": ((p.slots, width), BF, True),
            "all_picks": ((blk, 16, seq), jnp.int32, True),
            "disp_out": ((2, p.slots, seq), BF, False),
            "comb_out": ((2, seq, p.slots), BF, False),
            "pair_end": ((2, p.slots, LANES), BF, False),
            "all_w_out": ((width, p.all_cols), BF, False),
            "all_in_out": ((width, p.ff), BF, False),
            "all_back_out": ((p.ff, width), BF, False),
            **{k + "_out": (*v, False) for k, v in saved.items()},
        },
        {
            **attention_scratch,
            **forward_scratch,
            **expert_scratch,
            "disp": pltpu.VMEM((2, p.slots, seq), BF),
            "comb": pltpu.VMEM((2, seq, p.slots), BF),
            "pair": pltpu.VMEM((2, p.slots, LANES), BF),
            "pair_out": pltpu.VMEM((experts, 8, LANES), F32),
            "pair_in": pltpu.VMEM((experts, 8, LANES), F32),
            "routes": pltpu.VMEM((16, seq), jnp.int32),
            "outgoing": slots_bf,
            "ret_out": slots_bf,
            "ret_in": slots_bf,
            **pack_sems(p, "picks"),
            **dma("hi", 2 * (p.heads + 1) * (p.hi - 1)),
            **dma("lo", (p.heads + 1) * p.hi * (p.lo - 1)),
            **dma("wide", 2 * (p.local - 1)),
            **dma("near", 2 * p.local * (p.group - 1)),
            **dma("pair", p.experts),
            **dma("go", p.experts),
            **dma("ret", p.experts),
            "moves": pltpu.SemaphoreType.DMA((16,)),
        },
    )
    two = launch(
        functools.partial(turn_kernel, p),
        "turn",
        1,
        {
            "first": (one.first, True),
            "cot": (cotangent[0], True),
            "segments": (segments, True),
            "all_picks": (one.all_picks, True),
            "vectors": (vectors, True),
            "router_row": (router_row, True),
            "router_in": (router, True),
            "disp_in": (one.disp_out, False),
            "comb_in": (one.comb_out, False),
            "pair_in": (one.pair_end, False),
            "all_w_in": (one.all_w_out, False),
            "all_in_in": (one.all_in_out, False),
            "all_back_in": (one.all_back_out, False),
        },
        {
            "result": ((seq, width), BF, True),
            "grad_first": ((seq, width), F32, True),
            "grad_halt": ((1, width), F32, True),
            "grad_gain_one": ((1, width), F32, True),
            "grad_gain_two": ((1, width), F32, True),
            "grad_mixer": ((p.mixers, width), F32, True),
            "grad_router": ((experts, width), F32, True),
            "grad_in_out": ((width, p.ff), BF, False),
            "grad_back_out": ((p.ff, width), BF, False),
            "grad_w_out": ((width, p.all_cols), BF, False),
        },
        {
            **attention_scratch,
            **forward_scratch,
            **backward_scratch,
            **expert_scratch,
            **expert_back_scratch,
            "wo": pltpu.VMEM((p.mixers * cols, width), BF),
            "disp": pltpu.VMEM((p.slots, seq), BF),
            "comb": pltpu.VMEM((seq, p.slots), BF),
            "pair": pltpu.VMEM((p.slots, LANES), BF),
            "middle": pltpu.VMEM((seq, width), F32),
            "outgoing": slots_bf,
            "arrived": slots_bf,
            "gret_out": slots_bf,
            "ret_in": slots_bf,
            **dma("go", p.experts),
            **dma("ret", p.experts),
            "moves": pltpu.SemaphoreType.DMA((16,)),
        },
    )
    near, far = p.local * (p.group - 1), max(1, p.local - 1)
    small_rows = 8 + p.mixers + experts
    three = launch(
        functools.partial(backward_kernel, p),
        "backward",
        2,
        {
            "x": (inputs[0], True),
            "grad_first": (two.grad_first, True),
            "middle": (one.middle, True),
            "segments": (segments, True),
            "all_picks": (one.all_picks, True),
            "vectors": (vectors, True),
            "router_row": (router_row, True),
            "router_in": (router, True),
            "halt_before": (two.grad_halt, True),
            "gain_one_before": (two.grad_gain_one, True),
            "gain_two_before": (two.grad_gain_two, True),
            "mixer_before": (two.grad_mixer, True),
            "router_before": (two.grad_router, True),
            "disp_in": (one.disp_out, False),
            "comb_in": (one.comb_out, False),
            "pair_in": (one.pair_end, False),
            "arrived_in": (one.arrived, False),
            "produced_in": (one.produced, False),
            "all_w_in": (one.all_w_out, False),
            "all_in_in": (one.all_in_out, False),
            "all_back_in": (one.all_back_out, False),
            "grad_in_in": (two.grad_in_out, False),
            "grad_back_in": (two.grad_back_out, False),
            "grad_w_in": (two.grad_w_out, False),
            **{k + "_in": (getattr(one, k + "_out"), False) for k in SAVED},
        },
        {
            "input_grad": ((seq, width), BF, True),
            "out_w": ((share, p.all_cols), F32, True),
            "out_in": ((local, in_rows, p.ff), BF, True),
            "out_back": ((local, back_rows, width), BF, True),
            "out_small": ((small_rows, width), F32, True),
        },
        {
            **attention_scratch,
            **backward_scratch,
            **expert_scratch,
            **expert_back_scratch,
            "wo": pltpu.VMEM((p.mixers * cols, width), BF),
            "disp": pltpu.VMEM((p.slots, seq), BF),
            "comb": pltpu.VMEM((seq, p.slots), BF),
            "pair": pltpu.VMEM((p.slots, LANES), BF),
            "arrived": slots_bf,
            "produced": slots_bf,
            "in_near": pltpu.VMEM((near, in_rows, p.ff), BF),
            "back_near": pltpu.VMEM((near, back_rows, width), BF),
            "in_far_out": pltpu.VMEM((far, in_rows, p.ff), BF),
            "in_far": pltpu.VMEM((far, in_rows, p.ff), BF),
            "back_far_out": pltpu.VMEM((far, back_rows, width), BF),
            "back_far": pltpu.VMEM((far, back_rows, width), BF),
            "w_lo": pltpu.VMEM((hi * (p.lo - 1), share, p.all_cols), BF),
            "w_hi_out": pltpu.VMEM((hi - 1, share, p.all_cols), BF),
            "w_hi": pltpu.VMEM((hi - 1, share, p.all_cols), BF),
            "grad_router": pltpu.VMEM((experts, width), F32),
            "all_small": pltpu.VMEM((2 + p.chips + p.lo + hi, small_rows, width), F32),
            **dma("near", 2 * near),
            **dma("wide", 2 * (local - 1)),
            **dma("lo", (p.heads + 1) * hi * (p.lo - 1)),
            **dma("hi", (p.heads + 1) * (hi - 1)),
            **dma("tiny", 2 + p.chips + p.lo + hi),
            "moves": pltpu.SemaphoreType.DMA((24,)),
        },
    )
    four = launch(
        functools.partial(output_kernel, p),
        "outputs",
        None,
        {
            "result": (two.result, True),
            "input_grad": (three.input_grad, True),
            "out_w": (three.out_w, True),
            "out_in": (three.out_in, True),
            "out_back": (three.out_back, True),
            "small": (three.out_small, True),
        },
        {
            "result_out": ((seq, width), BF, True),
            "input_grad_out": ((seq, width), BF, True),
            "query_out": (weight_query.shape, F32, True),
            "key_out": (weight_key.shape, F32, True),
            "value_out": (weight_value.shape, F32, True),
            "out_out": ((p.mixers, share, cols), F32, True),
            "in_out": (weight_in.shape, F32, True),
            "back_out": (weight_back.shape, F32, True),
            "gain_one_out": ((1, width), F32, True),
            "gain_two_out": ((1, width), F32, True),
            "halt_out": ((1, width), F32, True),
            "mixer_out": ((p.mixers, width), F32, True),
            "router_out": ((experts, width), F32, True),
        },
        {},
    )
    return (
        four.result_out[None],
        four.input_grad_out[None],
        four.gain_one_out.reshape(width),
        four.gain_two_out.reshape(width),
        four.query_out,
        four.key_out,
        four.value_out,
        jnp.swapaxes(four.out_out, 1, 2),
        four.mixer_out.T,
        four.router_out.T,
        four.in_out,
        four.back_out,
        four.halt_out.reshape(width),
    )


def solution(mesh):
    return jax.shard_map(
        on_device,
        mesh=mesh,
        in_specs=(
            P("dp", "blk", None),
            P("dp", None),
            P(None, "dp", "blk", None),
            P(None, "dp", "blk", None),
            P(),
            P(),
            P(None, "dp", "blk"),
            P("dp", "blk"),
            P("dp", "blk"),
            P(None, "blk", "dp"),
            P(),
            P(),
            P("dp", "blk", None),
            P("dp", "blk", None),
            P(),
            P("dp", "blk", None),
        ),
        out_specs=(
            P("dp", "blk", None),
            P("dp", "blk", None),
            P(),
            P(),
            P(None, "dp", "blk"),
            P("dp", "blk"),
            P("dp", "blk"),
            P(None, "blk", "dp"),
            P(),
            P(),
            P("dp", "blk", None),
            P("dp", "blk", None),
            P(),
        ),
        check_vma=False,
    )
```
